256 devices in a mesh: side: 2 (over z_hi), fin: 4 (over x), fhid: 32 (over y, z_lo, core).
Axes of the slice: x: 4, y: 4, z: 8 (z_hi: 2, z_lo: 4; z = z_hi * 4 + z_lo), core: 2. Of those that a mesh axis runs over, the one named last changes fastest.
Arguments:
- queries: bfloat16 [256, 16384], P(('fin', 'fhid')), may hold values from -112 to 112
- new_entries: bfloat16 [256, 2048], P(('fin', 'fhid')), may hold values from -4 to 4
- cached_entries: bfloat16 [2, 256, 256, 2048], P('side', ('fin', 'fhid')), may hold values from -4 to 4
- lengths: int32 [256], P(('fin', 'fhid')), may hold values from 1 to 256, as said below
- residual: bfloat16 [256, 16384], P(('fin', 'fhid')), may hold values from -60 to 60
- norm_gain: bfloat16 [16384], P('fin'), may hold values from 0.099609375 to 1.8984375
- out_weight: bfloat16 [2, 16384, 16384], P('side', 'fhid', 'fin'), may hold values from -0.1875 to 0.1875
- gate_weight: bfloat16 [2, 16384, 8192], P('side', 'fin', 'fhid'), may hold values from -0.046875 to 0.046875
- up_weight: bfloat16 [2, 16384, 8192], P('side', 'fin', 'fhid'), may hold values from -0.046875 to 0.046875
- down_weight: bfloat16 [2, 8192, 16384], P('side', 'fhid', 'fin'), may hold values from -0.125 to 0.125
Outputs:
- next_hidden: bfloat16 [256, 16384], P(('fin', 'fhid'))
The draws below stay inside these ranges and needn't reach their ends.
Inputs may be any that keep to these rules, and one draw needn't show every extreme that they name: `lengths`: every row has at least one and at most 256 cached positions in use; in every draw some rows use all 256.
All inputs are finite; a program needn't handle non-finite values.
Results may differ from the reference program's by a relative error of at most 0.011.
Values may be sent and summed in bfloat16 or wider, within the bound.
A program may use at most 128 MiB of HBM per device.

```python
import math
import jax
import jax.numpy as jnp
from jax import lax

D = 16384
HEADS = 128
KVH = 8
HD = 128
FF = 8192
CACHE = 256
ROWS = 256


def first_positions(key):
    base = jax.random.normal(jax.random.fold_in(key, 101), (2, ROWS, 1, 2 * KVH * HD), jnp.float32)
    return jnp.clip(base, -4.0, 4.0)


def draw_cached_entries(key, part):
    first = first_positions(key)
    key = jax.random.fold_in(key, 1)
    later = jnp.clip(jax.random.normal(key, (2, ROWS, CACHE - 1, 2 * KVH * HD), jnp.float32), -4.0, 4.0)
    return jnp.concatenate([first, later], axis=2).astype(jnp.bfloat16)


def draw_queries(key, part):
    key = jax.random.fold_in(key, 2)
    base = jnp.clip(jax.random.normal(key, (ROWS, HEADS * HD), jnp.float32), -4.0, 4.0)
    return base.astype(jnp.bfloat16)


def draw_new_entries(key, part):
    key = jax.random.fold_in(key, 3)
    base = jnp.clip(jax.random.normal(key, (ROWS, 2 * KVH * HD), jnp.float32), -4.0, 4.0)
    return base.astype(jnp.bfloat16)


def draw_lengths(key, part):
    key = jax.random.fold_in(key, 5)
    drawn = jax.random.randint(key, (ROWS,), 1, CACHE + 1)
    filled = jnp.arange(ROWS) % 16 == 5
    return jnp.where(filled, CACHE, drawn).astype(jnp.int32)


def draw_residual(key, part):
    key = jax.random.fold_in(key, 4)
    key_rows, key_body = jax.random.split(key, 2)
    columns = jnp.arange(D, dtype=jnp.float32)[None, :] / D
    row_spread = jax.random.uniform(key_rows, (ROWS, 1), jnp.float32)
    base = jnp.clip(jax.random.normal(key_body, (ROWS, D), jnp.float32), -4.0, 4.0)
    column_scale = jnp.power(10.0, columns - 0.5)
    return (0.6 * base * jnp.power(10.0, row_spread - 0.5) * column_scale).astype(jnp.bfloat16)


def block_levels(rng, shape, pieces, low, largest):
    level = 1.0
    for position, parts in pieces:
        heights = jax.random.uniform(jax.random.fold_in(jax.random.fold_in(rng, 6), position), (parts,), jnp.float32, low / len(pieces), largest / len(pieces))
        level = level * jnp.repeat(jnp.exp(heights), shape[position] // parts).reshape((-1,) + (1,) * (len(shape) - 1 - position))
    return level


def gaussian(stream_key, shape, spread, bound, cuts=(), kind=jnp.bfloat16):
    entries = jax.random.normal(stream_key, shape, jnp.float32) * spread
    if len(cuts) > 0:
        entries = block_levels(stream_key, shape, cuts, -0.22, 0.18) * entries
    return jnp.clip(entries, min=-bound, max=bound).astype(kind)


def setup_inputs(seed: int = 0) -> dict:
    arg_keys = jax.random.split(jax.random.key(seed), 11)
    return {
        "queries": draw_queries(jax.random.fold_in(arg_keys[10], 71), 0),
        "new_entries": draw_new_entries(jax.random.fold_in(arg_keys[10], 71), 0),
        "cached_entries": draw_cached_entries(jax.random.fold_in(arg_keys[10], 71), 0),
        "lengths": draw_lengths(jax.random.fold_in(arg_keys[10], 71), 0),
        "residual": draw_residual(jax.random.fold_in(arg_keys[10], 71), 0),
        "norm_gain": jnp.clip(1.0 + 0.18 * jax.random.normal(arg_keys[5], (D,), jnp.float32), 0.099609375, 1.8984375).astype(jnp.bfloat16),
        "out_weight": gaussian(arg_keys[6], (2, HEADS * HD, D), (HEADS * HD // 16) ** -0.5, 0.1875, ((0, 2), (1, 32), (2, 4))),
        "gate_weight": gaussian(arg_keys[7], (2, D, FF), D ** -0.5, 0.046875, ((0, 2), (1, 4), (2, 32))),
        "up_weight": gaussian(arg_keys[8], (2, D, FF), D ** -0.5, 0.046875, ((0, 2), (1, 4), (2, 32))),
        "down_weight": gaussian(arg_keys[9], (2, FF, D), (FF // 4) ** -0.5, 0.125, ((0, 2), (1, 32), (2, 4))),
    }


def attend_row(inputs):
    query, fresh, cached, length = inputs
    per_group = HEADS // KVH
    key_width = KVH * HD
    score_scale = 1.0 / math.sqrt(HD)
    cached_keys = cached[:, :key_width].astype(jnp.float32).reshape(CACHE, KVH, HD)
    cached_values = cached[:, key_width:].astype(jnp.float32).reshape(CACHE, KVH, HD)
    heads = query.astype(jnp.float32).reshape(KVH, per_group, HD)
    new_key = fresh[:key_width].astype(jnp.float32).reshape(KVH, HD)
    new_value = fresh[key_width:].astype(jnp.float32).reshape(KVH, HD)
    scores = jnp.einsum('gqd,lgd->gql', heads, cached_keys) * score_scale
    own_score = jnp.einsum('gqd,gd->gq', heads, new_key) * score_scale
    valid = jnp.arange(CACHE) < length
    scores = jnp.where(valid[None, None, :], scores, jnp.float32(-1e+30))
    row_top = jnp.maximum(lax.optimization_barrier(jnp.max(scores, axis=-1)), own_score)
    expo = jnp.exp(scores - row_top[..., None])
    own_exp = jnp.exp(own_score - row_top)
    denominator = lax.optimization_barrier(jnp.sum(expo, axis=-1)) + own_exp
    weights = lax.optimization_barrier((expo / denominator[..., None]).astype(jnp.bfloat16))
    own_weight = lax.optimization_barrier((own_exp / denominator).astype(jnp.bfloat16))
    mixed = jnp.einsum('gql,lgd->gqd', weights.astype(jnp.float32), cached_values)
    mixed = mixed + own_weight.astype(jnp.float32)[..., None] * new_value[:, None, :]
    return mixed.reshape(HEADS * HD).astype(jnp.bfloat16)

def reference(queries, new_entries, cached_entries, lengths, residual, norm_gain, out_weight, gate_weight, up_weight, down_weight):
    mixed = lax.map(attend_row, (queries, new_entries, cached_entries[0], lengths.astype(jnp.int32)))
    projected = jnp.dot(mixed, out_weight[1], preferred_element_type=jnp.float32)
    stream = (residual.astype(jnp.float32) + projected).astype(jnp.bfloat16)
    stream_wide = stream.astype(jnp.float32)
    mean_square = lax.optimization_barrier(jnp.mean(stream_wide * stream_wide, axis=1, keepdims=True))
    normed = (stream_wide * lax.rsqrt(mean_square + 1e-05) * norm_gain.astype(jnp.float32)).astype(jnp.bfloat16)
    gate = jnp.dot(normed, gate_weight[1], preferred_element_type=jnp.float32)
    up_sum = jnp.dot(normed, up_weight[1], preferred_element_type=jnp.float32)
    hidden = (jax.nn.silu(gate) * up_sum).astype(jnp.bfloat16)
    lowered = jnp.dot(hidden, down_weight[1], preferred_element_type=jnp.float32)
    return (stream_wide + lowered).astype(jnp.bfloat16)
```

```python
import functools
import math

import jax
import jax.numpy as jnp
from jax import lax
from jax.experimental import pallas as pl
from jax.experimental.pallas import tpu as pltpu
from jax.sharding import PartitionSpec as P

D = 16384
HD = 128
BF = jnp.bfloat16
F32 = jnp.float32
MESH = pl.DeviceIdType.MESH
ORDER = (2, 1, 3, 0)


def attend(queries, new_entries, cached, lengths):
    row_count = queries.shape[0]
    positions = cached.shape[1]
    key_width = cached.shape[2] // 2
    heads_kv = key_width // HD
    per_group = queries.shape[1] // key_width
    score_scale = 1.0 / math.sqrt(HD)
    cached_keys = cached[:, :, :key_width].reshape(row_count, positions, heads_kv, HD)
    cached_values = cached[:, :, key_width:].reshape(row_count, positions, heads_kv, HD)
    heads = queries.reshape(row_count, heads_kv, per_group, HD)
    new_key = new_entries[:, :key_width].reshape(row_count, heads_kv, HD)
    new_value = new_entries[:, key_width:].reshape(row_count, heads_kv, HD)
    scores = (
        jnp.einsum("rgqd,rlgd->rgql", heads, cached_keys, preferred_element_type=F32) * score_scale
    )
    own_score = (
        jnp.einsum("rgqd,rgd->rgq", heads, new_key, preferred_element_type=F32) * score_scale
    )
    valid = jnp.arange(positions)[None, :] < lengths[:, None]
    scores = jnp.where(valid[:, None, None, :], scores, jnp.float32(-1e30))
    row_top = jnp.maximum(jnp.max(scores, axis=-1), own_score)
    expo = jnp.exp(scores - row_top[..., None])
    own_exp = jnp.exp(own_score - row_top)
    denominator = jnp.sum(expo, axis=-1) + own_exp
    weights = (expo / denominator[..., None]).astype(BF)
    own_weight = (own_exp / denominator).astype(BF)
    mixed = jnp.einsum("rgql,rlgd->rgqd", weights, cached_values, preferred_element_type=F32)
    mixed = (
        mixed + own_weight.astype(F32)[..., None] * new_value.astype(F32)[:, :, None, :]
    )
    return mixed.reshape(row_count, -1).astype(BF)


def iota(shape, axis):
    return lax.broadcasted_iota(jnp.int32, shape, axis)


def selection(source):
    t = iota((256, 256), 0)
    return (iota((256, 256), 1) == source(t)).astype(F32).astype(BF)


def arrived(ref, sem):
    pltpu.make_async_copy(ref, ref, sem).wait()


def kernel(
    m1_src, res_src, gain, ow_hbm, gw_hbm, uw_hbm, dw_hbm, out,
    ow, gw, uw, dw, m1, m2s, m2, lhs, rin, resid, acc,
    own, cs, cr, q, ya, yb, yfm, yfp, zs, zin,
    sbuf, gu, ss, xs, xr, hid,
    own2, cs2, cr2, q2, ya2, yb2, yfm2, yfp2, zs2, zin2, fo, fb, fin_in,
    w_sem, m1_s, m1_r, m2_s, m2_r, rs_s, rs_r, xa_s, xa_r, c_s, c_r, y_s, y_r, z_s, z_r,
    az_s, ay_s, ac_s, ag_r, ac_r, xs_s, xs_r, xh_s, xh_r, c2_s, c2_r, y2_s, y2_r, z2_s, z2_r,
    f_s, f_r,
):
    side, f, h = lax.axis_index("side"), lax.axis_index("fin"), lax.axis_index("fhid")
    y, z, c = h // 8, (h // 2) % 4, h % 2
    yz = h // 2
    oc = 1 - c

    def at(s, ff, yy, zz, cc):
        return (s, ff, (yy * 4 + zz) * 2 + cc)

    def send(src, dst, ss_, rs_, dev):
        cp = pltpu.make_async_remote_copy(
            src_ref=src, dst_ref=dst, send_sem=ss_, recv_sem=rs_, device_id=dev, device_id_type=MESH
        )
        cp.start()
        return cp

    barrier = pltpu.get_barrier_semaphore()

    def greet(dev):
        pl.semaphore_signal(barrier, inc=1, device_id=dev, device_id_type=MESH)

    j = f * 2 + c

    @pl.when(side == 0)
    def _attention_side():
        for d in range(1, 8):
            jj = (j + d) % 8
            greet(at(0, jj // 2, y, z, jj % 2))
        for d in range(8):
            greet(at(1, d // 2, y, z, d % 2))
        pl.semaphore_wait(barrier, 23)
        copies = []
        for d in range(1, 8):
            jj = (j + d) % 8
            copies.append(
                send(m1_src.at[jj], m1.at[j], m1_s.at[d], m1_r.at[j], at(0, jj // 2, y, z, jj % 2))
            )
        m1[j] = m1_src[j]
        sel = selection(
            lambda t: (((t // 2) % 4 * 2 + (t // 8) % 2) * 2 + t % 2) * 16 + t // 16
        )
        for d in range(1, 8):
            jj = (j + d) % 8
            arrived(m1.at[jj], m1_r.at[jj])
        m2s[...] = jnp.dot(sel, m1[...].reshape(256, 128), preferred_element_type=F32).astype(BF)
        for b in range(16):
            copies.append(
                send(
                    m2s.at[pl.ds(b * 16, 16)],
                    m2.at[pl.ds(pl.multiple_of(yz * 16, 16), 16)],
                    m2_s.at[b],
                    m2_r.at[yz],
                    at(1, f, b // 4, b % 4, c),
                )
            )
        for cp in copies:
            cp.wait_send()
        for s in range(8):
            arrived(fin_in.at[s], f_r.at[s])
        out[...] = fin_in[...]

    @pl.when(side == 1)
    def _mlp_side():
        up, down = (y + 1) % 4, (y + 3) % 4
        dev_up, dev_down = at(1, f, up, z, c), at(1, f, down, z, c)
        dev_core = at(1, f, y, z, oc)
        for d in range(16):
            greet(at(0, f, d // 4, d % 4, c))
        for d in range(1, 8):
            jj = (j + d) % 8
            greet(at(1, jj // 2, y, z, jj % 2))
        for d in range(1, 4):
            greet(at(1, f, y, (z + d) % 4, c))
        greet(dev_up)
        greet(dev_down)
        weights = [
            pltpu.make_async_copy(a, b, w_sem.at[k])
            for k, (a, b) in enumerate(((ow_hbm, ow), (gw_hbm, gw), (uw_hbm, uw), (dw_hbm, dw)))
        ]
        for cp in weights:
            cp.start()
        pl.semaphore_wait(barrier, 20)
        copies = []

        for d in range(1, 4):
            ff = (f + d) % 4
            copies.append(
                send(res_src.at[ff], rin.at[f], rs_s.at[d], rs_r.at[f], at(1, ff, y, z, c))
            )
        rin[f] = res_src[f]
        for d in range(1, 4):
            ff = (f + d) % 4
            arrived(rin.at[ff], rs_r.at[ff])
        sel = selection(
            lambda t: (t // 2) % 4 * 64 + ((t % 2) * 16 + (t // 8) % 16) * 2 + t // 128
        )
        resid[...] = jnp.dot(sel, rin[...].reshape(256, 128), preferred_element_type=F32)
        gu[...] = jnp.zeros_like(gu)
        ss[...] = jnp.zeros_like(ss)

        for s in range(16):
            arrived(m2.at[pl.ds(s * 16, 16)], m2_r.at[s])
        for d in range(1, 4):
            ff = (f + d) % 4
            copies.append(send(m2, lhs.at[f], xa_s.at[d], xa_r.at[f], at(1, ff, y, z, c)))
        lhs[f] = m2[...]
        weights[0].wait()
        for d in range(1, 4):
            ff = (f + d) % 4
            arrived(lhs.at[ff], xa_r.at[ff])

        def project(g):
            yy = (y + ORDER[g]) % 4

            def chunk(k, carry):
                n = yy * 4 + k
                x = jnp.concatenate([lhs[0], lhs[1], lhs[2], lhs[3]], axis=1)
                w = ow[:, pl.ds(pl.multiple_of(n * 256, 256), 256)]
                acc[...] = jnp.dot(x, w, preferred_element_type=F32)
                r8 = pl.ds(pl.multiple_of(h * 8, 8), 8)
                lo = resid[pl.ds(pl.multiple_of(n * 8, 8), 8), :]
                hi = resid[pl.ds(pl.multiple_of(128 + n * 8, 8), 8), :]
                acc[r8, :] = acc[r8, :] + jnp.concatenate([lo, hi], axis=1)
                own[n] = acc[pl.ds(pl.multiple_of(c * 128, 128), 128), :]
                cs[n] = acc[pl.ds(pl.multiple_of(oc * 128, 128), 128), :].astype(BF)
                return carry

            lax.fori_loop(0, 4, chunk, 0)
            part = pl.ds(yy * 4, 4)
            copies.append(send(cs.at[part], cr.at[part], c_s.at[g], c_r.at[g], dev_core))

        def paired(g):
            yy = (y + ORDER[g]) % 4
            part = pl.ds(yy * 4, 4)
            arrived(cr.at[part], c_r.at[g])
            if g < 3:
                q[part] = (own[part] + cr[part].astype(F32)).astype(BF)
            first, second = pl.ds(yy * 4, 2), pl.ds(yy * 4 + 2, 2)
            a, b = pl.ds(0, 2), pl.ds(2, 2)
            if g == 0:
                copies.append(send(q.at[first], ya, y_s.at[0], y_r.at[0], dev_up))
                copies.append(send(q.at[second], yb, y_s.at[1], y_r.at[1], dev_down))
            if g == 1:
                copies.append(send(q.at[second], yfm.at[b], y_s.at[2], y_r.at[2], dev_up))
            if g == 2:
                copies.append(send(q.at[first], yfp.at[a], y_s.at[3], y_r.at[3], dev_down))

        project(0)
        project(1)
        paired(0)
        project(2)
        paired(1)
        project(3)
        paired(2)
        a, b = pl.ds(0, 2), pl.ds(2, 2)
        arrived(ya, y_r.at[0])
        first = pl.ds(up * 4, 2)
        q[first] = (q[first].astype(F32) + ya[...].astype(F32)).astype(BF)
        copies.append(send(q.at[first], yfm.at[a], y_s.at[4], y_r.at[4], dev_up))
        arrived(yb, y_r.at[1])
        second = pl.ds(down * 4 + 2, 2)
        q[second] = (q[second].astype(F32) + yb[...].astype(F32)).astype(BF)
        copies.append(send(q.at[second], yfp.at[b], y_s.at[5], y_r.at[5], dev_down))
        paired(3)
        arrived(yfm.at[b], y_r.at[2])
        arrived(yfp.at[a], y_r.at[3])
        arrived(yfm.at[a], y_r.at[4])
        arrived(yfp.at[b], y_r.at[5])

        def summed(k):
            n = y * 4 + k
            return own[n] + cr[n].astype(F32) + yfm[k].astype(F32) + yfp[k].astype(F32)

        for d in range(1, 4):
            zz = (z + d) % 4
            zs[zz] = summed(zz).astype(BF)
            copies.append(send(zs.at[zz], zin.at[z], z_s.at[d], z_r.at[z], at(1, f, y, zz, c)))
        total = summed(z)
        for d in range(1, 4):
            zz = (z + d) % 4
            arrived(zin.at[zz], z_r.at[zz])
            total = total + zin[zz].astype(F32)
        sbuf[yz, c] = total.astype(BF)

        def give(n, sem, slot, dev):
            copies.append(
                send(sbuf.at[n, c], sbuf.at[n, c], sem.at[slot], ag_r.at[n], dev)
            )

        def give_core(n):
            copies.append(
                send(sbuf.at[n, c], sbuf.at[n, c], ac_s.at[n], ac_r.at[n], dev_core)
            )

        def use(n):
            arrived(sbuf.at[n, oc], ac_r.at[n])
            x = sbuf[n].reshape(256, 256).astype(F32)
            sq = x * x
            ss[...] += sq[:, :128] + sq[:, 128:]
            xg = (x * gain[n]).astype(BF)
            rows = pl.ds(pl.multiple_of(n * 256, 256), 256)
            gu[:, :256] += jnp.dot(xg, gw[rows, :], preferred_element_type=F32)
            gu[:, 256:] += jnp.dot(xg, uw[rows, :], preferred_element_type=F32)

        for d in range(1, 4):
            zz = (z + d) % 4
            give(yz, az_s, d, at(1, f, y, zz, c))
        give(yz, ay_s, 0, dev_up)
        give(yz, ay_s, 1, dev_down)
        give_core(yz)
        for d in range(1, 4):
            n = y * 4 + (z + d) % 4
            arrived(sbuf.at[n, c], ag_r.at[n])
            give(n, ay_s, d * 2, dev_up)
            give(n, ay_s, d * 2 + 1, dev_down)
            give_core(n)
        weights[1].wait()
        weights[2].wait()
        use(yz)
        for d in range(4):
            n = down * 4 + (z + d) % 4
            arrived(sbuf.at[n, c], ag_r.at[n])
            if d % 2 == 0:
                give(n, ay_s, 8 + d, dev_up)
            give_core(n)
            n = up * 4 + (z + d) % 4
            arrived(sbuf.at[n, c], ag_r.at[n])
            if d % 2 == 1:
                give(n, ay_s, 8 + d, dev_down)
            give_core(n)
            if d > 0:
                use(y * 4 + (z + d) % 4)
        far = (y + 2) % 4
        for d in range(4):
            use(down * 4 + (z + d) % 4)
            use(up * 4 + (z + d) % 4)
            n = far * 4 + (z + d) % 4
            arrived(sbuf.at[n, c], ag_r.at[n])
            give_core(n)
        for d in range(4):
            use(far * 4 + (z + d) % 4)

        tot = jnp.sum(ss[...], axis=1, keepdims=True)
        top = tot.astype(BF).astype(F32)
        lanes = iota((256, 128), 1)
        xs[:, :, 512:] = jnp.where(lanes < 64, top, tot - top).astype(BF).reshape(4, 64, 128)
        xs[:, :, :512] = gu[...].astype(BF).reshape(4, 64, 512)
        for d in range(1, 4):
            ff = (f + d) % 4
            copies.append(send(xs.at[ff], xr.at[f], xs_s.at[d], xs_r.at[f], at(1, ff, y, z, c)))
        mine = pl.ds(pl.multiple_of(f * 64, 64), 64)
        both = gu[mine, :]
        square = xs[f][:, 512:].astype(F32)
        for d in range(1, 4):
            ff = (f + d) % 4
            arrived(xr.at[ff], xs_r.at[ff])
            both = both + xr[ff][:, :512].astype(F32)
            square = square + xr[ff][:, 512:].astype(F32)
        scale = lax.rsqrt((square[:, 0:1] + square[:, 64:65]) / D + 1e-05)
        gate = both[:, :256] * scale
        hid[mine, :] = (gate / (1.0 + jnp.exp(-gate)) * (both[:, 256:] * scale)).astype(BF)
        for d in range(1, 4):
            ff = (f + d) % 4
            copies.append(
                send(hid.at[mine], hid.at[mine], xh_s.at[d], xh_r.at[f], at(1, ff, y, z, c))
            )
        weights[3].wait()
        for d in range(1, 4):
            ff = (f + d) % 4
            arrived(hid.at[pl.ds(pl.multiple_of(ff * 64, 64), 64)], xh_r.at[ff])

        def lower(g):
            yy = (y + ORDER[g]) % 4

            def chunk(k, carry):
                x = hid[pl.ds(pl.multiple_of(yy * 64, 64), 64), :]
                to = pl.ds(pl.multiple_of(k * 512, 512), 512)
                w = dw[:, pl.ds(pl.multiple_of(oc * 2048 + k * 512, 512), 512)]
                cs2[yy, :, to] = jnp.dot(x, w, preferred_element_type=F32).astype(BF)
                w = dw[:, pl.ds(pl.multiple_of(c * 2048 + k * 512, 512), 512)]
                own2[yy, :, to] = jnp.dot(x, w, preferred_element_type=F32)
                return carry

            lax.fori_loop(0, 4, chunk, 0)
            copies.append(send(cs2.at[yy], cr2.at[yy], c2_s.at[g], c2_r.at[g], dev_core))

        a2, b2 = pl.ds(0, 32), pl.ds(32, 32)

        def paired2(g):
            yy = (y + ORDER[g]) % 4
            arrived(cr2.at[yy], c2_r.at[g])
            if g < 3:
                q2[yy] = (own2[yy] + cr2[yy].astype(F32)).astype(BF)
            if g == 0:
                copies.append(send(q2.at[yy, a2], ya2, y2_s.at[0], y2_r.at[0], dev_up))
                copies.append(send(q2.at[yy, b2], yb2, y2_s.at[1], y2_r.at[1], dev_down))
            if g == 1:
                copies.append(send(q2.at[yy, b2], yfm2.at[b2], y2_s.at[2], y2_r.at[2], dev_up))
            if g == 2:
                copies.append(send(q2.at[yy, a2], yfp2.at[a2], y2_s.at[3], y2_r.at[3], dev_down))

        lower(0)
        lower(1)
        paired2(0)
        lower(2)
        paired2(1)
        lower(3)
        paired2(2)
        arrived(ya2, y2_r.at[0])
        q2[up, a2] = (q2[up, a2].astype(F32) + ya2[...].astype(F32)).astype(BF)
        copies.append(send(q2.at[up, a2], yfm2.at[a2], y2_s.at[4], y2_r.at[4], dev_up))
        arrived(yb2, y2_r.at[1])
        q2[down, b2] = (q2[down, b2].astype(F32) + yb2[...].astype(F32)).astype(BF)
        copies.append(send(q2.at[down, b2], yfp2.at[b2], y2_s.at[5], y2_r.at[5], dev_down))
        paired2(3)
        arrived(yfm2.at[b2], y2_r.at[2])
        arrived(yfp2.at[a2], y2_r.at[3])
        arrived(yfm2.at[a2], y2_r.at[4])
        arrived(yfp2.at[b2], y2_r.at[5])

        def summed2(k):
            rows = pl.ds(pl.multiple_of(k * 16, 16), 16)
            return (
                own2[y, rows, :]
                + cr2[y, rows, :].astype(F32)
                + yfm2[rows, :].astype(F32)
                + yfp2[rows, :].astype(F32)
            )

        for d in range(1, 4):
            zz = (z + d) % 4
            zs2[zz] = summed2(zz).astype(BF)
            copies.append(
                send(zs2.at[zz], zin2.at[z], z2_s.at[d], z2_r.at[z], at(1, f, y, zz, c))
            )
        rows = pl.ds(pl.multiple_of((yz % 8) * 16, 16), 16)
        kept = [sbuf[c * 8 + k, y // 2, rows, :].astype(F32) for k in range(8)]
        total = summed2(z) + jnp.concatenate(kept, axis=1)
        for d in range(1, 4):
            zz = (z + d) % 4
            arrived(zin2.at[zz], z2_r.at[zz])
            total = total + zin2[zz].astype(F32)

        for k in range(16):
            fo[:, k, :] = total[:, k * 128 : (k + 1) * 128]
        fb[...] = fo[...].astype(BF)
        for d in range(8):
            jj = (j + d) % 8
            part = fb.at[pl.ds((jj % 2) * 8 + (jj // 2) * 2, 2)]
            copies.append(send(part, fin_in.at[j], f_s.at[d], f_r.at[j], at(0, jj // 2, y, z, jj % 2)))
        for d in range(1, 8):
            jj = (j + d) % 8
            part = fb.at[pl.ds((jj % 2) * 8 + (jj // 2) * 2, 2)]
            copies.append(
                send(part, fin_in.at[j], f_s.at[7 + d], f_r.at[j], at(1, jj // 2, y, z, jj % 2))
            )
        fin_in[j] = fb[pl.ds(c * 8 + f * 2, 2)]
        for d in range(1, 8):
            jj = (j + d) % 8
            arrived(fin_in.at[jj], f_r.at[jj])
        out[...] = fin_in[...]
        for cp in copies:
            cp.wait_send()


def moved(m1_src, res_src, gain, ow, gw, uw, dw):
    def v(*shape, dtype=BF):
        return pltpu.VMEM(shape, dtype)

    scratch = [
        v(512, 4096), v(4096, 256), v(4096, 256), v(256, 4096),
        v(8, 32, 128), v(256, 128), v(256, 128), v(4, 256, 128),
        v(4, 64, 128), v(256, 128, dtype=F32), v(256, 256, dtype=F32),
        v(16, 128, 256, dtype=F32), v(16, 128, 256), v(16, 128, 256), v(16, 128, 256),
        v(2, 128, 256), v(2, 128, 256), v(4, 128, 256), v(4, 128, 256),
        v(4, 128, 256), v(4, 128, 256),
        v(16, 2, 128, 256), v(256, 512, dtype=F32), v(256, 128, dtype=F32),
        v(4, 64, 640), v(4, 64, 640), v(256, 256),
        v(4, 64, 2048, dtype=F32), v(4, 64, 2048), v(4, 64, 2048), v(4, 64, 2048),
        v(32, 2048), v(32, 2048), v(64, 2048), v(64, 2048),
        v(4, 16, 2048), v(4, 16, 2048),
        v(16, 16, 128, dtype=F32), v(16, 16, 128), v(8, 2, 16, 128),
    ]
    counts = [
        4, 8, 8, 16, 16, 4, 4, 4, 4, 4, 4, 6, 6, 4, 4,
        4, 12, 16, 16, 16, 4, 4, 4, 4, 4, 4, 6, 6, 4, 4,
        15, 8,
    ]
    scratch += [pltpu.SemaphoreType.DMA((k,)) for k in counts]
    vm, hbm = pl.BlockSpec(memory_space=pltpu.VMEM), pl.BlockSpec(memory_space=pl.ANY)
    return pl.pallas_call(
        kernel,
        out_shape=jax.ShapeDtypeStruct((8, 2, 16, 128), BF),
        in_specs=[vm, vm, vm, hbm, hbm, hbm, hbm],
        out_specs=vm,
        scratch_shapes=scratch,
        compiler_params=pltpu.CompilerParams(
            collective_id=0, has_side_effects=True, vmem_limit_bytes=56 * 1024 * 1024
        ),
    )(m1_src, res_src, gain, ow, gw, uw, dw)


def on_device(
    queries, new_entries, cached_entries, lengths, residual, norm_gain,
    out_weight, gate_weight, up_weight, down_weight,
):
    mixed = attend(queries, new_entries, cached_entries[0], lengths)
    m1_src = mixed.reshape(2, 16, 2, 4, 128).transpose(3, 2, 0, 1, 4).reshape(8, 32, 128)
    res_src = residual.reshape(2, 4, 32, 128).transpose(1, 0, 2, 3).reshape(4, 64, 128)
    gain = norm_gain.astype(F32).reshape(16, 1, 256)
    res = moved(
        m1_src, res_src, gain, out_weight[0], gate_weight[0], up_weight[0], down_weight[0]
    )
    return res.transpose(1, 0, 2, 3).reshape(2, D)


def solution(mesh):
    placed = (
        P(("fin", "fhid"), None),
        P(("fin", "fhid"), None),
        P("side", ("fin", "fhid"), None, None),
        P(("fin", "fhid")),
        P(("fin", "fhid"), None),
        P("fin"),
        P("side", "fhid", "fin"),
        P("side", "fin", "fhid"),
        P("side", "fin", "fhid"),
        P("side", "fhid", "fin"),
    )
    return jax.shard_map(
        on_device, mesh=mesh, in_specs=placed, out_specs=P(("fin", "fhid"), None), check_vma=False
    )
```

```python
import math

import jax
import jax.numpy as jnp
from jax import lax
from jax.experimental import pallas as pl
from jax.experimental.pallas import tpu as pltpu
from jax.sharding import PartitionSpec as P

D = 16384
BF = jnp.bfloat16
F32 = jnp.float32
MESH = pl.DeviceIdType.MESH
ORDER = (2, 1, 3, 0)


def iota(shape, axis):
    return lax.broadcasted_iota(jnp.int32, shape, axis)


def selection(source, rows=256):
    t = iota((rows, 256), 0)
    return (iota((rows, 256), 1) == source(t)).astype(F32).astype(BF)


def arrived(ref, sem):
    pltpu.make_async_copy(ref, ref, sem).wait()


def attend(q, fresh, lens, kv, kv_copies, sco):
    scale = 1.0 / math.sqrt(128)
    for i in range(2):
        kv_copies[i * 2].wait()
        for g in range(8):
            at = (i * 8 + g) * 16
            sco[at : at + 16, :] = lax.dot_general(
                q[at : at + 16, :],
                kv[i, :, g * 128 : (g + 1) * 128],
                (((1,), (1,)), ((), ())),
                preferred_element_type=F32,
            )
    first = iota((256, 1), 0) < 128
    length = jnp.where(first, lens[0], lens[1])
    scores = jnp.where(iota((256, 256), 1) < length, sco[...] * scale, jnp.float32(-1e30))

    def spread(offset):
        rows = [
            jnp.broadcast_to(fresh[i * 16 + offset + g : i * 16 + offset + g + 1, :], (16, 128))
            for i in range(2)
            for g in range(8)
        ]
        return jnp.concatenate(rows, axis=0)

    own = jnp.sum(q[...].astype(F32) * spread(0), axis=1, keepdims=True) * scale
    top = jnp.maximum(jnp.max(scores, axis=1, keepdims=True), own)
    expo = jnp.exp(scores - top)
    own_exp = jnp.exp(own - top)
    total = jnp.sum(expo, axis=1, keepdims=True) + own_exp
    weights = (expo / total).astype(BF)
    own_weight = (own_exp / total).astype(BF).astype(F32)
    parts = []
    for i in range(2):
        kv_copies[i * 2 + 1].wait()
        for g in range(8):
            at = (i * 8 + g) * 16
            parts.append(
                jnp.dot(
                    weights[at : at + 16, :],
                    kv[i, :, 1024 + g * 128 : 1024 + (g + 1) * 128],
                    preferred_element_type=F32,
                )
            )
    return (jnp.concatenate(parts, axis=0) + own_weight * spread(8)).astype(BF)


def kernel(
    q_hbm, fresh_hbm, lens, kv_hbm, res_hbm, gain_hbm, ow_hbm, gw_hbm, uw_hbm, dw_hbm, out,
    wide, wide_f, narrow, narrow_f, q, res_src, gain_in, gain, fin_f,
    kv, sco, m1s, m1, comb, m2s,
    ow, gw, uw, dw, m2, m2all, lhs, rin, resid, acc,
    own, cs, cr, qs, ya, yb, yfm, yfp, zs, zin, tot,
    sbuf, gu, ss, xs, xr, hid,
    own2, cs2, cr2, qs2, ya2, yb2, yfm2, yfp2, zs2, zin2, tot2, fo, fb, fin_in,
    in_sem, w_sem, kv_sem, m1_s, m1_r, m2_s, m2_r, rs_s, rs_r, xa_s, xa_r,
    c_s, c_r, y_s, y_r, z_s, z_r, az_s, ay_s, ac_s, ag_r, ac_r,
    xs_s, xs_r, xh_s, xh_r, c2_s, c2_r, y2_s, y2_r, z2_s, z2_r, f_s, f_r,
):
    side, f, h = lax.axis_index("side"), lax.axis_index("fin"), lax.axis_index("fhid")
    y, z, c = h // 8, (h // 2) % 4, h % 2
    yz = h // 2
    oc = 1 - c
    j = f * 2 + c
    zt = 3 - z
    copies = []

    def at(s, ff, yy, zz, cc):
        return (s, ff, (yy * 4 + zz) * 2 + cc)

    def send(src, dst, s_sem, r_sem, dev):
        cp = pltpu.make_async_remote_copy(
            src_ref=src, dst_ref=dst, send_sem=s_sem, recv_sem=r_sem,
            device_id=dev, device_id_type=MESH,
        )
        cp.start()
        copies.append(cp)

    barrier = pltpu.get_barrier_semaphore()

    def greet(dev):
        pl.semaphore_signal(barrier, inc=1, device_id=dev, device_id_type=MESH)

    def deliver():
        for s in range(8):
            arrived(fin_in.at[s], f_r.at[s])
        fin_f[...] = fin_in[...].astype(F32)
        parts = [fin_f[s, :, k, :] for s in range(8) for k in range(16)]
        out[...] = jnp.concatenate(parts, axis=1).astype(BF)

    @pl.when(side == 0)
    def _attention_side():
        kv_copies = []
        for i in range(2):
            for k in range(2):
                part = (i, slice(None), pl.ds(k * 1024, 1024))
                cp = pltpu.make_async_copy(kv_hbm.at[part], kv.at[part], kv_sem.at[i * 2 + k])
                cp.start()
                kv_copies.append(cp)
        first_in = pltpu.make_async_copy(q_hbm, wide, in_sem.at[0])
        second_in = pltpu.make_async_copy(fresh_hbm, narrow, in_sem.at[1])
        first_in.start()
        second_in.start()
        greet(at(0, f, y, z, oc))
        for d in range(8):
            greet(at(1, d // 2, y, zt, d % 2))
        first_in.wait()
        second_in.wait()
        value = wide[...].astype(F32)
        for k in range(128):
            wide_f[:, k, :] = value[:, k * 128 : (k + 1) * 128]
        q[...] = wide_f[...].reshape(256, 128).astype(BF)
        value = narrow[...].astype(F32)
        for k in range(16):
            narrow_f[:, k, :] = value[:, k * 128 : (k + 1) * 128]
        fresh = narrow_f[...].reshape(32, 128)
        mixed = attend(q, fresh, lens, kv, kv_copies, sco)
        sel = selection(
            lambda t: (t // 4) % 2 * 128 + (t // 8) % 16 * 8 + (t // 128 + c) % 2 * 4 + t % 4
        )
        moved_rows = jnp.dot(sel, mixed, preferred_element_type=F32)
        m1s[...] = moved_rows[128:, :].astype(BF)
        comb[:, pl.ds(pl.multiple_of(c * 8, 8), 8), :] = moved_rows[:128, :].reshape(16, 8, 128)
        pl.semaphore_wait(barrier, 17)
        send(m1s, m1, m1_s, m1_r, at(0, f, y, z, oc))
        arrived(m1, m1_r)
        comb[:, pl.ds(pl.multiple_of(oc * 8, 8), 8), :] = m1[...].astype(F32).reshape(16, 8, 128)
        m2s[...] = comb[...].reshape(256, 128).astype(BF)
        for b in range(16):
            send(
                m2s.at[pl.ds(b * 16, 16)],
                m2.at[pl.ds(pl.multiple_of(yz * 16, 16), 16)],
                m2_s.at[b],
                m2_r.at[yz],
                at(1, f, b // 4, b % 4, c),
            )
        for cp in copies:
            cp.wait_send()
        deliver()

    @pl.when(side == 1)
    def _mlp_side():
        copies.clear()
        up, down, far = (y + 1) % 4, (y + 3) % 4, (y + 2) % 4
        dev_up, dev_down = at(1, f, up, z, c), at(1, f, down, z, c)
        dev_core = at(1, f, y, z, oc)
        first_in = pltpu.make_async_copy(res_hbm, wide, in_sem.at[0])
        second_in = pltpu.make_async_copy(gain_hbm, gain_in, in_sem.at[1])
        first_in.start()
        second_in.start()
        for d in range(16):
            greet(at(0, f, d // 4, d % 4, c))
        for d in range(1, 4):
            greet(at(1, (f + d) % 4, y, z, c))
            greet(at(1, f, y, (z + d) % 4, c))
        greet(dev_up)
        greet(dev_down)
        greet(dev_core)
        for d in range(8):
            greet(at(1, d // 2, y, zt, d % 2))
        weights = [
            pltpu.make_async_copy(a, b, w_sem.at[k])
            for k, (a, b) in enumerate(((ow_hbm, ow), (gw_hbm, gw), (uw_hbm, uw), (dw_hbm, dw)))
        ]
        for cp in weights:
            cp.start()
        gu[...] = jnp.zeros_like(gu)
        ss[...] = jnp.zeros_like(ss)
        first_in.wait()
        second_in.wait()
        value = wide[...].astype(F32)
        for k in range(128):
            wide_f[:, k, :] = value[:, k * 128 : (k + 1) * 128]
        for k in range(4):
            rows = wide_f[:, k * 32 : (k + 1) * 32, :]
            res_src[k] = rows.reshape(64, 128).astype(BF)
        gain[...] = gain_in[...].astype(F32).reshape(32, 128)
        pl.semaphore_wait(barrier, 25)

        for d in range(1, 4):
            ff = (f + d) % 4
            send(res_src.at[ff], rin.at[f], rs_s.at[d], rs_r.at[f], at(1, ff, y, z, c))
        rin[f] = res_src[f]
        for d in range(1, 4):
            ff = (f + d) % 4
            arrived(rin.at[ff], rs_r.at[ff])
        sel = selection(
            lambda t: (t // 2) % 4 * 64 + ((t % 2) * 16 + (t // 8) % 16) * 2 + t // 128
        )
        resid[...] = jnp.dot(sel, rin[...].reshape(256, 128), preferred_element_type=F32)

        pick = selection(
            lambda t: (t // 8) % 16 * 16 + (t // 128) % 2 * 8 + t % 2 * 4 + t // 256, 1024
        )
        row_fin = (iota((1024, 128), 0) // 2) % 4
        for s in range(16):
            arrived(m2.at[pl.ds(s * 16, 16)], m2_r.at[s])
        for d in range(1, 4):
            ff = (f + d) % 4
            send(m2, m2all.at[f], xa_s.at[d], xa_r.at[f], at(1, ff, y, z, c))
        picked = jnp.where(
            row_fin == f, jnp.dot(pick, m2[...], preferred_element_type=F32), 0.0
        )
        for d in (1, 3, 2):
            ff = (f + d) % 4
            arrived(m2all.at[ff], xa_r.at[ff])
            picked = jnp.where(
                row_fin == ff, jnp.dot(pick, m2all[ff], preferred_element_type=F32), picked
            )
        for k in range(4):
            lhs[:, k * 128 : (k + 1) * 128] = picked[k * 256 : (k + 1) * 256, :].astype(BF)
        weights[0].wait()

        def project(p, g):
            mine = (c == p).astype(F32)
            yy = (y + ORDER[g]) % 4

            def chunk(k, carry):
                n = yy * 4 + k
                w = ow[:, pl.ds(pl.multiple_of(n * 256, 256), 256)]
                acc[...] = jnp.dot(
                    lhs[p * 128 : (p + 1) * 128, :], w, preferred_element_type=F32
                )
                r8 = pl.ds(pl.multiple_of(yz * 8, 8), 8)
                lo = resid[pl.ds(pl.multiple_of(n * 8, 8), 8), :]
                hi = resid[pl.ds(pl.multiple_of(128 + n * 8, 8), 8), :]
                acc[r8, :] = acc[r8, :] + jnp.concatenate([lo, hi], axis=1) * mine
                own[p, n] = acc[pl.ds(pl.multiple_of(c * 64, 64), 64), :]
                cs[p, n] = acc[pl.ds(pl.multiple_of(oc * 64, 64), 64), :].astype(BF)
                return carry

            lax.fori_loop(0, 4, chunk, 0)
            part = pl.ds(yy * 4, 4)
            send(cs.at[p, part], cr.at[p, part], c_s.at[p, g], c_r.at[p, g], dev_core)

        a, b = pl.ds(0, 2), pl.ds(2, 2)

        def paired(p, yy, half):
            part = pl.ds(yy * 4 + half * 2, 2)
            return own[p, part] + cr[p, part].astype(F32)

        def opposite(p):
            arrived(cr.at[p, pl.ds(far * 4, 4)], c_r.at[p, 0])
            qs[p, far, a] = paired(p, far, 0).astype(BF)
            send(qs.at[p, far, a], ya.at[p], y_s.at[p, 0], y_r.at[p, 0], dev_up)
            qs[p, far, b] = paired(p, far, 1).astype(BF)
            send(qs.at[p, far, b], yb.at[p], y_s.at[p, 1], y_r.at[p, 1], dev_down)

        def beside(p):
            arrived(cr.at[p, pl.ds(up * 4, 4)], c_r.at[p, 1])
            qs[p, up, b] = paired(p, up, 1).astype(BF)
            send(qs.at[p, up, b], yfm.at[p, b], y_s.at[p, 2], y_r.at[p, 2], dev_up)
            arrived(cr.at[p, pl.ds(down * 4, 4)], c_r.at[p, 2])
            qs[p, down, a] = paired(p, down, 0).astype(BF)
            send(qs.at[p, down, a], yfp.at[p, a], y_s.at[p, 3], y_r.at[p, 3], dev_down)

        def onward(p):
            arrived(ya.at[p], y_r.at[p, 0])
            qs[p, up, a] = (paired(p, up, 0) + ya[p].astype(F32)).astype(BF)
            send(qs.at[p, up, a], yfm.at[p, a], y_s.at[p, 4], y_r.at[p, 4], dev_up)
            arrived(yb.at[p], y_r.at[p, 1])
            qs[p, down, b] = (paired(p, down, 1) + yb[p].astype(F32)).astype(BF)
            send(qs.at[p, down, b], yfp.at[p, b], y_s.at[p, 5], y_r.at[p, 5], dev_down)

        def over_z(p):
            part = pl.ds(y * 4, 4)
            arrived(cr.at[p, part], c_r.at[p, 3])
            arrived(yfm.at[p, b], y_r.at[p, 2])
            arrived(yfp.at[p, a], y_r.at[p, 3])
            arrived(yfm.at[p, a], y_r.at[p, 4])
            arrived(yfp.at[p, b], y_r.at[p, 5])

            def summed(k):
                value = own[p, y * 4 + k] + cr[p, y * 4 + k].astype(F32)
                return value + yfm[p, k].astype(F32) + yfp[p, k].astype(F32)

            for d in (2, 1, 3):
                zz = (z + d) % 4
                zs[p, zz] = summed(zz).astype(BF)
                send(zs.at[p, zz], zin.at[p, z], z_s.at[p, d], z_r.at[p, z], at(1, f, y, zz, c))
            tot[p] = summed(z)

        def give(p, n, slot, dev):
            ref = sbuf.at[p, n, c]
            send(ref, ref, ay_s.at[p, slot], ag_r.at[p, n], dev)

        def give_y(p, n, k):
            give(p, n, 2 * k, dev_up)
            give(p, n, 2 * k + 1, dev_down)

        def give_core(p, n):
            ref = sbuf.at[p, n, c]
            send(ref, ref, ac_s.at[p, n], ac_r.at[p, n], dev_core)

        def use(p, n):
            arrived(sbuf.at[p, n, oc], ac_r.at[p, n])
            x = sbuf[p, n].reshape(128, 256).astype(F32)
            sq = x * x
            ss[p] += sq[:, :128] + sq[:, 128:]
            pair = [gain[pl.ds(n * 2 + k, 1), :] for k in range(2)]
            xg = (x * jnp.concatenate(pair, axis=1)).astype(BF)
            rows = pl.ds(pl.multiple_of(n * 256, 256), 256)
            gu[p, :, :256] += jnp.dot(xg, gw[rows, :], preferred_element_type=F32)
            gu[p, :, 256:] += jnp.dot(xg, uw[rows, :], preferred_element_type=F32)

        def near(p):
            total = tot[p]
            for d in (1, 3, 2):
                zz = (z + d) % 4
                arrived(zin.at[p, zz], z_r.at[p, zz])
                total = total + zin[p, zz].astype(F32)
            sbuf[p, yz, c] = total.astype(BF)
            for d in (2, 1, 3):
                zz = (z + d) % 4
                ref = sbuf.at[p, yz, c]
                send(ref, ref, az_s.at[p, d], ag_r.at[p, yz], at(1, f, y, zz, c))
            give_y(p, yz, 0)
            give_core(p, yz)

        def forward(p):
            for d in range(1, 4):
                n = y * 4 + (z + d) % 4
                arrived(sbuf.at[p, n, c], ag_r.at[p, n])
                give_y(p, n, d)
                give_core(p, n)

        def beside_arrived(p, d):
            n = down * 4 + (z + d) % 4
            arrived(sbuf.at[p, n, c], ag_r.at[p, n])
            if d % 2 == 0:
                give(p, n, 8 + d, dev_up)
            give_core(p, n)
            n = up * 4 + (z + d) % 4
            arrived(sbuf.at[p, n, c], ag_r.at[p, n])
            if d % 2 == 1:
                give(p, n, 8 + d, dev_down)
            give_core(p, n)

        def opposite_arrived(p, d):
            n = far * 4 + (z + d) % 4
            arrived(sbuf.at[p, n, c], ag_r.at[p, n])
            give_core(p, n)

        def use_all(p, group):
            for d in range(4):
                use(p, group * 4 + (z + d) % 4)

        def over_fin(p):
            tt = jnp.sum(ss[p], axis=1, keepdims=True)
            top = tt.astype(BF).astype(F32)
            low = iota((128, 128), 1) < 64
            xs[p, :, :, 512:] = jnp.where(low, top, tt - top).astype(BF).reshape(4, 32, 128)
            xs[p, :, :, :512] = gu[p].astype(BF).reshape(4, 32, 512)
            for d in (2, 1, 3):
                ff = (f + d) % 4
                send(xs.at[p, ff], xr.at[p, f], xs_s.at[p, d], xs_r.at[p, f], at(1, ff, y, z, c))

        def hide(p):
            mine = pl.ds(pl.multiple_of(f * 32, 32), 32)
            both = gu[p, mine, :]
            square = xs[p, f][:, 512:].astype(F32)
            for d in (1, 3, 2):
                ff = (f + d) % 4
                arrived(xr.at[p, ff], xs_r.at[p, ff])
                both = both + xr[p, ff][:, :512].astype(F32)
                square = square + xr[p, ff][:, 512:].astype(F32)
            scale = lax.rsqrt((square[:, 0:1] + square[:, 64:65]) / D + 1e-05)
            gate = both[:, :256] * scale
            hid[p, mine, :] = (gate / (1.0 + jnp.exp(-gate)) * (both[:, 256:] * scale)).astype(BF)
            for d in (2, 1, 3):
                ff = (f + d) % 4
                ref = hid.at[p, mine]
                send(ref, ref, xh_s.at[p, d], xh_r.at[p, f], at(1, ff, y, z, c))

        def lower(p):
            for d in (1, 3, 2):
                ff = (f + d) % 4
                ref = hid.at[p, pl.ds(pl.multiple_of(ff * 32, 32), 32)]
                arrived(ref, xh_r.at[p, ff])

            def columns(core, k):
                parts = []
                for half in range(2):
                    start = core * 2048 + half * 1024 + k * 512
                    w = dw[:, pl.ds(pl.multiple_of(start, 512), 512)]
                    value = jnp.dot(hid[p], w, preferred_element_type=F32)
                    parts.append(value.reshape(16, 8, 512))
                return jnp.concatenate(parts, axis=1)

            for k in range(2):
                cs2[p, :, :, k * 512 : (k + 1) * 512] = columns(oc, k).astype(BF)
            for g in range(4):
                part = pl.ds((y + ORDER[g]) % 4 * 4, 4)
                send(cs2.at[p, part], cr2.at[p, part], c2_s.at[p, g], c2_r.at[p, g], dev_core)
            for k in range(2):
                own2[p, :, :, k * 512 : (k + 1) * 512] = columns(c, k)

        def paired2(p, yy, half):
            part = pl.ds(yy * 4 + half * 2, 2)
            return own2[p, part] + cr2[p, part].astype(F32)

        def opposite2(p):
            arrived(cr2.at[p, pl.ds(far * 4, 4)], c2_r.at[p, 0])
            qs2[p, far, a] = paired2(p, far, 0).astype(BF)
            send(qs2.at[p, far, a], ya2.at[p], y2_s.at[p, 0], y2_r.at[p, 0], dev_up)
            qs2[p, far, b] = paired2(p, far, 1).astype(BF)
            send(qs2.at[p, far, b], yb2.at[p], y2_s.at[p, 1], y2_r.at[p, 1], dev_down)

        def beside2(p):
            arrived(cr2.at[p, pl.ds(up * 4, 4)], c2_r.at[p, 1])
            qs2[p, up, b] = paired2(p, up, 1).astype(BF)
            send(qs2.at[p, up, b], yfm2.at[p, b], y2_s.at[p, 2], y2_r.at[p, 2], dev_up)
            arrived(cr2.at[p, pl.ds(down * 4, 4)], c2_r.at[p, 2])
            qs2[p, down, a] = paired2(p, down, 0).astype(BF)
            send(qs2.at[p, down, a], yfp2.at[p, a], y2_s.at[p, 3], y2_r.at[p, 3], dev_down)

        def onward2(p):
            arrived(ya2.at[p], y2_r.at[p, 0])
            qs2[p, up, a] = (paired2(p, up, 0) + ya2[p].astype(F32)).astype(BF)
            send(qs2.at[p, up, a], yfm2.at[p, a], y2_s.at[p, 4], y2_r.at[p, 4], dev_up)
            arrived(yb2.at[p], y2_r.at[p, 1])
            qs2[p, down, b] = (paired2(p, down, 1) + yb2[p].astype(F32)).astype(BF)
            send(qs2.at[p, down, b], yfp2.at[p, b], y2_s.at[p, 5], y2_r.at[p, 5], dev_down)

        def over_z2(p):
            part = pl.ds(y * 4, 4)
            arrived(cr2.at[p, part], c2_r.at[p, 3])
            arrived(yfm2.at[p, b], y2_r.at[p, 2])
            arrived(yfp2.at[p, a], y2_r.at[p, 3])
            arrived(yfm2.at[p, a], y2_r.at[p, 4])
            arrived(yfp2.at[p, b], y2_r.at[p, 5])

            def summed(k):
                value = own2[p, y * 4 + k] + cr2[p, y * 4 + k].astype(F32)
                return value + yfm2[p, k].astype(F32) + yfp2[p, k].astype(F32)

            for d in (2, 1, 3):
                zz = (z + d) % 4
                zs2[p, zz] = summed(3 - zz).astype(BF)
                send(
                    zs2.at[p, zz], zin2.at[p, z], z2_s.at[p, d], z2_r.at[p, z], at(1, f, y, zz, c)
                )
            slab = pl.ds(pl.multiple_of(((y * 4 + zt) % 8) // 2 * 16, 16), 16)
            halves = []
            for half in range(2):
                kept = [
                    sbuf[p, c * 8 + half * 4 + m, y // 2, slab, :].astype(F32) for m in range(4)
                ]
                kept = jnp.concatenate(kept, axis=1)
                halves.append(jnp.where(zt % 2 == 0, kept[:8], kept[8:]))
            tot2[p] = summed(zt) + jnp.concatenate(halves, axis=0)

        def finish(p):
            total = tot2[p]
            for d in (1, 3, 2):
                zz = (z + d) % 4
                arrived(zin2.at[p, zz], z2_r.at[p, zz])
                total = total + zin2[p, zz].astype(F32)
            for k in range(16):
                rows = slice(k // 8 * 8, k // 8 * 8 + 8)
                fo[:, k, :] = total[rows, k % 8 * 128 : (k % 8 + 1) * 128]
            fb[p] = fo[...].astype(BF)
            for d in range(8):
                ff = (f + d // 2) % 4
                send(
                    fb.at[p, pl.ds(ff * 2, 2)], fin_in.at[j], f_s.at[p, d], f_r.at[j],
                    at(d % 2, ff, y, zt, p),
                )

        project(0, 0)
        project(1, 0)
        opposite(0)
        project(0, 1)
        opposite(1)
        project(0, 2)
        project(1, 1)
        beside(0)
        project(1, 2)
        project(0, 3)
        beside(1)
        project(1, 3)
        onward(0)
        onward(1)
        over_z(0)
        over_z(1)
        near(0)
        near(1)
        weights[1].wait()
        weights[2].wait()
        forward(0)
        forward(1)
        for d in range(4):
            beside_arrived(0, d)
            use(0, y * 4 + (z + d) % 4)
        for d in range(4):
            beside_arrived(1, d)
            use(0, down * 4 + (z + d) % 4)
            use(0, up * 4 + (z + d) % 4)
        for d in range(4):
            opposite_arrived(0, d)
            use(1, y * 4 + (z + d) % 4)
        use_all(0, far)
        over_fin(0)
        for d in range(4):
            opposite_arrived(1, d)
            use(1, down * 4 + (z + d) % 4)
            use(1, up * 4 + (z + d) % 4)
        use_all(1, far)
        over_fin(1)
        hide(0)
        hide(1)
        weights[3].wait()
        lower(0)
        opposite2(0)
        beside2(0)
        lower(1)
        opposite2(1)
        beside2(1)
        onward2(0)
        onward2(1)
        over_z2(0)
        over_z2(1)
        finish(0)
        finish(1)
        deliver()
        for cp in copies:
            cp.wait_send()


def moved(*args):
    def v(*shape, dtype=BF):
        return pltpu.VMEM(shape, dtype)

    scratch = [
        v(2, D), v(2, 128, 128, dtype=F32), v(2, 2048), v(2, 16, 128, dtype=F32), v(256, 128),
        v(4, 64, 128), v(4096), v(32, 128, dtype=F32), v(8, 2, 16, 128, dtype=F32),
        v(2, 256, 2048), v(256, 256, dtype=F32), v(128, 128), v(128, 128),
        v(16, 16, 128, dtype=F32), v(256, 128),
        v(512, 4096), v(4096, 256), v(4096, 256), v(256, 4096),
        v(256, 128), v(4, 256, 128), v(256, 512),
        v(4, 64, 128), v(256, 128, dtype=F32), v(128, 256, dtype=F32),
        v(2, 16, 64, 256, dtype=F32), v(2, 16, 64, 256), v(2, 16, 64, 256), v(2, 4, 4, 64, 256),
        v(2, 2, 64, 256), v(2, 2, 64, 256), v(2, 4, 64, 256), v(2, 4, 64, 256),
        v(2, 4, 64, 256), v(2, 4, 64, 256), v(2, 64, 256, dtype=F32),
        v(2, 16, 2, 64, 256), v(2, 128, 512, dtype=F32), v(2, 128, 128, dtype=F32),
        v(2, 4, 32, 640), v(2, 4, 32, 640), v(2, 128, 256),
        v(2, 16, 16, 1024, dtype=F32), v(2, 16, 16, 1024), v(2, 16, 16, 1024),
        v(2, 4, 4, 16, 1024), v(2, 2, 16, 1024), v(2, 2, 16, 1024),
        v(2, 4, 16, 1024), v(2, 4, 16, 1024), v(2, 4, 16, 1024), v(2, 4, 16, 1024),
        v(2, 16, 1024, dtype=F32), v(8, 16, 128, dtype=F32), v(2, 8, 16, 128), v(8, 2, 16, 128),
    ]
    counts = [
        (2,), (4,), (4,), (), (), (16,), (16,), (4,), (4,), (4,), (4,),
        (2, 4), (2, 4), (2, 6), (2, 6), (2, 4), (2, 4),
        (2, 4), (2, 12), (2, 16), (2, 16), (2, 16),
        (2, 4), (2, 4), (2, 4), (2, 4), (2, 4), (2, 4), (2, 6), (2, 6), (2, 4), (2, 4),
        (2, 8), (8,),
    ]
    scratch += [pltpu.SemaphoreType.DMA(k) for k in counts]
    vm, hbm = pl.BlockSpec(memory_space=pltpu.VMEM), pl.BlockSpec(memory_space=pl.ANY)
    sm = pl.BlockSpec(memory_space=pltpu.SMEM)
    return pl.pallas_call(
        kernel,
        out_shape=jax.ShapeDtypeStruct((2, D), BF),
        in_specs=[hbm, hbm, sm, hbm, hbm, hbm, hbm, hbm, hbm, hbm],
        out_specs=vm,
        scratch_shapes=scratch,
        compiler_params=pltpu.CompilerParams(
            collective_id=0, has_side_effects=True, vmem_limit_bytes=56 * 1024 * 1024
        ),
    )(*args)


def on_device(
    queries, new_entries, cached_entries, lengths, residual, norm_gain,
    out_weight, gate_weight, up_weight, down_weight,
):
    return moved(
        queries, new_entries, lengths, cached_entries[0], residual, norm_gain,
        out_weight[0], gate_weight[0], up_weight[0], down_weight[0],
    )


def solution(mesh):
    placed = (
        P(("fin", "fhid"), None),
        P(("fin", "fhid"), None),
        P("side", ("fin", "fhid"), None, None),
        P(("fin", "fhid")),
        P(("fin", "fhid"), None),
        P("fin"),
        P("side", "fhid", "fin"),
        P("side", "fin", "fhid"),
        P("side", "fin", "fhid"),
        P("side", "fhid", "fin"),
    )
    return jax.shard_map(
        on_device, mesh=mesh, in_specs=placed, out_specs=P(("fin", "fhid"), None), check_vma=False
    )
```

```python
import math

import jax
import jax.numpy as jnp
from jax import lax
from jax.experimental import pallas as pl
from jax.experimental.pallas import tpu as pltpu
from jax.sharding import PartitionSpec as P

D = 16384
BF = jnp.bfloat16
F32 = jnp.float32
MESH = pl.DeviceIdType.MESH
ORDER = (1, 3, 2, 0)


def iota(shape, axis):
    return lax.broadcasted_iota(jnp.int32, shape, axis)


def selection(source, rows=256):
    t = iota((rows, 256), 0)
    return (iota((rows, 256), 1) == source(t)).astype(F32).astype(BF)


def arrived(ref, sem):
    pltpu.make_async_copy(ref, ref, sem).wait()


def attend(q, fresh, lens, kv, kv_copies, sco):
    scale = 1.0 / math.sqrt(128)
    for i in range(2):
        kv_copies[i * 2].wait()
        for g in range(8):
            at = (i * 8 + g) * 16
            sco[at : at + 16, :] = lax.dot_general(
                q[at : at + 16, :],
                kv[i, :, g * 128 : (g + 1) * 128],
                (((1,), (1,)), ((), ())),
                preferred_element_type=F32,
            )
    first = iota((256, 1), 0) < 128
    length = jnp.where(first, lens[0], lens[1])
    scores = jnp.where(iota((256, 256), 1) < length, sco[...] * scale, jnp.float32(-1e30))

    def spread(offset):
        rows = [
            jnp.broadcast_to(fresh[i * 16 + offset + g : i * 16 + offset + g + 1, :], (16, 128))
            for i in range(2)
            for g in range(8)
        ]
        return jnp.concatenate(rows, axis=0)

    own = jnp.sum(q[...].astype(F32) * spread(0), axis=1, keepdims=True) * scale
    top = jnp.maximum(jnp.max(scores, axis=1, keepdims=True), own)
    expo = jnp.exp(scores - top)
    own_exp = jnp.exp(own - top)
    total = jnp.sum(expo, axis=1, keepdims=True) + own_exp
    weights = (expo / total).astype(BF)
    own_weight = (own_exp / total).astype(BF).astype(F32)
    parts = []
    for i in range(2):
        kv_copies[i * 2 + 1].wait()
        for g in range(8):
            at = (i * 8 + g) * 16
            parts.append(
                jnp.dot(
                    weights[at : at + 16, :],
                    kv[i, :, 1024 + g * 128 : 1024 + (g + 1) * 128],
                    preferred_element_type=F32,
                )
            )
    return (jnp.concatenate(parts, axis=0) + own_weight * spread(8)).astype(BF)


def kernel(
    q_hbm, fresh_hbm, lens, kv_hbm, res_hbm, gain_hbm, ow_hbm, gw_hbm, uw_hbm, dw_hbm, out,
    wide, wide_f, narrow, narrow_f, q, res_src, gain_in, gain, fin_f,
    kv, sco, m1s, m1, comb, m2s,
    ow, gw, uw, dw, m2, m2all, lhs, rin, resid, acc,
    own, cs, cr, qs, zfar, fs, ffar, yfm, yfp, zs, zin, tot,
    sbuf, gu, ss, xs, xr, hid,
    own2, cs2, cr2, qs2, zfar2, fs2, ffar2, yfm2, yfp2, zs2, zin2, tot2, fo, fb, fin_in,
    in_sem, w_sem, kv_sem, m1_s, m1_r, m2_s, m2_r, rs_s, rs_r, xa_s, xa_r,
    c_s, c_r, y_s, y_r, z_s, z_r, zf_s, zf_r, az_s, ay_s, ac_s, ag_r, ac_r,
    xs_s, xs_r, xh_s, xh_r, c2_s, c2_r, y2_s, y2_r, z2_s, z2_r, zf2_s, zf2_r, f_s, f_r,
):
    side, f, h = lax.axis_index("side"), lax.axis_index("fin"), lax.axis_index("fhid")
    y, z, c = h // 8, (h // 2) % 4, h % 2
    yz = h // 2
    oc = 1 - c
    j = f * 2 + c
    zt = 3 - z
    copies = []

    def at(s, ff, yy, zz, cc):
        return (s, ff, (yy * 4 + zz) * 2 + cc)

    def send(src, dst, s_sem, r_sem, dev):
        cp = pltpu.make_async_remote_copy(
            src_ref=src, dst_ref=dst, send_sem=s_sem, recv_sem=r_sem,
            device_id=dev, device_id_type=MESH,
        )
        cp.start()
        copies.append(cp)

    barrier = pltpu.get_barrier_semaphore()

    def greet(dev):
        pl.semaphore_signal(barrier, inc=1, device_id=dev, device_id_type=MESH)

    def deliver():
        for s in range(8):
            arrived(fin_in.at[s], f_r.at[s])
        fin_f[...] = fin_in[...].astype(F32)
        parts = [fin_f[s, :, k, :] for s in range(8) for k in range(16)]
        out[...] = jnp.concatenate(parts, axis=1).astype(BF)

    @pl.when(side == 0)
    def _attention_side():
        kv_copies = []
        for i in range(2):
            for k in range(2):
                part = (i, slice(None), pl.ds(k * 1024, 1024))
                cp = pltpu.make_async_copy(kv_hbm.at[part], kv.at[part], kv_sem.at[i * 2 + k])
                cp.start()
                kv_copies.append(cp)
        first_in = pltpu.make_async_copy(q_hbm, wide, in_sem.at[0])
        second_in = pltpu.make_async_copy(fresh_hbm, narrow, in_sem.at[1])
        first_in.start()
        second_in.start()
        greet(at(0, f, y, z, oc))
        for d in range(8):
            greet(at(1, d // 2, y, zt, d % 2))
        first_in.wait()
        second_in.wait()
        value = wide[...].astype(F32)
        for k in range(128):
            wide_f[:, k, :] = value[:, k * 128 : (k + 1) * 128]
        q[...] = wide_f[...].reshape(256, 128).astype(BF)
        value = narrow[...].astype(F32)
        for k in range(16):
            narrow_f[:, k, :] = value[:, k * 128 : (k + 1) * 128]
        fresh = narrow_f[...].reshape(32, 128)
        mixed = attend(q, fresh, lens, kv, kv_copies, sco)
        sel = selection(
            lambda t: (t // 4) % 2 * 128 + (t // 8) % 16 * 8 + (t // 128 + c) % 2 * 4 + t % 4
        )
        moved_rows = jnp.dot(sel, mixed, preferred_element_type=F32)
        m1s[...] = moved_rows[128:, :].astype(BF)
        comb[:, pl.ds(pl.multiple_of(c * 8, 8), 8), :] = moved_rows[:128, :].reshape(16, 8, 128)
        pl.semaphore_wait(barrier, 17)
        send(m1s, m1, m1_s, m1_r, at(0, f, y, z, oc))
        arrived(m1, m1_r)
        comb[:, pl.ds(pl.multiple_of(oc * 8, 8), 8), :] = m1[...].astype(F32).reshape(16, 8, 128)
        m2s[...] = comb[...].reshape(256, 128).astype(BF)
        for b in range(16):
            send(
                m2s.at[pl.ds(b * 16, 16)],
                m2.at[pl.ds(pl.multiple_of(yz * 16, 16), 16)],
                m2_s.at[b],
                m2_r.at[yz],
                at(1, f, b // 4, b % 4, c),
            )
        for cp in copies:
            cp.wait_send()
        deliver()

    @pl.when(side == 1)
    def _mlp_side():
        copies.clear()
        up, down, far = (y + 1) % 4, (y + 3) % 4, (y + 2) % 4
        dev_up, dev_down, dev_far = (at(1, f, yy, z, c) for yy in (up, down, far))
        dev_core = at(1, f, y, z, oc)
        first_in = pltpu.make_async_copy(res_hbm, wide, in_sem.at[0])
        second_in = pltpu.make_async_copy(gain_hbm, gain_in, in_sem.at[1])
        first_in.start()
        second_in.start()
        for d in range(16):
            greet(at(0, f, d // 4, d % 4, c))
        for d in range(1, 4):
            greet(at(1, (f + d) % 4, y, z, c))
            greet(at(1, f, y, (z + d) % 4, c))
        greet(dev_up)
        greet(dev_down)
        greet(dev_far)
        greet(dev_core)
        for d in range(8):
            greet(at(1, d // 2, y, zt, d % 2))
        weights = [
            pltpu.make_async_copy(a, b, w_sem.at[k])
            for k, (a, b) in enumerate(((ow_hbm, ow), (gw_hbm, gw), (uw_hbm, uw), (dw_hbm, dw)))
        ]
        for cp in weights:
            cp.start()
        gu[...] = jnp.zeros_like(gu)
        ss[...] = jnp.zeros_like(ss)
        first_in.wait()
        second_in.wait()
        value = wide[...].astype(F32)
        for k in range(128):
            wide_f[:, k, :] = value[:, k * 128 : (k + 1) * 128]
        for k in range(4):
            rows = wide_f[:, k * 32 : (k + 1) * 32, :]
            res_src[k] = rows.reshape(64, 128).astype(BF)
        gain[...] = gain_in[...].astype(F32).reshape(32, 128)
        pl.semaphore_wait(barrier, 26)

        for d in range(1, 4):
            ff = (f + d) % 4
            send(res_src.at[ff], rin.at[f], rs_s.at[d], rs_r.at[f], at(1, ff, y, z, c))
        rin[f] = res_src[f]
        for d in range(1, 4):
            ff = (f + d) % 4
            arrived(rin.at[ff], rs_r.at[ff])
        sel = selection(
            lambda t: (t // 2) % 4 * 64 + ((t % 2) * 16 + (t // 8) % 16) * 2 + t // 128
        )
        resid[...] = jnp.dot(sel, rin[...].reshape(256, 128), preferred_element_type=F32)

        pick = selection(
            lambda t: (t // 8) % 16 * 16 + (t // 128) % 2 * 8 + t % 2 * 4 + t // 256, 1024
        )
        row_fin = (iota((1024, 128), 0) // 2) % 4
        for e in (0, 1, 3, 2):
            yy = (y + e) % 4
            for k in range(4):
                n = yy * 4 + k
                arrived(m2.at[pl.ds(pl.multiple_of(n * 16, 16), 16)], m2_r.at[n])
            part = pl.ds(pl.multiple_of(yy * 64, 64), 64)
            for d in (2, 1, 3):
                ff = (f + d) % 4
                send(
                    m2.at[part], m2all.at[f, part], xa_s.at[d, e], xa_r.at[f, yy],
                    at(1, ff, y, z, c),
                )
        picked = jnp.where(
            row_fin == f, jnp.dot(pick, m2[...], preferred_element_type=F32), 0.0
        )
        for d in (1, 3, 2):
            ff = (f + d) % 4
            for k in range(4):
                arrived(m2all.at[ff, pl.ds(k * 64, 64)], xa_r.at[ff, k])
            picked = jnp.where(
                row_fin == ff, jnp.dot(pick, m2all[ff], preferred_element_type=F32), picked
            )
        for k in range(4):
            lhs[:, k * 128 : (k + 1) * 128] = picked[k * 256 : (k + 1) * 256, :].astype(BF)
        weights[0].wait()

        def project(p, g):
            mine = (c == p).astype(F32)
            yy = (y + ORDER[g]) % 4

            def chunk(k, carry):
                n = yy * 4 + k
                w = ow[:, pl.ds(pl.multiple_of(n * 256, 256), 256)]
                acc[...] = jnp.dot(
                    lhs[p * 128 : (p + 1) * 128, :], w, preferred_element_type=F32
                )
                r8 = pl.ds(pl.multiple_of(yz * 8, 8), 8)
                lo = resid[pl.ds(pl.multiple_of(n * 8, 8), 8), :]
                hi = resid[pl.ds(pl.multiple_of(128 + n * 8, 8), 8), :]
                acc[r8, :] = acc[r8, :] + jnp.concatenate([lo, hi], axis=1) * mine
                own[p, n] = acc[pl.ds(pl.multiple_of(c * 64, 64), 64), :]
                cs[p, n] = acc[pl.ds(pl.multiple_of(oc * 64, 64), 64), :].astype(BF)
                return carry

            lax.fori_loop(0, 4, chunk, 0)
            part = pl.ds(yy * 4, 4)
            send(cs.at[p, part], cr.at[p, part], c_s.at[p, g], c_r.at[p, g], dev_core)

        def paired(p, n):
            return own[p, n] + cr[p, n].astype(F32)

        def beside(p, g):
            yy = (y + ORDER[g]) % 4
            part = pl.ds(yy * 4, 4)
            arrived(cr.at[p, part], c_r.at[p, g])
            qs[p, yy] = (own[p, part] + cr[p, part].astype(F32)).astype(BF)
            to, dev = ((yfm, dev_up), (yfp, dev_down))[g]
            send(qs.at[p, yy], to.at[p], y_s.at[p, g], y_r.at[p, g], dev)

        def opposite(p):
            arrived(cr.at[p, pl.ds(far * 4, 4)], c_r.at[p, 2])
            for d in (2, 1, 3):
                zz = (z + d) % 4
                qs[p, far, zz] = paired(p, far * 4 + zz).astype(BF)
                send(
                    qs.at[p, far, zz], zfar.at[p, z], zf_s.at[p, d], zf_r.at[p, z],
                    at(1, f, y, zz, c),
                )

        def onward(p):
            value = paired(p, far * 4 + z)
            for d in (1, 3, 2):
                zz = (z + d) % 4
                arrived(zfar.at[p, zz], zf_r.at[p, zz])
                value = value + zfar[p, zz].astype(F32)
            fs[p] = value.astype(BF)
            send(fs.at[p], ffar.at[p], y_s.at[p, 2], y_r.at[p, 2], dev_far)

        def over_z(p):
            part = pl.ds(y * 4, 4)
            arrived(cr.at[p, part], c_r.at[p, 3])
            arrived(yfm.at[p], y_r.at[p, 0])
            arrived(yfp.at[p], y_r.at[p, 1])

            def summed(k):
                return paired(p, y * 4 + k) + yfm[p, k].astype(F32) + yfp[p, k].astype(F32)

            for d in (2, 1, 3):
                zz = (z + d) % 4
                zs[p, zz] = summed(zz).astype(BF)
                send(zs.at[p, zz], zin.at[p, z], z_s.at[p, d], z_r.at[p, z], at(1, f, y, zz, c))
            tot[p] = summed(z)

        def give(p, n, slot, dev):
            ref = sbuf.at[p, n, c]
            send(ref, ref, ay_s.at[p, slot], ag_r.at[p, n], dev)

        def give_y(p, n, k):
            give(p, n, 2 * k, dev_up)
            give(p, n, 2 * k + 1, dev_down)

        def give_core(p, n):
            ref = sbuf.at[p, n, c]
            send(ref, ref, ac_s.at[p, n], ac_r.at[p, n], dev_core)

        def use(p, n):
            arrived(sbuf.at[p, n, oc], ac_r.at[p, n])
            x = sbuf[p, n].reshape(128, 256).astype(F32)
            sq = x * x
            ss[p] += sq[:, :128] + sq[:, 128:]
            pair = [gain[pl.ds(n * 2 + k, 1), :] for k in range(2)]
            xg = (x * jnp.concatenate(pair, axis=1)).astype(BF)
            rows = pl.ds(pl.multiple_of(n * 256, 256), 256)
            gu[p, :, :256] += jnp.dot(xg, gw[rows, :], preferred_element_type=F32)
            gu[p, :, 256:] += jnp.dot(xg, uw[rows, :], preferred_element_type=F32)

        def near(p):
            total = tot[p]
            for d in (1, 3, 2):
                zz = (z + d) % 4
                arrived(zin.at[p, zz], z_r.at[p, zz])
                total = total + zin[p, zz].astype(F32)
            arrived(ffar.at[p], y_r.at[p, 2])
            total = total + ffar[p].astype(F32)
            sbuf[p, yz, c] = total.astype(BF)
            for d in (2, 1, 3):
                zz = (z + d) % 4
                ref = sbuf.at[p, yz, c]
                send(ref, ref, az_s.at[p, d], ag_r.at[p, yz], at(1, f, y, zz, c))
            give_y(p, yz, 0)
            give(p, yz, 8, dev_far)
            give_core(p, yz)

        def forward(p):
            for d in range(1, 4):
                n = y * 4 + (z + d) % 4
                arrived(sbuf.at[p, n, c], ag_r.at[p, n])
                give_y(p, n, d)
                give_core(p, n)

        def spread_opposite(p):
            n = far * 4 + z
            arrived(sbuf.at[p, n, c], ag_r.at[p, n])
            for d in (2, 1, 3):
                ref = sbuf.at[p, n, c]
                send(
                    ref, ref, az_s.at[p, 4 + d], ag_r.at[p, n], at(1, f, y, (z + d) % 4, c)
                )
            give_core(p, n)

        def taken(p, group, d):
            n = group * 4 + (z + d) % 4
            arrived(sbuf.at[p, n, c], ag_r.at[p, n])
            give_core(p, n)

        def use_at(p, *places):
            for group, d in places:
                use(p, group * 4 + (z + d) % 4)

        def over_fin(p):
            tt = jnp.sum(ss[p], axis=1, keepdims=True)
            top = tt.astype(BF).astype(F32)
            low = iota((128, 128), 1) < 64
            xs[p, :, :, 512:] = jnp.where(low, top, tt - top).astype(BF).reshape(4, 32, 128)
            xs[p, :, :, :512] = gu[p].astype(BF).reshape(4, 32, 512)
            for d in (2, 1, 3):
                ff = (f + d) % 4
                send(xs.at[p, ff], xr.at[p, f], xs_s.at[p, d], xs_r.at[p, f], at(1, ff, y, z, c))

        def hide(p):
            mine = pl.ds(pl.multiple_of(f * 32, 32), 32)
            both = gu[p, mine, :]
            square = xs[p, f][:, 512:].astype(F32)
            for d in (1, 3, 2):
                ff = (f + d) % 4
                arrived(xr.at[p, ff], xs_r.at[p, ff])
                both = both + xr[p, ff][:, :512].astype(F32)
                square = square + xr[p, ff][:, 512:].astype(F32)
            scale = lax.rsqrt((square[:, 0:1] + square[:, 64:65]) / D + 1e-05)
            gate = both[:, :256] * scale
            hid[p, mine, :] = (gate / (1.0 + jnp.exp(-gate)) * (both[:, 256:] * scale)).astype(BF)
            for d in (2, 1, 3):
                ff = (f + d) % 4
                ref = hid.at[p, mine]
                send(ref, ref, xh_s.at[p, d], xh_r.at[p, f], at(1, ff, y, z, c))

        def lower(p):
            for d in (1, 3, 2):
                ff = (f + d) % 4
                ref = hid.at[p, pl.ds(pl.multiple_of(ff * 32, 32), 32)]
                arrived(ref, xh_r.at[p, ff])

            def columns(core, k):
                parts = []
                for half in range(2):
                    start = core * 2048 + half * 1024 + k * 512
                    w = dw[:, pl.ds(pl.multiple_of(start, 512), 512)]
                    value = jnp.dot(hid[p], w, preferred_element_type=F32)
                    parts.append(value.reshape(16, 8, 512))
                return jnp.concatenate(parts, axis=1)

            for k in range(2):
                cs2[p, :, :, k * 512 : (k + 1) * 512] = columns(oc, k).astype(BF)
            for g in range(4):
                part = pl.ds((y + ORDER[g]) % 4 * 4, 4)
                send(cs2.at[p, part], cr2.at[p, part], c2_s.at[p, g], c2_r.at[p, g], dev_core)
            for k in range(2):
                own2[p, :, :, k * 512 : (k + 1) * 512] = columns(c, k)

        def paired2(p, n):
            return own2[p, n] + cr2[p, n].astype(F32)

        def beside2(p, g):
            yy = (y + ORDER[g]) % 4
            part = pl.ds(yy * 4, 4)
            arrived(cr2.at[p, part], c2_r.at[p, g])
            qs2[p, yy] = (own2[p, part] + cr2[p, part].astype(F32)).astype(BF)
            to, dev = ((yfm2, dev_up), (yfp2, dev_down))[g]
            send(qs2.at[p, yy], to.at[p], y2_s.at[p, g], y2_r.at[p, g], dev)

        def opposite2(p):
            arrived(cr2.at[p, pl.ds(far * 4, 4)], c2_r.at[p, 2])
            for d in (2, 1, 3):
                zz = (z + d) % 4
                qs2[p, far, zz] = paired2(p, far * 4 + (3 - zz)).astype(BF)
                send(
                    qs2.at[p, far, zz], zfar2.at[p, z], zf2_s.at[p, d], zf2_r.at[p, z],
                    at(1, f, y, zz, c),
                )

        def onward2(p):
            value = paired2(p, far * 4 + zt)
            for d in (1, 3, 2):
                zz = (z + d) % 4
                arrived(zfar2.at[p, zz], zf2_r.at[p, zz])
                value = value + zfar2[p, zz].astype(F32)
            fs2[p] = value.astype(BF)
            send(fs2.at[p], ffar2.at[p], y2_s.at[p, 2], y2_r.at[p, 2], dev_far)

        def over_z2(p):
            part = pl.ds(y * 4, 4)
            arrived(cr2.at[p, part], c2_r.at[p, 3])
            arrived(yfm2.at[p], y2_r.at[p, 0])
            arrived(yfp2.at[p], y2_r.at[p, 1])

            def summed(k):
                return paired2(p, y * 4 + k) + yfm2[p, k].astype(F32) + yfp2[p, k].astype(F32)

            for d in (2, 1, 3):
                zz = (z + d) % 4
                zs2[p, zz] = summed(3 - zz).astype(BF)
                send(
                    zs2.at[p, zz], zin2.at[p, z], z2_s.at[p, d], z2_r.at[p, z], at(1, f, y, zz, c)
                )
            slab = pl.ds(pl.multiple_of(((y * 4 + zt) % 8) // 2 * 16, 16), 16)
            halves = []
            for half in range(2):
                kept = [
                    sbuf[p, c * 8 + half * 4 + m, y // 2, slab, :].astype(F32) for m in range(4)
                ]
                kept = jnp.concatenate(kept, axis=1)
                halves.append(jnp.where(zt % 2 == 0, kept[:8], kept[8:]))
            tot2[p] = summed(zt) + jnp.concatenate(halves, axis=0)

        def finish(p):
            total = tot2[p]
            for d in (1, 3, 2):
                zz = (z + d) % 4
                arrived(zin2.at[p, zz], z2_r.at[p, zz])
                total = total + zin2[p, zz].astype(F32)
            arrived(ffar2.at[p], y2_r.at[p, 2])
            total = total + ffar2[p].astype(F32)
            for k in range(16):
                rows = slice(k // 8 * 8, k // 8 * 8 + 8)
                fo[:, k, :] = total[rows, k % 8 * 128 : (k % 8 + 1) * 128]
            fb[p] = fo[...].astype(BF)
            for d in range(8):
                ff = (f + d // 2) % 4
                send(
                    fb.at[p, pl.ds(ff * 2, 2)], fin_in.at[j], f_s.at[p, d], f_r.at[j],
                    at(d % 2, ff, y, zt, p),
                )

        project(0, 0)
        project(0, 1)
        beside(0, 0)
        project(0, 2)
        beside(0, 1)
        project(1, 0)
        opposite(0)
        project(1, 1)
        beside(1, 0)
        project(1, 2)
        beside(1, 1)
        project(0, 3)
        opposite(1)
        project(1, 3)
        onward(0)
        over_z(0)
        onward(1)
        over_z(1)
        near(0)
        near(1)
        weights[1].wait()
        weights[2].wait()
        forward(0)
        forward(1)
        for p in range(2):
            spread_opposite(p)
            taken(p, up, 0)
            taken(p, down, 0)
        use_at(0, (y, 0), (y, 1), (y, 2), (y, 3), (up, 0), (down, 0), (far, 0))
        for d in range(1, 4):
            taken(0, up, d)
            taken(0, down, d)
            use_at(1, (y, d - 1))
            if d > 1:
                use_at(0, (up, d - 1), (down, d - 1))
        for d in range(1, 4):
            taken(0, far, d)
        use_at(0, (up, 3), (down, 3), (far, 1), (far, 2), (far, 3))
        over_fin(0)
        for d in range(1, 4):
            taken(1, up, d)
            taken(1, down, d)
            use_at(1, ((y, 3), (up, 0), (down, 0))[d - 1])
        use_at(1, (far, 0), (up, 1), (down, 1), (up, 2), (down, 2))
        for d in range(1, 4):
            taken(1, far, d)
        use_at(1, (up, 3), (down, 3), (far, 1), (far, 2), (far, 3))
        over_fin(1)
        hide(0)
        hide(1)
        weights[3].wait()
        lower(0)
        beside2(0, 0)
        beside2(0, 1)
        opposite2(0)
        lower(1)
        beside2(1, 0)
        beside2(1, 1)
        opposite2(1)
        onward2(0)
        over_z2(0)
        onward2(1)
        over_z2(1)
        finish(0)
        finish(1)
        deliver()
        for cp in copies:
            cp.wait_send()


def moved(*args):
    def v(*shape, dtype=BF):
        return pltpu.VMEM(shape, dtype)

    scratch = [
        v(2, D), v(2, 128, 128, dtype=F32), v(2, 2048), v(2, 16, 128, dtype=F32), v(256, 128),
        v(4, 64, 128), v(4096), v(32, 128, dtype=F32), v(8, 2, 16, 128, dtype=F32),
        v(2, 256, 2048), v(256, 256, dtype=F32), v(128, 128), v(128, 128),
        v(16, 16, 128, dtype=F32), v(256, 128),
        v(512, 4096), v(4096, 256), v(4096, 256), v(256, 4096),
        v(256, 128), v(4, 256, 128), v(256, 512),
        v(4, 64, 128), v(256, 128, dtype=F32), v(128, 256, dtype=F32),
        v(2, 16, 64, 256, dtype=F32), v(2, 16, 64, 256), v(2, 16, 64, 256), v(2, 4, 4, 64, 256),
        v(2, 4, 64, 256), v(2, 64, 256), v(2, 64, 256), v(2, 4, 64, 256), v(2, 4, 64, 256),
        v(2, 4, 64, 256), v(2, 4, 64, 256), v(2, 64, 256, dtype=F32),
        v(2, 16, 2, 64, 256), v(2, 128, 512, dtype=F32), v(2, 128, 128, dtype=F32),
        v(2, 4, 32, 640), v(2, 4, 32, 640), v(2, 128, 256),
        v(2, 16, 16, 1024, dtype=F32), v(2, 16, 16, 1024), v(2, 16, 16, 1024),
        v(2, 4, 4, 16, 1024), v(2, 4, 16, 1024), v(2, 16, 1024), v(2, 16, 1024),
        v(2, 4, 16, 1024), v(2, 4, 16, 1024), v(2, 4, 16, 1024), v(2, 4, 16, 1024),
        v(2, 16, 1024, dtype=F32), v(8, 16, 128, dtype=F32), v(2, 8, 16, 128), v(8, 2, 16, 128),
    ]
    counts = [
        (2,), (4,), (4,), (), (), (16,), (16,), (4,), (4,), (4, 4), (4, 4),
        (2, 4), (2, 4), (2, 3), (2, 3), (2, 4), (2, 4), (2, 4), (2, 4),
        (2, 8), (2, 9), (2, 16), (2, 16), (2, 16),
        (2, 4), (2, 4), (2, 4), (2, 4), (2, 4), (2, 4), (2, 3), (2, 3), (2, 4), (2, 4),
        (2, 4), (2, 4), (2, 8), (8,),
    ]
    scratch += [pltpu.SemaphoreType.DMA(k) for k in counts]
    vm, hbm = pl.BlockSpec(memory_space=pltpu.VMEM), pl.BlockSpec(memory_space=pl.ANY)
    sm = pl.BlockSpec(memory_space=pltpu.SMEM)
    return pl.pallas_call(
        kernel,
        out_shape=jax.ShapeDtypeStruct((2, D), BF),
        in_specs=[hbm, hbm, sm, hbm, hbm, hbm, hbm, hbm, hbm, hbm],
        out_specs=vm,
        scratch_shapes=scratch,
        compiler_params=pltpu.CompilerParams(
            collective_id=0, has_side_effects=True, vmem_limit_bytes=56 * 1024 * 1024
        ),
    )(*args)


def on_device(
    queries, new_entries, cached_entries, lengths, residual, norm_gain,
    out_weight, gate_weight, up_weight, down_weight,
):
    return moved(
        queries, new_entries, lengths, cached_entries[0], residual, norm_gain,
        out_weight[0], gate_weight[0], up_weight[0], down_weight[0],
    )


def solution(mesh):
    placed = (
        P(("fin", "fhid"), None),
        P(("fin", "fhid"), None),
        P("side", ("fin", "fhid"), None, None),
        P(("fin", "fhid")),
        P(("fin", "fhid"), None),
        P("fin"),
        P("side", "fhid", "fin"),
        P("side", "fin", "fhid"),
        P("side", "fin", "fhid"),
        P("side", "fhid", "fin"),
    )
    return jax.shard_map(
        on_device, mesh=mesh, in_specs=placed, out_specs=P(("fin", "fhid"), None), check_vma=False
    )
```

```python
import math

import jax
import jax.numpy as jnp
from jax import lax
from jax.experimental import pallas as pl
from jax.experimental.pallas import tpu as pltpu
from jax.sharding import PartitionSpec as P

D = 16384
BF = jnp.bfloat16
F32 = jnp.float32
MESH = pl.DeviceIdType.MESH
ORDER = (2, 1, 3, 0)


def iota(shape, axis):
    return lax.broadcasted_iota(jnp.int32, shape, axis)


def selection(source, rows=256):
    t = iota((rows, 256), 0)
    return (iota((rows, 256), 1) == source(t)).astype(F32).astype(BF)


def arrived(ref, sem):
    pltpu.make_async_copy(ref, ref, sem).wait()


def attend(q, fresh, lens, kv, kv_copies, sco):
    scale = 1.0 / math.sqrt(128)
    for i in range(2):
        kv_copies[i * 2].wait()
        for g in range(8):
            at = (i * 8 + g) * 16
            sco[at : at + 16, :] = lax.dot_general(
                q[at : at + 16, :],
                kv[i, :, g * 128 : (g + 1) * 128],
                (((1,), (1,)), ((), ())),
                preferred_element_type=F32,
            )
    first = iota((256, 1), 0) < 128
    length = jnp.where(first, lens[0], lens[1])
    scores = jnp.where(iota((256, 256), 1) < length, sco[...] * scale, jnp.float32(-1e30))

    def spread(offset):
        rows = [
            jnp.broadcast_to(fresh[i * 16 + offset + g : i * 16 + offset + g + 1, :], (16, 128))
            for i in range(2)
            for g in range(8)
        ]
        return jnp.concatenate(rows, axis=0)

    own = jnp.sum(q[...].astype(F32) * spread(0), axis=1, keepdims=True) * scale
    top = jnp.maximum(jnp.max(scores, axis=1, keepdims=True), own)
    expo = jnp.exp(scores - top)
    own_exp = jnp.exp(own - top)
    total = jnp.sum(expo, axis=1, keepdims=True) + own_exp
    weights = (expo / total).astype(BF)
    own_weight = (own_exp / total).astype(BF).astype(F32)
    parts = []
    for i in range(2):
        kv_copies[i * 2 + 1].wait()
        for g in range(8):
            at = (i * 8 + g) * 16
            parts.append(
                jnp.dot(
                    weights[at : at + 16, :],
                    kv[i, :, 1024 + g * 128 : 1024 + (g + 1) * 128],
                    preferred_element_type=F32,
                )
            )
    return (jnp.concatenate(parts, axis=0) + own_weight * spread(8)).astype(BF)


def kernel(
    q_hbm, fresh_hbm, lens, kv_hbm, res_hbm, gain_hbm, ow_hbm, gw_hbm, uw_hbm, dw_hbm, out,
    wide, wide_f, narrow, narrow_f, q, res_src, gain_in, gain, fin_f,
    kv, sco, m1s, m1, comb, m2s,
    ow, guw, dw, m2, m2all, lhs, rin, resid,
    own, cs, cr, qs, zfar, fs, ffar, yfm, yfp, zs, zin, tot,
    sbuf, gu, ss, xs, xr, hid,
    own2, cs2, cr2, qs2, zfar2, fs2, ffar2, yfm2, yfp2, zs2, zin2, tot2, fo, fb, fin_in,
    in_sem, w_sem, kv_sem, m1_s, m1_r, m2_s, m2_r, rs_s, rs_r, xa_s, xa_r,
    c_s, c_r, y_s, y_r, z_s, z_r, zf_s, zf_r, az_s, ay_s, ac_s, ag_r, ac_r,
    xs_s, xs_r, xh_s, xh_r, c2_s, c2_r, y2_s, y2_r, z2_s, z2_r, zf2_s, zf2_r, f_s, f_r,
):
    side, f, h = lax.axis_index("side"), lax.axis_index("fin"), lax.axis_index("fhid")
    y, z, c = h // 8, (h // 2) % 4, h % 2
    yz = h // 2
    oc = 1 - c
    j = f * 2 + c
    zt = 3 - z
    copies = []

    def at(s, ff, yy, zz, cc):
        return (s, ff, (yy * 4 + zz) * 2 + cc)

    def make(src, dst, s_sem, r_sem, dev):
        return pltpu.make_async_remote_copy(
            src_ref=src, dst_ref=dst, send_sem=s_sem, recv_sem=r_sem,
            device_id=dev, device_id_type=MESH,
        )

    def send(*what):
        cp = make(*what)
        cp.start()
        copies.append(cp)

    maybe = []

    def send_if(cond, *what):
        pl.when(cond)(lambda: make(*what).start())
        maybe.append((cond, what))

    barrier = pltpu.get_barrier_semaphore()

    def greet(dev):
        pl.semaphore_signal(barrier, inc=1, device_id=dev, device_id_type=MESH)

    def deliver():
        for s in range(8):
            arrived(fin_in.at[s], f_r.at[s])
        fin_f[...] = fin_in[...].astype(F32)
        parts = [fin_f[s, :, k, :] for s in range(8) for k in range(16)]
        out[...] = jnp.concatenate(parts, axis=1).astype(BF)

    @pl.when(side == 0)
    def _attention_side():
        kv_copies = []
        for i in range(2):
            for k in range(2):
                part = (i, slice(None), pl.ds(k * 1024, 1024))
                cp = pltpu.make_async_copy(kv_hbm.at[part], kv.at[part], kv_sem.at[i * 2 + k])
                cp.start()
                kv_copies.append(cp)
        first_in = pltpu.make_async_copy(q_hbm, wide, in_sem.at[0])
        second_in = pltpu.make_async_copy(fresh_hbm, narrow, in_sem.at[1])
        first_in.start()
        second_in.start()
        greet(at(0, f, y, z, oc))
        for d in range(8):
            greet(at(1, d // 2, y, zt, d % 2))
        first_in.wait()
        second_in.wait()
        value = wide[...].astype(F32)
        for k in range(128):
            wide_f[:, k, :] = value[:, k * 128 : (k + 1) * 128]
        q[...] = wide_f[...].reshape(256, 128).astype(BF)
        value = narrow[...].astype(F32)
        for k in range(16):
            narrow_f[:, k, :] = value[:, k * 128 : (k + 1) * 128]
        fresh = narrow_f[...].reshape(32, 128)
        mixed = attend(q, fresh, lens, kv, kv_copies, sco)
        sel = selection(
            lambda t: (t // 4) % 2 * 128 + (t // 8) % 16 * 8 + (t // 128 + c) % 2 * 4 + t % 4
        )
        moved_rows = jnp.dot(sel, mixed, preferred_element_type=F32)
        m1s[...] = moved_rows[128:, :].astype(BF)
        comb[:, pl.ds(pl.multiple_of(c * 8, 8), 8), :] = moved_rows[:128, :].reshape(16, 8, 128)
        pl.semaphore_wait(barrier, 17)
        send(m1s, m1, m1_s, m1_r, at(0, f, y, z, oc))
        arrived(m1, m1_r)
        comb[:, pl.ds(pl.multiple_of(oc * 8, 8), 8), :] = m1[...].astype(F32).reshape(16, 8, 128)
        m2s[...] = comb[...].reshape(256, 128).astype(BF)
        for b in range(16):
            send(
                m2s.at[pl.ds(b * 16, 16)],
                m2.at[pl.ds(pl.multiple_of(yz * 16, 16), 16)],
                m2_s.at[b],
                m2_r.at[yz],
                at(1, f, b // 4, b % 4, c),
            )
        for cp in copies:
            cp.wait_send()
        deliver()

    @pl.when(side == 1)
    def _mlp_side():
        copies.clear()
        up, down, far = (y + 1) % 4, (y + 3) % 4, (y + 2) % 4
        dev_up, dev_down, dev_far = (at(1, f, yy, z, c) for yy in (up, down, far))
        dev_core = at(1, f, y, z, oc)
        first_in = pltpu.make_async_copy(res_hbm, wide, in_sem.at[0])
        second_in = pltpu.make_async_copy(gain_hbm, gain_in, in_sem.at[1])
        first_in.start()
        second_in.start()
        for d in range(16):
            greet(at(0, f, d // 4, d % 4, c))
        for d in range(1, 4):
            greet(at(1, (f + d) % 4, y, z, c))
            greet(at(1, f, y, (z + d) % 4, c))
        greet(dev_up)
        greet(dev_down)
        greet(dev_far)
        greet(dev_core)
        for d in range(8):
            greet(at(1, d // 2, y, zt, d % 2))
        weights = [
            pltpu.make_async_copy(a, b, w_sem.at[k])
            for k, (a, b) in enumerate(
                (
                    (ow_hbm, ow.at[pl.ds(0, 512)]),
                    (gw_hbm, guw.at[:, pl.ds(0, 256)]),
                    (uw_hbm, guw.at[:, pl.ds(256, 256)]),
                    (dw_hbm, dw),
                )
            )
        ]
        for cp in weights:
            cp.start()
        gu[...] = jnp.zeros_like(gu)
        ss[...] = jnp.zeros_like(ss)
        first_in.wait()
        second_in.wait()
        value = wide[...].astype(F32)
        for k in range(128):
            wide_f[:, k, :] = value[:, k * 128 : (k + 1) * 128]
        for k in range(4):
            rows = wide_f[:, k * 32 : (k + 1) * 32, :]
            res_src[k] = rows.reshape(64, 128).astype(BF)
        gain[...] = gain_in[...].astype(F32).reshape(32, 128)
        pl.semaphore_wait(barrier, 26)

        for d in range(1, 4):
            ff = (f + d) % 4
            send(res_src.at[ff], rin.at[f], rs_s.at[d], rs_r.at[f], at(1, ff, y, z, c))
        rin[f] = res_src[f]
        for d in range(1, 4):
            ff = (f + d) % 4
            arrived(rin.at[ff], rs_r.at[ff])
        sel = selection(
            lambda t: (t // 2) % 4 * 64 + ((t % 2) * 16 + (t // 8) % 16) * 2 + t // 128
        )
        resid[...] = jnp.dot(sel, rin[...].reshape(256, 128), preferred_element_type=F32)
        eight = [
            resid[half * 128 + n * 8 : half * 128 + n * 8 + 8, :] for n in range(16) for half in range(2)
        ]
        eight = jnp.concatenate(eight, axis=1)
        ow[512:528, :] = jnp.concatenate([eight, jnp.zeros_like(eight)], axis=0).astype(BF)
        ow[528:, :] = jnp.zeros((112, 4096), BF)
        t = iota((256, 128), 0)
        row_yz = ((t // 128 + c) % 2 * 64 + t % 64) // 8
        here = (row_yz == yz) & (t // 64 % 2 == c) & (t % 8 == iota((256, 128), 1))
        lhs[:, 512:] = here.astype(F32).astype(BF)

        pick = selection(
            lambda t: ((t // 128 + c) % 2 * 8 + (t // 8) % 8) * 16
            + (t // 64) % 2 * 8
            + t % 2 * 4
            + t // 256,
            1024,
        )
        row_fin = (iota((1024, 128), 0) // 2) % 4
        for e in (0, 1, 3, 2):
            yy = (y + e) % 4
            for k in range(4):
                n = yy * 4 + k
                arrived(m2.at[pl.ds(pl.multiple_of(n * 16, 16), 16)], m2_r.at[n])
            part = pl.ds(pl.multiple_of(yy * 64, 64), 64)
            for d in (2, 1, 3):
                ff = (f + d) % 4
                send(
                    m2.at[part], m2all.at[f, part], xa_s.at[d, e], xa_r.at[f, yy],
                    at(1, ff, y, z, c),
                )
        picked = jnp.where(
            row_fin == f, jnp.dot(pick, m2[...], preferred_element_type=F32), 0.0
        )
        for d in (1, 3, 2):
            ff = (f + d) % 4
            for k in range(4):
                arrived(m2all.at[ff, pl.ds(k * 64, 64)], xa_r.at[ff, k])
            picked = jnp.where(
                row_fin == ff, jnp.dot(pick, m2all[ff], preferred_element_type=F32), picked
            )
        for k in range(4):
            lhs[:, k * 128 : (k + 1) * 128] = picked[k * 256 : (k + 1) * 256, :].astype(BF)
        weights[0].wait()

        def project(g):
            yy = (y + ORDER[g]) % 4

            w = ow[:, pl.ds(pl.multiple_of(yy * 1024, 1024), 1024)]
            value = jnp.dot(lhs[...], w, preferred_element_type=F32)
            for p in range(2):
                for k in range(4):
                    cols = slice(k * 256, (k + 1) * 256)
                    cs[p, yy * 4 + k] = value[128 + p * 64 : 192 + p * 64, cols].astype(BF)
                    own[p, yy * 4 + k] = value[p * 64 : p * 64 + 64, cols]
            part = pl.ds(yy * 4, 4)
            for p in range(2):
                send(cs.at[p, part], cr.at[p, part], c_s.at[p, g], c_r.at[p, g], dev_core)

        def paired(p, n):
            return own[p, n] + cr[p, n].astype(F32)

        def beside(p, g):
            yy = (y + ORDER[g]) % 4
            arrived(cr.at[p, pl.ds(yy * 4, 4)], c_r.at[p, g])
            to, dev = ((yfm, dev_up), (yfp, dev_down))[g - 1]
            for d in (2, 1, 3, 0):
                k = (z + d) % 4
                qs[p, yy, k] = paired(p, yy * 4 + k).astype(BF)
                send(
                    qs.at[p, yy, k], to.at[p, k],
                    y_s.at[p, (g - 1) * 4 + d], y_r.at[p, (g - 1) * 4 + k], dev,
                )

        def opposite(p):
            arrived(cr.at[p, pl.ds(far * 4, 4)], c_r.at[p, 0])
            for d in (2, 1, 3):
                zz = (z + d) % 4
                qs[p, far, zz] = paired(p, far * 4 + zz).astype(BF)
                send(
                    qs.at[p, far, zz], zfar.at[p, z], zf_s.at[p, d], zf_r.at[p, z],
                    at(1, f, y, zz, c),
                )

        def onward(p):
            value = paired(p, far * 4 + z)
            for d in (1, 3, 2):
                zz = (z + d) % 4
                arrived(zfar.at[p, zz], zf_r.at[p, zz])
                value = value + zfar[p, zz].astype(F32)
            fs[p] = value.astype(BF)
            send(fs.at[p], ffar.at[p], y_s.at[p, 8], y_r.at[p, 8], dev_far)

        def over_z(p):
            part = pl.ds(y * 4, 4)
            arrived(cr.at[p, part], c_r.at[p, 3])

            def summed(k):
                arrived(yfm.at[p, k], y_r.at[p, k])
                arrived(yfp.at[p, k], y_r.at[p, 4 + k])
                return paired(p, y * 4 + k) + yfm[p, k].astype(F32) + yfp[p, k].astype(F32)

            for d in (2, 1, 3):
                zz = (z + d) % 4
                zs[p, zz] = summed(zz).astype(BF)
                send(zs.at[p, zz], zin.at[p, z], z_s.at[p, d], z_r.at[p, z], at(1, f, y, zz, c))
            tot[p] = summed(z)

        def give(p, n, slot, dev):
            ref = sbuf.at[p, n, c]
            send(ref, ref, ay_s.at[p, slot], ag_r.at[p, n], dev)

        def give_y(p, n, k):
            give(p, n, 2 * k, dev_up)
            give(p, n, 2 * k + 1, dev_down)

        def give_core(p, n):
            ref = sbuf.at[p, n, c]
            send(ref, ref, ac_s.at[p, n], ac_r.at[p, n], dev_core)

        def use(p, yy):
            parts = []
            for k in range(4):
                n = yy * 4 + k
                arrived(sbuf.at[p, n, oc], ac_r.at[p, n])
                x = sbuf[p, n].reshape(128, 256).astype(F32)
                sq = x * x
                ss[p] += sq[:, :128] + sq[:, 128:]
                pair = [gain[pl.ds(n * 2 + m, 1), :] for m in range(2)]
                parts.append((x * jnp.concatenate(pair, axis=1)).astype(BF))
            w = guw[pl.ds(pl.multiple_of(yy * 1024, 1024), 1024), :]
            gu[p] += jnp.dot(jnp.concatenate(parts, axis=1), w, preferred_element_type=F32)

        def near(p):
            total = tot[p]
            for d in (1, 3, 2):
                zz = (z + d) % 4
                arrived(zin.at[p, zz], z_r.at[p, zz])
                total = total + zin[p, zz].astype(F32)
            arrived(ffar.at[p], y_r.at[p, 8])
            total = total + ffar[p].astype(F32)
            sbuf[p, yz, c] = total.astype(BF)
            for d in (2, 1, 3):
                zz = (z + d) % 4
                ref = sbuf.at[p, yz, c]
                send(ref, ref, az_s.at[p, d], ag_r.at[p, yz], at(1, f, y, zz, c))
            give_y(p, yz, 0)
            give(p, yz, 8, dev_far)
            give_core(p, yz)

        def forward(p):
            for d in range(1, 4):
                n = y * 4 + (z + d) % 4
                arrived(sbuf.at[p, n, c], ag_r.at[p, n])
                give_y(p, n, d)
                if d != 2:
                    ref = sbuf.at[p, n, c]
                    last = z == (3 if d == 1 else 0)
                    send_if(last, ref, ref, ay_s.at[p, 8 + d], ag_r.at[p, n], dev_far)
                give_core(p, n)

        def spread_opposite(p):
            n = far * 4 + z
            arrived(sbuf.at[p, n, c], ag_r.at[p, n])
            ref = sbuf.at[p, n, c]
            for d in (2, 1, 3):
                what = (ref, ref, az_s.at[p, 4 + d], ag_r.at[p, n], at(1, f, y, (z + d) % 4, c))
                if d == 2:
                    send(*what)
                else:
                    send_if(z != (3 if d == 1 else 0), *what)
            give_core(p, n)

        def taken(p, group, d):
            n = group * 4 + (z + d) % 4
            arrived(sbuf.at[p, n, c], ag_r.at[p, n])
            give_core(p, n)

        def over_fin(p):
            tt = jnp.sum(ss[p], axis=1, keepdims=True)
            top = tt.astype(BF).astype(F32)
            low = iota((128, 128), 1) < 64
            xs[p, :, :, 512:] = jnp.where(low, top, tt - top).astype(BF).reshape(4, 32, 128)
            xs[p, :, :, :512] = gu[p].astype(BF).reshape(4, 32, 512)
            for d in (2, 1, 3):
                ff = (f + d) % 4
                send(xs.at[p, ff], xr.at[p, f], xs_s.at[p, d], xs_r.at[p, f], at(1, ff, y, z, c))

        def hide(p):
            mine = pl.ds(pl.multiple_of(f * 32, 32), 32)
            both = gu[p, mine, :]
            square = xs[p, f][:, 512:].astype(F32)
            for d in (1, 3, 2):
                ff = (f + d) % 4
                arrived(xr.at[p, ff], xs_r.at[p, ff])
                both = both + xr[p, ff][:, :512].astype(F32)
                square = square + xr[p, ff][:, 512:].astype(F32)
            scale = lax.rsqrt((square[:, 0:1] + square[:, 64:65]) / D + 1e-05)
            gate = both[:, :256] * scale
            hid[p, mine, :] = (gate / (1.0 + jnp.exp(-gate)) * (both[:, 256:] * scale)).astype(BF)
            for d in (2, 1, 3):
                ff = (f + d) % 4
                ref = hid.at[p, mine]
                send(ref, ref, xh_s.at[p, d], xh_r.at[p, f], at(1, ff, y, z, c))

        def lower(p):
            for d in (1, 3, 2):
                ff = (f + d) % 4
                ref = hid.at[p, pl.ds(pl.multiple_of(ff * 32, 32), 32)]
                arrived(ref, xh_r.at[p, ff])

            def columns(core):
                parts = []
                for half in range(2):
                    start = core * 2048 + half * 1024
                    w = dw[:, pl.ds(pl.multiple_of(start, 1024), 1024)]
                    value = jnp.dot(hid[p], w, preferred_element_type=F32)
                    parts.append(value.reshape(16, 8, 1024))
                return jnp.concatenate(parts, axis=1)

            cs2[p] = columns(oc).astype(BF)
            for g in range(4):
                part = pl.ds((y + ORDER[g]) % 4 * 4, 4)
                send(cs2.at[p, part], cr2.at[p, part], c2_s.at[p, g], c2_r.at[p, g], dev_core)
            own2[p] = columns(c)

        def paired2(p, n):
            return own2[p, n] + cr2[p, n].astype(F32)

        def beside2(p, g):
            yy = (y + ORDER[g]) % 4
            arrived(cr2.at[p, pl.ds(yy * 4, 4)], c2_r.at[p, g])
            to, dev = ((yfm2, dev_up), (yfp2, dev_down))[g - 1]
            for d in (2, 1, 3, 0):
                k = 3 - (z + d) % 4
                qs2[p, yy, k] = paired2(p, yy * 4 + k).astype(BF)
                send(
                    qs2.at[p, yy, k], to.at[p, k],
                    y2_s.at[p, (g - 1) * 4 + d], y2_r.at[p, (g - 1) * 4 + k], dev,
                )

        def opposite2(p):
            arrived(cr2.at[p, pl.ds(far * 4, 4)], c2_r.at[p, 0])
            for d in (2, 1, 3):
                zz = (z + d) % 4
                qs2[p, far, zz] = paired2(p, far * 4 + (3 - zz)).astype(BF)
                send(
                    qs2.at[p, far, zz], zfar2.at[p, z], zf2_s.at[p, d], zf2_r.at[p, z],
                    at(1, f, y, zz, c),
                )

        def onward2(p):
            value = paired2(p, far * 4 + zt)
            for d in (1, 3, 2):
                zz = (z + d) % 4
                arrived(zfar2.at[p, zz], zf2_r.at[p, zz])
                value = value + zfar2[p, zz].astype(F32)
            fs2[p] = value.astype(BF)
            send(fs2.at[p], ffar2.at[p], y2_s.at[p, 8], y2_r.at[p, 8], dev_far)

        def over_z2(p):
            part = pl.ds(y * 4, 4)
            arrived(cr2.at[p, part], c2_r.at[p, 3])

            def summed(k):
                arrived(yfm2.at[p, k], y2_r.at[p, k])
                arrived(yfp2.at[p, k], y2_r.at[p, 4 + k])
                return paired2(p, y * 4 + k) + yfm2[p, k].astype(F32) + yfp2[p, k].astype(F32)

            for d in (2, 1, 3):
                zz = (z + d) % 4
                zs2[p, zz] = summed(3 - zz).astype(BF)
                send(
                    zs2.at[p, zz], zin2.at[p, z], z2_s.at[p, d], z2_r.at[p, z], at(1, f, y, zz, c)
                )
            slab = pl.ds(pl.multiple_of(((y * 4 + zt) % 8) // 2 * 16, 16), 16)
            halves = []
            for half in range(2):
                kept = [
                    sbuf[p, c * 8 + half * 4 + m, y // 2, slab, :].astype(F32) for m in range(4)
                ]
                kept = jnp.concatenate(kept, axis=1)
                halves.append(jnp.where(zt % 2 == 0, kept[:8], kept[8:]))
            tot2[p] = summed(zt) + jnp.concatenate(halves, axis=0)

        def finish(p):
            total = tot2[p]
            for d in (1, 3, 2):
                zz = (z + d) % 4
                arrived(zin2.at[p, zz], z2_r.at[p, zz])
                total = total + zin2[p, zz].astype(F32)
            arrived(ffar2.at[p], y2_r.at[p, 8])
            total = total + ffar2[p].astype(F32)
            for k in range(16):
                rows = slice(k // 8 * 8, k // 8 * 8 + 8)
                fo[:, k, :] = total[rows, k % 8 * 128 : (k % 8 + 1) * 128]
            fb[p] = fo[...].astype(BF)
            for d in range(8):
                ff = (f + d // 2) % 4
                send(
                    fb.at[p, pl.ds(ff * 2, 2)], fin_in.at[j], f_s.at[p, d], f_r.at[j],
                    at(d % 2, ff, y, zt, p),
                )

        project(0)
        project(1)
        opposite(0)
        opposite(1)
        beside(0, 1)
        project(2)
        beside(1, 1)
        beside(0, 2)
        project(3)
        beside(1, 2)
        onward(0)
        over_z(0)
        onward(1)
        over_z(1)
        near(0)
        near(1)
        weights[1].wait()
        weights[2].wait()
        forward(0)
        forward(1)
        for p in range(2):
            spread_opposite(p)
            taken(p, up, 0)
            taken(p, down, 0)
        use(0, y)
        use(1, y)
        for d in range(1, 4):
            taken(0, up, d)
            taken(0, down, d)
        for d in range(1, 4):
            taken(0, far, d)
        use(0, up)
        use(0, down)
        for d in range(1, 4):
            taken(1, up, d)
            taken(1, down, d)
        use(0, far)
        over_fin(0)
        for d in range(1, 4):
            taken(1, far, d)
        use(1, up)
        use(1, down)
        use(1, far)
        over_fin(1)
        hide(0)
        hide(1)
        weights[3].wait()
        lower(0)
        opposite2(0)
        beside2(0, 1)
        beside2(0, 2)
        lower(1)
        opposite2(1)
        beside2(1, 1)
        beside2(1, 2)
        onward2(0)
        over_z2(0)
        onward2(1)
        over_z2(1)
        finish(0)
        finish(1)
        deliver()
        for cp in copies:
            cp.wait_send()
        for cond, what in maybe:
            pl.when(cond)(lambda what=what: make(*what).wait_send())


def moved(*args):
    def v(*shape, dtype=BF):
        return pltpu.VMEM(shape, dtype)

    scratch = [
        v(2, D), v(2, 128, 128, dtype=F32), v(2, 2048), v(2, 16, 128, dtype=F32), v(256, 128),
        v(4, 64, 128), v(4096), v(32, 128, dtype=F32), v(8, 2, 16, 128, dtype=F32),
        v(2, 256, 2048), v(256, 256, dtype=F32), v(128, 128), v(128, 128),
        v(16, 16, 128, dtype=F32), v(256, 128),
        v(640, 4096), v(4096, 512), v(256, 4096),
        v(256, 128), v(4, 256, 128), v(256, 640),
        v(4, 64, 128), v(256, 128, dtype=F32),
        v(2, 16, 64, 256, dtype=F32), v(2, 16, 64, 256), v(2, 16, 64, 256), v(2, 4, 4, 64, 256),
        v(2, 4, 64, 256), v(2, 64, 256), v(2, 64, 256), v(2, 4, 64, 256), v(2, 4, 64, 256),
        v(2, 4, 64, 256), v(2, 4, 64, 256), v(2, 64, 256, dtype=F32),
        v(2, 16, 2, 64, 256), v(2, 128, 512, dtype=F32), v(2, 128, 128, dtype=F32),
        v(2, 4, 32, 640), v(2, 4, 32, 640), v(2, 128, 256),
        v(2, 16, 16, 1024, dtype=F32), v(2, 16, 16, 1024), v(2, 16, 16, 1024),
        v(2, 4, 4, 16, 1024), v(2, 4, 16, 1024), v(2, 16, 1024), v(2, 16, 1024),
        v(2, 4, 16, 1024), v(2, 4, 16, 1024), v(2, 4, 16, 1024), v(2, 4, 16, 1024),
        v(2, 16, 1024, dtype=F32), v(8, 16, 128, dtype=F32), v(2, 8, 16, 128), v(8, 2, 16, 128),
    ]
    counts = [
        (2,), (4,), (4,), (), (), (16,), (16,), (4,), (4,), (4, 4), (4, 4),
        (2, 4), (2, 4), (2, 9), (2, 9), (2, 4), (2, 4), (2, 4), (2, 4),
        (2, 8), (2, 12), (2, 16), (2, 16), (2, 16),
        (2, 4), (2, 4), (2, 4), (2, 4), (2, 4), (2, 4), (2, 9), (2, 9), (2, 4), (2, 4),
        (2, 4), (2, 4), (2, 8), (8,),
    ]
    scratch += [pltpu.SemaphoreType.DMA(k) for k in counts]
    vm, hbm = pl.BlockSpec(memory_space=pltpu.VMEM), pl.BlockSpec(memory_space=pl.ANY)
    sm = pl.BlockSpec(memory_space=pltpu.SMEM)
    return pl.pallas_call(
        kernel,
        out_shape=jax.ShapeDtypeStruct((2, D), BF),
        in_specs=[hbm, hbm, sm, hbm, hbm, hbm, hbm, hbm, hbm, hbm],
        out_specs=vm,
        scratch_shapes=scratch,
        compiler_params=pltpu.CompilerParams(
            collective_id=0, has_side_effects=True, vmem_limit_bytes=56 * 1024 * 1024
        ),
    )(*args)


def on_device(
    queries, new_entries, cached_entries, lengths, residual, norm_gain,
    out_weight, gate_weight, up_weight, down_weight,
):
    return moved(
        queries, new_entries, lengths, cached_entries[0], residual, norm_gain,
        out_weight[0], gate_weight[0], up_weight[0], down_weight[0],
    )


def solution(mesh):
    placed = (
        P(("fin", "fhid"), None),
        P(("fin", "fhid"), None),
        P("side", ("fin", "fhid"), None, None),
        P(("fin", "fhid")),
        P(("fin", "fhid"), None),
        P("fin"),
        P("side", "fhid", "fin"),
        P("side", "fin", "fhid"),
        P("side", "fin", "fhid"),
        P("side", "fhid", "fin"),
    )
    return jax.shard_map(
        on_device, mesh=mesh, in_specs=placed, out_specs=P(("fin", "fhid"), None), check_vma=False
    )
```

```python
import math

import jax
import jax.numpy as jnp
from jax import lax
from jax.experimental import pallas as pl
from jax.experimental.pallas import tpu as pltpu
from jax.sharding import PartitionSpec as P

D = 16384
BF = jnp.bfloat16
F32 = jnp.float32
MESH = pl.DeviceIdType.MESH
ORDER = (2, 1, 3, 0)


def iota(shape, axis):
    return lax.broadcasted_iota(jnp.int32, shape, axis)


def selection(source, rows=256):
    t = iota((rows, 256), 0)
    return (iota((rows, 256), 1) == source(t)).astype(F32).astype(BF)


def arrived(ref, sem):
    pltpu.make_async_copy(ref, ref, sem).wait()


def attend(q, fresh, lens, kv, kv_copies, sco):
    scale = 1.0 / math.sqrt(128)
    for i in range(2):
        kv_copies[i * 2].wait()
        for g in range(8):
            at = (i * 8 + g) * 16
            sco[at : at + 16, :] = lax.dot_general(
                q[at : at + 16, :],
                kv[i, :, g * 128 : (g + 1) * 128],
                (((1,), (1,)), ((), ())),
                preferred_element_type=F32,
            )
    first = iota((256, 1), 0) < 128
    length = jnp.where(first, lens[0], lens[1])
    scores = jnp.where(iota((256, 256), 1) < length, sco[...] * scale, jnp.float32(-1e30))

    def spread(offset):
        rows = [
            jnp.broadcast_to(fresh[i * 16 + offset + g : i * 16 + offset + g + 1, :], (16, 128))
            for i in range(2)
            for g in range(8)
        ]
        return jnp.concatenate(rows, axis=0)

    own = jnp.sum(q[...].astype(F32) * spread(0), axis=1, keepdims=True) * scale
    top = jnp.maximum(jnp.max(scores, axis=1, keepdims=True), own)
    expo = jnp.exp(scores - top)
    own_exp = jnp.exp(own - top)
    total = jnp.sum(expo, axis=1, keepdims=True) + own_exp
    weights = (expo / total).astype(BF)
    own_weight = (own_exp / total).astype(BF).astype(F32)
    parts = []
    for i in range(2):
        kv_copies[i * 2 + 1].wait()
        for g in range(8):
            at = (i * 8 + g) * 16
            parts.append(
                jnp.dot(
                    weights[at : at + 16, :],
                    kv[i, :, 1024 + g * 128 : 1024 + (g + 1) * 128],
                    preferred_element_type=F32,
                )
            )
    return (jnp.concatenate(parts, axis=0) + own_weight * spread(8)).astype(BF)


def kernel(
    q_hbm, fresh_hbm, lens, kv_hbm, res_hbm, gain_hbm, ow_hbm, gw_hbm, uw_hbm, dw_hbm, out,
    wide, wide_f, narrow, narrow_f, q, res_src, gain_in, gain, fin_f,
    kv, sco, m2s,
    ow, guw, dw, m2, comb, m2o, m2all, lhs, rin, resid,
    own, cs, cr, qs, zfar, fs, ffar, yfm, yfp, zs, zin, tot,
    sbuf, gu, ss, xs, xr, hid,
    own2, cs2, cr2, qs2, zfar2, fs2, ffar2, yfm2, yfp2, zs2, zin2, tot2, fo, fb, fin_in,
    in_sem, w_sem, kv_sem, m2_s, m2_r, rs_s, rs_r, xa_s, xa_r,
    c_s, c_r, y_s, y_r, z_s, z_r, zf_s, zf_r, az_s, ay_s, ac_s, ag_r, ac_r,
    xs_s, xs_r, xh_s, xh_r, c2_s, c2_r, y2_s, y2_r, z2_s, z2_r, zf2_s, zf2_r, f_s, f_r,
):
    side, f, h = lax.axis_index("side"), lax.axis_index("fin"), lax.axis_index("fhid")
    y, z, c = h // 8, (h // 2) % 4, h % 2
    yz = h // 2
    oc = 1 - c
    j = f * 2 + c
    zt = 3 - z
    along_z = (z, z + 1 - 2 * (z % 2), (z + 2) % 4, 3 - z)
    at_end = z % 3 == 0
    copies = []

    def at(s, ff, yy, zz, cc):
        return (s, ff, (yy * 4 + zz) * 2 + cc)

    def make(src, dst, s_sem, r_sem, dev):
        return pltpu.make_async_remote_copy(
            src_ref=src, dst_ref=dst, send_sem=s_sem, recv_sem=r_sem,
            device_id=dev, device_id_type=MESH,
        )

    def send(*what):
        cp = make(*what)
        cp.start()
        copies.append(cp)

    maybe = []

    def send_if(cond, *what):
        pl.when(cond)(lambda: make(*what).start())
        maybe.append((cond, what))

    barrier = pltpu.get_barrier_semaphore()

    def greet(dev):
        pl.semaphore_signal(barrier, inc=1, device_id=dev, device_id_type=MESH)

    def deliver():
        for s in range(8):
            arrived(fin_in.at[s], f_r.at[s])
            fin_f[s] = fin_in[s].astype(F32)
            parts = [fin_f[s, :, k, :] for k in range(16)]
            out[:, s * 2048 : (s + 1) * 2048] = jnp.concatenate(parts, axis=1).astype(BF)

    @pl.when(side == 0)
    def _attention_side():
        kv_copies = []
        for i in range(2):
            for k in range(2):
                part = (i, slice(None), pl.ds(k * 1024, 1024))
                cp = pltpu.make_async_copy(kv_hbm.at[part], kv.at[part], kv_sem.at[i * 2 + k])
                cp.start()
                kv_copies.append(cp)
        first_in = pltpu.make_async_copy(q_hbm, wide, in_sem.at[0])
        second_in = pltpu.make_async_copy(fresh_hbm, narrow, in_sem.at[1])
        first_in.start()
        second_in.start()
        for d in range(8):
            greet(at(1, d // 2, y, zt, d % 2))
        first_in.wait()
        second_in.wait()
        value = wide[...].astype(F32)
        for k in range(128):
            wide_f[:, k, :] = value[:, k * 128 : (k + 1) * 128]
        q[...] = wide_f[...].reshape(256, 128).astype(BF)
        value = narrow[...].astype(F32)
        for k in range(16):
            narrow_f[:, k, :] = value[:, k * 128 : (k + 1) * 128]
        fresh = narrow_f[...].reshape(32, 128)
        mixed = attend(q, fresh, lens, kv, kv_copies, sco)
        sel = selection(
            lambda t: (t // 4) % 2 * 128 + t // 16 * 8 + (t // 8) % 2 * 4 + t % 4
        )
        m2s[...] = jnp.dot(sel, mixed, preferred_element_type=F32).astype(BF)
        pl.semaphore_wait(barrier, 16)
        for b in range(16):
            send(
                m2s.at[pl.ds(b * 16, 16)],
                m2.at[pl.ds(pl.multiple_of(yz * 16, 16), 16)],
                m2_s.at[b],
                m2_r.at[yz],
                at(1, f, b // 4, b % 4, c),
            )
        for cp in copies:
            cp.wait_send()
        deliver()

    @pl.when(side == 1)
    def _mlp_side():
        copies.clear()
        up, down, far = (y + 1) % 4, (y + 3) % 4, (y + 2) % 4
        dev_up, dev_down, dev_far = (at(1, f, yy, z, c) for yy in (up, down, far))
        dev_core = at(1, f, y, z, oc)
        first_in = pltpu.make_async_copy(res_hbm, wide, in_sem.at[0])
        second_in = pltpu.make_async_copy(gain_hbm, gain_in, in_sem.at[1])
        first_in.start()
        second_in.start()
        for d in range(16):
            greet(at(0, f, d // 4, d % 4, c))
        for d in range(1, 4):
            greet(at(1, (f + d) % 4, y, z, c))
            greet(at(1, (f + d) % 4, y, z, oc))
            greet(at(1, f, y, along_z[d], c))
        greet(dev_up)
        greet(dev_down)
        greet(dev_far)
        greet(dev_core)
        for d in range(8):
            greet(at(1, d // 2, y, zt, d % 2))
        weights = [
            pltpu.make_async_copy(a, b, w_sem.at[k])
            for k, (a, b) in enumerate(
                (
                    (ow_hbm, ow.at[pl.ds(0, 512)]),
                    (gw_hbm, guw.at[:, pl.ds(0, 256)]),
                    (uw_hbm, guw.at[:, pl.ds(256, 256)]),
                    (dw_hbm, dw),
                )
            )
        ]
        for cp in weights:
            cp.start()
        gu[...] = jnp.zeros_like(gu)
        ss[...] = jnp.zeros_like(ss)
        first_in.wait()
        second_in.wait()
        value = wide[...].astype(F32)
        for k in range(128):
            wide_f[:, k, :] = value[:, k * 128 : (k + 1) * 128]
        for k in range(4):
            rows = wide_f[:, k * 32 : (k + 1) * 32, :]
            res_src[k] = rows.reshape(64, 128).astype(BF)
        gain[...] = gain_in[...].astype(F32).reshape(32, 128)
        pl.semaphore_wait(barrier, 29)

        for d in range(1, 4):
            ff = (f + d) % 4
            send(res_src.at[ff], rin.at[f], rs_s.at[d], rs_r.at[f], at(1, ff, y, z, c))
        rin[f] = res_src[f]
        for d in range(1, 4):
            ff = (f + d) % 4
            arrived(rin.at[ff], rs_r.at[ff])
        sel = selection(
            lambda t: (t // 2) % 4 * 64 + ((t % 2) * 16 + (t // 8) % 16) * 2 + t // 128
        )
        resid[...] = jnp.dot(sel, rin[...].reshape(256, 128), preferred_element_type=F32)
        eight = [
            resid[half * 128 + n * 8 : half * 128 + n * 8 + 8, :] for n in range(16) for half in range(2)
        ]
        eight = jnp.concatenate(eight, axis=1)
        ow[512:528, :] = jnp.concatenate([eight, jnp.zeros_like(eight)], axis=0).astype(BF)
        ow[528:, :] = jnp.zeros((112, 4096), BF)
        t = iota((256, 128), 0)
        row_yz = ((t // 128 + c) % 2 * 64 + t % 64) // 8
        here = (row_yz == yz) & (t // 64 % 2 == c) & (t % 8 == iota((256, 128), 1))
        lhs[:, 512:] = here.astype(F32).astype(BF)

        pick = selection(
            lambda t: (t // 64) % 2 * 128
            + ((t // 128 + c) % 2 * 8 + (t // 8) % 8) * 8
            + t % 2 * 4
            + t // 256,
            1024,
        )
        row_fin = (iota((1024, 128), 0) // 2) % 4
        for e in (0, 1, 3, 2):
            yy = (y + e) % 4
            for k in range(4):
                n = yy * 4 + k
                arrived(m2.at[pl.ds(pl.multiple_of(n * 16, 16), 16)], m2_r.at[n])
            rows = pl.ds(pl.multiple_of(yy * 64, 64), 64)
            part = pl.ds(pl.multiple_of(yy * 32, 32), 32)
            comb[...] = m2[rows, :].astype(F32).reshape(4, 16, 128)
            other = comb[:, pl.ds(pl.multiple_of(oc * 8, 8), 8), :]
            m2o[part, :] = other.reshape(32, 128).astype(BF)
            mine = comb[:, pl.ds(pl.multiple_of(c * 8, 8), 8), :]
            m2all[f, c, part, :] = mine.reshape(32, 128).astype(BF)
            for d in (2, 1, 3):
                ff = (f + d) % 4
                to = m2all.at[f, c, part]
                send(to, to, xa_s.at[d, e], xa_r.at[j, yy], at(1, ff, y, z, c))
                send(m2o.at[part], to, xa_s.at[4 + d, e], xa_r.at[j, yy], at(1, ff, y, z, oc))
            send(m2o.at[part], m2all.at[f, c, part], xa_s.at[0, e], xa_r.at[j, yy], dev_core)

        def quarter(ff, cc):
            for k in range(4):
                arrived(m2all.at[ff, cc, pl.ds(k * 32, 32)], xa_r.at[ff * 2 + cc, k])

        quarter(f, oc)
        picked = jnp.where(
            row_fin == f, jnp.dot(pick, m2all[f].reshape(256, 128), preferred_element_type=F32), 0.0
        )
        for d in (1, 3, 2):
            ff = (f + d) % 4
            quarter(ff, c)
            quarter(ff, oc)
            picked = jnp.where(
                row_fin == ff,
                jnp.dot(pick, m2all[ff].reshape(256, 128), preferred_element_type=F32),
                picked,
            )
        for k in range(4):
            lhs[:, k * 128 : (k + 1) * 128] = picked[k * 256 : (k + 1) * 256, :].astype(BF)
        weights[0].wait()

        def project(g):
            yy = (y + ORDER[g]) % 4

            w = ow[:, pl.ds(pl.multiple_of(yy * 1024, 1024), 1024)]
            value = jnp.dot(lhs[...], w, preferred_element_type=F32)
            for p in range(2):
                for k in range(4):
                    cols = slice(k * 256, (k + 1) * 256)
                    cs[p, yy * 4 + k] = value[128 + p * 64 : 192 + p * 64, cols].astype(BF)
                    own[p, yy * 4 + k] = value[p * 64 : p * 64 + 64, cols]
            part = pl.ds(yy * 4, 4)
            for p in range(2):
                send(cs.at[p, part], cr.at[p, part], c_s.at[p, g], c_r.at[p, g], dev_core)

        def paired(p, n):
            return own[p, n] + cr[p, n].astype(F32)

        def beside(p, g):
            yy = (y + ORDER[g]) % 4
            arrived(cr.at[p, pl.ds(yy * 4, 4)], c_r.at[p, g])
            to, dev = ((yfm, dev_up), (yfp, dev_down))[g - 1]
            for d in (3, 2, 1, 0):
                k = along_z[d]
                qs[p, yy, k] = paired(p, yy * 4 + k).astype(BF)
                send(
                    qs.at[p, yy, k], to.at[p, k],
                    y_s.at[p, (g - 1) * 4 + d], y_r.at[p, (g - 1) * 4 + k], dev,
                )

        def opposite(p):
            arrived(cr.at[p, pl.ds(far * 4, 4)], c_r.at[p, 0])
            for d in (3, 2, 1):
                zz = along_z[d]
                qs[p, far, zz] = paired(p, far * 4 + zz).astype(BF)
                send(
                    qs.at[p, far, zz], zfar.at[p, z], zf_s.at[p, d], zf_r.at[p, z],
                    at(1, f, y, zz, c),
                )

        def onward(p):
            value = paired(p, far * 4 + z)
            for d in (3, 2, 1):
                zz = along_z[d]
                arrived(zfar.at[p, zz], zf_r.at[p, zz])
                value = value + zfar[p, zz].astype(F32)
            fs[p] = value.astype(BF)
            send(fs.at[p], ffar.at[p], y_s.at[p, 8], y_r.at[p, 8], dev_far)

        def over_z(p):
            part = pl.ds(y * 4, 4)
            arrived(cr.at[p, part], c_r.at[p, 3])

            def summed(k):
                arrived(yfm.at[p, k], y_r.at[p, k])
                arrived(yfp.at[p, k], y_r.at[p, 4 + k])
                return paired(p, y * 4 + k) + yfm[p, k].astype(F32) + yfp[p, k].astype(F32)

            for d in (3, 2, 1):
                zz = along_z[d]
                zs[p, zz] = summed(zz).astype(BF)
                send(zs.at[p, zz], zin.at[p, z], z_s.at[p, d], z_r.at[p, z], at(1, f, y, zz, c))
            tot[p] = summed(z)

        def give(p, n, slot, dev):
            ref = sbuf.at[p, n, c]
            send(ref, ref, ay_s.at[p, slot], ag_r.at[p, n], dev)

        def give_y(p, n, k):
            give(p, n, 2 * k, dev_up)
            give(p, n, 2 * k + 1, dev_down)

        def give_core(p, n):
            ref = sbuf.at[p, n, c]
            send(ref, ref, ac_s.at[p, n], ac_r.at[p, n], dev_core)

        def use(p, yy):
            parts = []
            for k in range(4):
                n = yy * 4 + k
                arrived(sbuf.at[p, n, oc], ac_r.at[p, n])
                x = sbuf[p, n].reshape(128, 256).astype(F32)
                sq = x * x
                ss[p] += sq[:, :128] + sq[:, 128:]
                pair = [gain[pl.ds(n * 2 + m, 1), :] for m in range(2)]
                parts.append((x * jnp.concatenate(pair, axis=1)).astype(BF))
            w = guw[pl.ds(pl.multiple_of(yy * 1024, 1024), 1024), :]
            gu[p] += jnp.dot(jnp.concatenate(parts, axis=1), w, preferred_element_type=F32)

        def near(p):
            total = tot[p]
            for d in (3, 2, 1):
                zz = along_z[d]
                arrived(zin.at[p, zz], z_r.at[p, zz])
                total = total + zin[p, zz].astype(F32)
            arrived(ffar.at[p], y_r.at[p, 8])
            total = total + ffar[p].astype(F32)
            sbuf[p, yz, c] = total.astype(BF)
            give(p, yz, 8, dev_far)
            for d in (3, 2, 1):
                zz = along_z[d]
                ref = sbuf.at[p, yz, c]
                send(ref, ref, az_s.at[p, d], ag_r.at[p, yz], at(1, f, y, zz, c))
            give_y(p, yz, 0)
            give_core(p, yz)

        def forward(p):
            for d in (3, 2, 1):
                n = y * 4 + along_z[d]
                arrived(sbuf.at[p, n, c], ag_r.at[p, n])
                if d == 3:
                    ref = sbuf.at[p, n, c]
                    send_if(at_end, ref, ref, ay_s.at[p, 9], ag_r.at[p, n], dev_far)
                give_y(p, n, d)
                give_core(p, n)

        def spread_opposite(p):
            n = far * 4 + z
            arrived(sbuf.at[p, n, c], ag_r.at[p, n])
            ref = sbuf.at[p, n, c]
            for d in (3, 2, 1):
                what = (ref, ref, az_s.at[p, 4 + d], ag_r.at[p, n], at(1, f, y, along_z[d], c))
                if d == 3:
                    send_if(z % 3 != 0, *what)
                else:
                    send(*what)
            give_core(p, n)

        def taken(p, group, d):
            n = group * 4 + along_z[d]
            arrived(sbuf.at[p, n, c], ag_r.at[p, n])
            give_core(p, n)

        def over_fin(p):
            tt = jnp.sum(ss[p], axis=1, keepdims=True)
            top = tt.astype(BF).astype(F32)
            low = iota((128, 128), 1) < 64
            xs[p, :, :, 512:] = jnp.where(low, top, tt - top).astype(BF).reshape(4, 32, 128)
            xs[p, :, :, :512] = gu[p].astype(BF).reshape(4, 32, 512)
            for d in (2, 1, 3):
                ff = (f + d) % 4
                send(xs.at[p, ff], xr.at[p, f], xs_s.at[p, d], xs_r.at[p, f], at(1, ff, y, z, c))

        def hide(p):
            mine = pl.ds(pl.multiple_of(f * 32, 32), 32)
            both = gu[p, mine, :]
            square = xs[p, f][:, 512:].astype(F32)
            for d in (1, 3, 2):
                ff = (f + d) % 4
                arrived(xr.at[p, ff], xs_r.at[p, ff])
                both = both + xr[p, ff][:, :512].astype(F32)
                square = square + xr[p, ff][:, 512:].astype(F32)
            scale = lax.rsqrt((square[:, 0:1] + square[:, 64:65]) / D + 1e-05)
            gate = both[:, :256] * scale
            hid[p, mine, :] = (gate / (1.0 + jnp.exp(-gate)) * (both[:, 256:] * scale)).astype(BF)
            for d in (2, 1, 3):
                ff = (f + d) % 4
                ref = hid.at[p, mine]
                send(ref, ref, xh_s.at[p, d], xh_r.at[p, f], at(1, ff, y, z, c))

        def lower(p):
            for d in (1, 3, 2):
                ff = (f + d) % 4
                ref = hid.at[p, pl.ds(pl.multiple_of(ff * 32, 32), 32)]
                arrived(ref, xh_r.at[p, ff])

            def columns(core):
                parts = []
                for half in range(2):
                    start = core * 2048 + half * 1024
                    w = dw[:, pl.ds(pl.multiple_of(start, 1024), 1024)]
                    value = jnp.dot(hid[p], w, preferred_element_type=F32)
                    parts.append(value.reshape(16, 8, 1024))
                return jnp.concatenate(parts, axis=1)

            cs2[p] = columns(oc).astype(BF)
            for g in range(4):
                part = pl.ds((y + ORDER[g]) % 4 * 4, 4)
                send(cs2.at[p, part], cr2.at[p, part], c2_s.at[p, g], c2_r.at[p, g], dev_core)
            own2[p] = columns(c)

        def paired2(p, n):
            return own2[p, n] + cr2[p, n].astype(F32)

        def beside2(p, g):
            yy = (y + ORDER[g]) % 4
            arrived(cr2.at[p, pl.ds(yy * 4, 4)], c2_r.at[p, g])
            to, dev = ((yfm2, dev_up), (yfp2, dev_down))[g - 1]
            for d in (3, 2, 1, 0):
                k = 3 - along_z[d]
                qs2[p, yy, k] = paired2(p, yy * 4 + k).astype(BF)
                send(
                    qs2.at[p, yy, k], to.at[p, k],
                    y2_s.at[p, (g - 1) * 4 + d], y2_r.at[p, (g - 1) * 4 + k], dev,
                )

        def opposite2(p):
            arrived(cr2.at[p, pl.ds(far * 4, 4)], c2_r.at[p, 0])
            for d in (3, 2, 1):
                zz = along_z[d]
                qs2[p, far, zz] = paired2(p, far * 4 + (3 - zz)).astype(BF)
                send(
                    qs2.at[p, far, zz], zfar2.at[p, z], zf2_s.at[p, d], zf2_r.at[p, z],
                    at(1, f, y, zz, c),
                )

        def onward2(p):
            value = paired2(p, far * 4 + zt)
            for d in (3, 2, 1):
                zz = along_z[d]
                arrived(zfar2.at[p, zz], zf2_r.at[p, zz])
                value = value + zfar2[p, zz].astype(F32)
            fs2[p] = value.astype(BF)
            send(fs2.at[p], ffar2.at[p], y2_s.at[p, 8], y2_r.at[p, 8], dev_far)

        def over_z2(p):
            part = pl.ds(y * 4, 4)
            arrived(cr2.at[p, part], c2_r.at[p, 3])

            def summed(k):
                arrived(yfm2.at[p, k], y2_r.at[p, k])
                arrived(yfp2.at[p, k], y2_r.at[p, 4 + k])
                return paired2(p, y * 4 + k) + yfm2[p, k].astype(F32) + yfp2[p, k].astype(F32)

            for d in (3, 2, 1):
                zz = along_z[d]
                zs2[p, zz] = summed(3 - zz).astype(BF)
                send(
                    zs2.at[p, zz], zin2.at[p, z], z2_s.at[p, d], z2_r.at[p, z], at(1, f, y, zz, c)
                )
            slab = pl.ds(pl.multiple_of(((y * 4 + zt) % 8) // 2 * 16, 16), 16)
            halves = []
            for half in range(2):
                kept = [
                    sbuf[p, c * 8 + half * 4 + m, y // 2, slab, :].astype(F32) for m in range(4)
                ]
                kept = jnp.concatenate(kept, axis=1)
                halves.append(jnp.where(zt % 2 == 0, kept[:8], kept[8:]))
            tot2[p] = summed(zt) + jnp.concatenate(halves, axis=0)

        def finish(p):
            total = tot2[p]
            for d in (3, 2, 1):
                zz = along_z[d]
                arrived(zin2.at[p, zz], z2_r.at[p, zz])
                total = total + zin2[p, zz].astype(F32)
            arrived(ffar2.at[p], y2_r.at[p, 8])
            total = total + ffar2[p].astype(F32)
            for k in range(16):
                rows = slice(k // 8 * 8, k // 8 * 8 + 8)
                fo[:, k, :] = total[rows, k % 8 * 128 : (k % 8 + 1) * 128]
            fb[p] = fo[...].astype(BF)
            for d in range(8):
                ff = (f + d // 2) % 4
                send(
                    fb.at[p, pl.ds(ff * 2, 2)], fin_in.at[j], f_s.at[p, d], f_r.at[j],
                    at(d % 2, ff, y, zt, p),
                )

        project(0)
        project(1)
        opposite(0)
        opposite(1)
        beside(0, 1)
        project(2)
        beside(1, 1)
        beside(0, 2)
        project(3)
        beside(1, 2)
        onward(0)
        over_z(0)
        onward(1)
        over_z(1)
        near(0)
        near(1)
        weights[1].wait()
        weights[2].wait()
        forward(0)
        forward(1)
        for p in range(2):
            spread_opposite(p)
            taken(p, up, 0)
            taken(p, down, 0)
        use(0, y)
        use(1, y)
        for d in (3, 2, 1):
            taken(0, up, d)
            taken(0, down, d)
            taken(0, far, d)
        use(0, up)
        use(0, down)
        use(0, far)
        over_fin(0)
        for d in (3, 2, 1):
            taken(1, far, d)
            taken(1, up, d)
            taken(1, down, d)
        use(1, far)
        use(1, up)
        use(1, down)
        over_fin(1)
        hide(0)
        hide(1)
        weights[3].wait()
        lower(0)
        opposite2(0)
        beside2(0, 1)
        beside2(0, 2)
        lower(1)
        opposite2(1)
        beside2(1, 1)
        beside2(1, 2)
        onward2(0)
        over_z2(0)
        onward2(1)
        over_z2(1)
        finish(0)
        finish(1)
        deliver()
        for cp in copies:
            cp.wait_send()
        for cond, what in maybe:
            pl.when(cond)(lambda what=what: make(*what).wait_send())


def moved(*args):
    def v(*shape, dtype=BF):
        return pltpu.VMEM(shape, dtype)

    scratch = [
        v(2, D), v(2, 128, 128, dtype=F32), v(2, 2048), v(2, 16, 128, dtype=F32), v(256, 128),
        v(4, 64, 128), v(4096), v(32, 128, dtype=F32), v(8, 2, 16, 128, dtype=F32),
        v(2, 256, 2048), v(256, 256, dtype=F32), v(256, 128),
        v(640, 4096), v(4096, 512), v(256, 4096),
        v(256, 128), v(4, 16, 128, dtype=F32), v(128, 128), v(4, 2, 128, 128), v(256, 640),
        v(4, 64, 128), v(256, 128, dtype=F32),
        v(2, 16, 64, 256, dtype=F32), v(2, 16, 64, 256), v(2, 16, 64, 256), v(2, 4, 4, 64, 256),
        v(2, 4, 64, 256), v(2, 64, 256), v(2, 64, 256), v(2, 4, 64, 256), v(2, 4, 64, 256),
        v(2, 4, 64, 256), v(2, 4, 64, 256), v(2, 64, 256, dtype=F32),
        v(2, 16, 2, 64, 256), v(2, 128, 512, dtype=F32), v(2, 128, 128, dtype=F32),
        v(2, 4, 32, 640), v(2, 4, 32, 640), v(2, 128, 256),
        v(2, 16, 16, 1024, dtype=F32), v(2, 16, 16, 1024), v(2, 16, 16, 1024),
        v(2, 4, 4, 16, 1024), v(2, 4, 16, 1024), v(2, 16, 1024), v(2, 16, 1024),
        v(2, 4, 16, 1024), v(2, 4, 16, 1024), v(2, 4, 16, 1024), v(2, 4, 16, 1024),
        v(2, 16, 1024, dtype=F32), v(8, 16, 128, dtype=F32), v(2, 8, 16, 128), v(8, 2, 16, 128),
    ]
    counts = [
        (2,), (4,), (4,), (16,), (16,), (4,), (4,), (8, 4), (8, 4),
        (2, 4), (2, 4), (2, 9), (2, 9), (2, 4), (2, 4), (2, 4), (2, 4),
        (2, 8), (2, 12), (2, 16), (2, 16), (2, 16),
        (2, 4), (2, 4), (2, 4), (2, 4), (2, 4), (2, 4), (2, 9), (2, 9), (2, 4), (2, 4),
        (2, 4), (2, 4), (2, 8), (8,),
    ]
    scratch += [pltpu.SemaphoreType.DMA(k) for k in counts]
    vm, hbm = pl.BlockSpec(memory_space=pltpu.VMEM), pl.BlockSpec(memory_space=pl.ANY)
    sm = pl.BlockSpec(memory_space=pltpu.SMEM)
    return pl.pallas_call(
        kernel,
        out_shape=jax.ShapeDtypeStruct((2, D), BF),
        in_specs=[hbm, hbm, sm, hbm, hbm, hbm, hbm, hbm, hbm, hbm],
        out_specs=vm,
        scratch_shapes=scratch,
        compiler_params=pltpu.CompilerParams(
            collective_id=0, has_side_effects=True, vmem_limit_bytes=56 * 1024 * 1024
        ),
    )(*args)


def on_device(
    queries, new_entries, cached_entries, lengths, residual, norm_gain,
    out_weight, gate_weight, up_weight, down_weight,
):
    return moved(
        queries, new_entries, lengths, cached_entries[0], residual, norm_gain,
        out_weight[0], gate_weight[0], up_weight[0], down_weight[0],
    )


def solution(mesh):
    placed = (
        P(("fin", "fhid"), None),
        P(("fin", "fhid"), None),
        P("side", ("fin", "fhid"), None, None),
        P(("fin", "fhid")),
        P(("fin", "fhid"), None),
        P("fin"),
        P("side", "fhid", "fin"),
        P("side", "fin", "fhid"),
        P("side", "fin", "fhid"),
        P("side", "fhid", "fin"),
    )
    return jax.shard_map(
        on_device, mesh=mesh, in_specs=placed, out_specs=P(("fin", "fhid"), None), check_vma=False
    )
```

```python
import math

import jax
import jax.numpy as jnp
from jax import lax
from jax.experimental import pallas as pl
from jax.experimental.pallas import tpu as pltpu
from jax.sharding import PartitionSpec as P

D = 16384
BF = jnp.bfloat16
F32 = jnp.float32
MESH = pl.DeviceIdType.MESH
ORDER = (2, 1, 3, 0)


def iota(shape, axis):
    return lax.broadcasted_iota(jnp.int32, shape, axis)


def selection(source, rows=256):
    t = iota((rows, 256), 0)
    return (iota((rows, 256), 1) == source(t)).astype(F32).astype(BF)


def arrived(ref, sem):
    pltpu.make_async_copy(ref, ref, sem).wait()


def attend(q, fresh, lens, kv, kv_copies, sco):
    scale = 1.0 / math.sqrt(128)
    for i in range(2):
        kv_copies[i * 2].wait()
        for g in range(8):
            at = (i * 8 + g) * 16
            sco[at : at + 16, :] = lax.dot_general(
                q[at : at + 16, :],
                kv[i, :, g * 128 : (g + 1) * 128],
                (((1,), (1,)), ((), ())),
                preferred_element_type=F32,
            )
    first = iota((256, 1), 0) < 128
    length = jnp.where(first, lens[0], lens[1])
    scores = jnp.where(iota((256, 256), 1) < length, sco[...] * scale, jnp.float32(-1e30))

    def spread(offset):
        rows = [
            jnp.broadcast_to(fresh[i * 16 + offset + g : i * 16 + offset + g + 1, :], (16, 128))
            for i in range(2)
            for g in range(8)
        ]
        return jnp.concatenate(rows, axis=0)

    own = jnp.sum(q[...].astype(F32) * spread(0), axis=1, keepdims=True) * scale
    top = jnp.maximum(jnp.max(scores, axis=1, keepdims=True), own)
    expo = jnp.exp(scores - top)
    own_exp = jnp.exp(own - top)
    total = jnp.sum(expo, axis=1, keepdims=True) + own_exp
    weights = (expo / total).astype(BF)
    own_weight = (own_exp / total).astype(BF).astype(F32)
    parts = []
    for i in range(2):
        kv_copies[i * 2 + 1].wait()
        for g in range(8):
            at = (i * 8 + g) * 16
            parts.append(
                jnp.dot(
                    weights[at : at + 16, :],
                    kv[i, :, 1024 + g * 128 : 1024 + (g + 1) * 128],
                    preferred_element_type=F32,
                )
            )
    return (jnp.concatenate(parts, axis=0) + own_weight * spread(8)).astype(BF)


def kernel(
    q_hbm, fresh_hbm, lens, kv_hbm, res_hbm, gain_hbm, ow_hbm, gw_hbm, uw_hbm, dw_hbm, out,
    wide, wide_f, narrow, narrow_f, q, res_src, gain_in, gain, fin_f,
    kv, sco, m2s,
    ow, guw, dw, m2, comb, m2o, m2all, lhs, rin, resid,
    own, cs, cr, qs, yd, sum1, zfar, fs, ffar, yfm, yfp, zs, zin, tot,
    sbuf, gu, ss, xs, xr, hid,
    own2, cs2, cr2, qs2, yd2, sum2, zfar2, fs2, ffar2, yfm2, yfp2, zs2, zin2, tot2, fo, fb, fin_in,
    in_sem, w_sem, kv_sem, m2_s, m2_r, rs_s, rs_r, xa_s, xa_r,
    c_s, c_r, y_s, y_r, z_s, z_r, zf_s, zf_r, az_s, ay_s, ac_s, ag_r, ac_r,
    xs_s, xs_r, xh_s, xh_r, c2_s, c2_r, y2_s, y2_r, z2_s, z2_r, zf2_s, zf2_r, f_s, f_r,
):
    side, f, h = lax.axis_index("side"), lax.axis_index("fin"), lax.axis_index("fhid")
    y, z, c = h // 8, (h // 2) % 4, h % 2
    yz = h // 2
    oc = 1 - c
    j = f * 2 + c
    zt = 3 - z
    along_z = (z, z + 1 - 2 * (z % 2), (z + 2) % 4, 3 - z)
    at_end = z % 3 == 0
    copies = []

    def at(s, ff, yy, zz, cc):
        return (s, ff, (yy * 4 + zz) * 2 + cc)

    def make(src, dst, s_sem, r_sem, dev):
        return pltpu.make_async_remote_copy(
            src_ref=src, dst_ref=dst, send_sem=s_sem, recv_sem=r_sem,
            device_id=dev, device_id_type=MESH,
        )

    def send(*what):
        cp = make(*what)
        cp.start()
        copies.append(cp)

    maybe = []

    def send_if(cond, *what):
        pl.when(cond)(lambda: make(*what).start())
        maybe.append((cond, what))

    barrier = pltpu.get_barrier_semaphore()

    def greet(dev):
        pl.semaphore_signal(barrier, inc=1, device_id=dev, device_id_type=MESH)

    def deliver():
        for s in range(8):
            arrived(fin_in.at[s], f_r.at[s])
            fin_f[s] = fin_in[s].astype(F32)
            parts = [fin_f[s, :, k, :] for k in range(16)]
            out[:, s * 2048 : (s + 1) * 2048] = jnp.concatenate(parts, axis=1).astype(BF)

    @pl.when(side == 0)
    def _attention_side():
        kv_copies = []
        for i in range(2):
            for k in range(2):
                part = (i, slice(None), pl.ds(k * 1024, 1024))
                cp = pltpu.make_async_copy(kv_hbm.at[part], kv.at[part], kv_sem.at[i * 2 + k])
                cp.start()
                kv_copies.append(cp)
        first_in = pltpu.make_async_copy(q_hbm, wide, in_sem.at[0])
        second_in = pltpu.make_async_copy(fresh_hbm, narrow, in_sem.at[1])
        first_in.start()
        second_in.start()
        for d in range(8):
            greet(at(1, d // 2, y, zt, d % 2))
        first_in.wait()
        second_in.wait()
        value = wide[...].astype(F32)
        for k in range(128):
            wide_f[:, k, :] = value[:, k * 128 : (k + 1) * 128]
        q[...] = wide_f[...].reshape(256, 128).astype(BF)
        value = narrow[...].astype(F32)
        for k in range(16):
            narrow_f[:, k, :] = value[:, k * 128 : (k + 1) * 128]
        fresh = narrow_f[...].reshape(32, 128)
        mixed = attend(q, fresh, lens, kv, kv_copies, sco)
        sel = selection(
            lambda t: (t // 4) % 2 * 128 + t // 16 * 8 + (t // 8) % 2 * 4 + t % 4
        )
        m2s[...] = jnp.dot(sel, mixed, preferred_element_type=F32).astype(BF)
        pl.semaphore_wait(barrier, 16)
        for b in range(16):
            send(
                m2s.at[pl.ds(b * 16, 16)],
                m2.at[pl.ds(pl.multiple_of(yz * 16, 16), 16)],
                m2_s.at[b],
                m2_r.at[yz],
                at(1, f, b // 4, b % 4, c),
            )
        for cp in copies:
            cp.wait_send()
        deliver()

    @pl.when(side == 1)
    def _mlp_side():
        copies.clear()
        up, down, far = (y + 1) % 4, (y + 3) % 4, (y + 2) % 4
        dev_up, dev_down, dev_far = (at(1, f, yy, z, c) for yy in (up, down, far))
        dev_core = at(1, f, y, z, oc)
        first_in = pltpu.make_async_copy(res_hbm, wide, in_sem.at[0])
        second_in = pltpu.make_async_copy(gain_hbm, gain_in, in_sem.at[1])
        first_in.start()
        second_in.start()
        for d in range(16):
            greet(at(0, f, d // 4, d % 4, c))
        for d in range(1, 4):
            greet(at(1, (f + d) % 4, y, z, c))
            greet(at(1, (f + d) % 4, y, z, oc))
            greet(at(1, f, y, along_z[d], c))
        greet(dev_up)
        greet(dev_down)
        greet(dev_far)
        greet(dev_core)
        for d in range(8):
            greet(at(1, d // 2, y, zt, d % 2))
        weights = [
            pltpu.make_async_copy(a, b, w_sem.at[k])
            for k, (a, b) in enumerate(
                (
                    (ow_hbm, ow.at[pl.ds(0, 512)]),
                    (gw_hbm, guw.at[:, pl.ds(0, 256)]),
                    (uw_hbm, guw.at[:, pl.ds(256, 256)]),
                    (dw_hbm, dw),
                )
            )
        ]
        for cp in weights:
            cp.start()
        gu[...] = jnp.zeros_like(gu)
        ss[...] = jnp.zeros_like(ss)
        first_in.wait()
        second_in.wait()
        value = wide[...].astype(F32)
        for k in range(128):
            wide_f[:, k, :] = value[:, k * 128 : (k + 1) * 128]
        for k in range(4):
            rows = wide_f[:, k * 32 : (k + 1) * 32, :]
            res_src[k] = rows.reshape(64, 128).astype(BF)
        gain[...] = gain_in[...].astype(F32).reshape(32, 128)
        pl.semaphore_wait(barrier, 29)

        for d in range(1, 4):
            ff = (f + d) % 4
            send(res_src.at[ff], rin.at[f], rs_s.at[d], rs_r.at[f], at(1, ff, y, z, c))
        rin[f] = res_src[f]
        for d in range(1, 4):
            ff = (f + d) % 4
            arrived(rin.at[ff], rs_r.at[ff])
        sel = selection(
            lambda t: (t // 2) % 4 * 64 + ((t % 2) * 16 + (t // 8) % 16) * 2 + t // 128
        )
        resid[...] = jnp.dot(sel, rin[...].reshape(256, 128), preferred_element_type=F32)
        eight = [
            resid[half * 128 + n * 8 : half * 128 + n * 8 + 8, :] for n in range(16) for half in range(2)
        ]
        eight = jnp.concatenate(eight, axis=1)
        ow[512:528, :] = jnp.concatenate([eight, jnp.zeros_like(eight)], axis=0).astype(BF)
        ow[528:, :] = jnp.zeros((112, 4096), BF)
        t = iota((256, 128), 0)
        row_yz = ((t // 128 + c) % 2 * 64 + t % 64) // 8
        here = (row_yz == yz) & (t // 64 % 2 == c) & (t % 8 == iota((256, 128), 1))
        lhs[:, 512:] = here.astype(F32).astype(BF)

        pick = selection(
            lambda t: (t // 64) % 2 * 128
            + ((t // 128 + c) % 2 * 8 + (t // 8) % 8) * 8
            + t % 2 * 4
            + t // 256,
            1024,
        )
        row_fin = (iota((1024, 128), 0) // 2) % 4
        for e in (0, 1, 3, 2):
            yy = (y + e) % 4
            for k in range(4):
                n = yy * 4 + k
                arrived(m2.at[pl.ds(pl.multiple_of(n * 16, 16), 16)], m2_r.at[n])
            rows = pl.ds(pl.multiple_of(yy * 64, 64), 64)
            part = pl.ds(pl.multiple_of(yy * 32, 32), 32)
            comb[...] = m2[rows, :].astype(F32).reshape(4, 16, 128)
            other = comb[:, pl.ds(pl.multiple_of(oc * 8, 8), 8), :]
            m2o[part, :] = other.reshape(32, 128).astype(BF)
            mine = comb[:, pl.ds(pl.multiple_of(c * 8, 8), 8), :]
            m2all[f, c, part, :] = mine.reshape(32, 128).astype(BF)
            for d in (2, 1, 3):
                ff = (f + d) % 4
                to = m2all.at[f, c, part]
                send(to, to, xa_s.at[d, e], xa_r.at[j, yy], at(1, ff, y, z, c))
                send(m2o.at[part], to, xa_s.at[4 + d, e], xa_r.at[j, yy], at(1, ff, y, z, oc))
            send(m2o.at[part], m2all.at[f, c, part], xa_s.at[0, e], xa_r.at[j, yy], dev_core)

        def quarter(ff, cc):
            for k in range(4):
                arrived(m2all.at[ff, cc, pl.ds(k * 32, 32)], xa_r.at[ff * 2 + cc, k])

        quarter(f, oc)
        picked = jnp.where(
            row_fin == f, jnp.dot(pick, m2all[f].reshape(256, 128), preferred_element_type=F32), 0.0
        )
        for d in (1, 3, 2):
            ff = (f + d) % 4
            quarter(ff, c)
            quarter(ff, oc)
            picked = jnp.where(
                row_fin == ff,
                jnp.dot(pick, m2all[ff].reshape(256, 128), preferred_element_type=F32),
                picked,
            )
        for k in range(4):
            lhs[:, k * 128 : (k + 1) * 128] = picked[k * 256 : (k + 1) * 256, :].astype(BF)
        weights[0].wait()

        def project(g):
            yy = (y + ORDER[g]) % 4

            w = ow[:, pl.ds(pl.multiple_of(yy * 1024, 1024), 1024)]
            value = jnp.dot(lhs[...], w, preferred_element_type=F32)
            for p in range(2):
                for k in range(4):
                    cols = slice(k * 256, (k + 1) * 256)
                    cs[p, yy * 4 + k] = value[128 + p * 64 : 192 + p * 64, cols].astype(BF)
                    own[p, yy * 4 + k] = value[p * 64 : p * 64 + 64, cols]
            part = pl.ds(yy * 4, 4)
            for p in range(2):
                send(cs.at[p, part], cr.at[p, part], c_s.at[p, g], c_r.at[p, g], dev_core)

        def paired(p, n):
            return own[p, n] + cr[p, n].astype(F32)

        def beside(p, g):
            yy = (y + ORDER[g]) % 4
            arrived(cr.at[p, pl.ds(yy * 4, 4)], c_r.at[p, g])
            to, dev = ((yfm, dev_up), (yfp, dev_down))[g - 1]
            for d in (3, 2, 1, 0):
                k = along_z[d]
                qs[p, yy, k] = paired(p, yy * 4 + k).astype(BF)
                send(
                    qs.at[p, yy, k], to.at[p, k],
                    y_s.at[p, (g - 1) * 4 + d], y_r.at[p, (g - 1) * 4 + k], dev,
                )

        def opposite(p):
            arrived(cr.at[p, pl.ds(far * 4, 4)], c_r.at[p, 0])
            for d in (3, 2, 1):
                zz = along_z[d]
                qs[p, far, zz] = paired(p, far * 4 + zz).astype(BF)
                what = (
                    qs.at[p, far, zz], zfar.at[p, z], zf_s.at[p, d], zf_r.at[p, z],
                    at(1, f, y, zz, c),
                )
                if d == 3:
                    send_if(z % 3 != 0, *what)
                    send_if(
                        at_end, qs.at[p, far, zz], yd.at[p], y_s.at[p, 9], y_r.at[p, 9], dev_far
                    )
                else:
                    send(*what)

        def onward(p):
            value = paired(p, far * 4 + z)
            for d in (2, 1):
                zz = along_z[d]
                arrived(zfar.at[p, zz], zf_r.at[p, zz])
                value = value + zfar[p, zz].astype(F32)
            sum1[...] = value

            @pl.when(z % 3 != 0)
            def _from_third():
                arrived(zfar.at[p, zt], zf_r.at[p, zt])
                sum1[...] += zfar[p, zt].astype(F32)

            fs[p] = sum1[...].astype(BF)
            send(fs.at[p], ffar.at[p], y_s.at[p, 8], y_r.at[p, 8], dev_far)

        def over_z(p):
            part = pl.ds(y * 4, 4)
            arrived(cr.at[p, part], c_r.at[p, 3])

            def summed(k):
                arrived(yfm.at[p, k], y_r.at[p, k])
                arrived(yfp.at[p, k], y_r.at[p, 4 + k])
                return paired(p, y * 4 + k) + yfm[p, k].astype(F32) + yfp[p, k].astype(F32)

            for d in (3, 2, 1):
                zz = along_z[d]
                value = summed(zz)
                if d == 3:
                    sum1[...] = value

                    @pl.when(at_end)
                    def _from_opposite():
                        arrived(yd.at[p], y_r.at[p, 9])
                        sum1[...] += yd[p].astype(F32)

                    value = sum1[...]
                zs[p, zz] = value.astype(BF)
                send(zs.at[p, zz], zin.at[p, z], z_s.at[p, d], z_r.at[p, z], at(1, f, y, zz, c))
            tot[p] = summed(z)

        def give(p, n, slot, dev):
            ref = sbuf.at[p, n, c]
            send(ref, ref, ay_s.at[p, slot], ag_r.at[p, n], dev)

        def give_y(p, n, k):
            give(p, n, 2 * k, dev_up)
            give(p, n, 2 * k + 1, dev_down)

        def give_core(p, n):
            ref = sbuf.at[p, n, c]
            send(ref, ref, ac_s.at[p, n], ac_r.at[p, n], dev_core)

        def use(p, yy):
            parts = []
            for k in range(4):
                n = yy * 4 + k
                arrived(sbuf.at[p, n, oc], ac_r.at[p, n])
                x = sbuf[p, n].reshape(128, 256).astype(F32)
                sq = x * x
                ss[p] += sq[:, :128] + sq[:, 128:]
                pair = [gain[pl.ds(n * 2 + m, 1), :] for m in range(2)]
                parts.append((x * jnp.concatenate(pair, axis=1)).astype(BF))
            w = guw[pl.ds(pl.multiple_of(yy * 1024, 1024), 1024), :]
            gu[p] += jnp.dot(jnp.concatenate(parts, axis=1), w, preferred_element_type=F32)

        def near(p):
            total = tot[p]
            for d in (3, 2, 1):
                zz = along_z[d]
                arrived(zin.at[p, zz], z_r.at[p, zz])
                total = total + zin[p, zz].astype(F32)
            arrived(ffar.at[p], y_r.at[p, 8])
            total = total + ffar[p].astype(F32)
            sbuf[p, yz, c] = total.astype(BF)
            give(p, yz, 8, dev_far)
            for d in (3, 2, 1):
                zz = along_z[d]
                ref = sbuf.at[p, yz, c]
                send(ref, ref, az_s.at[p, d], ag_r.at[p, yz], at(1, f, y, zz, c))
            give_y(p, yz, 0)
            give_core(p, yz)

        def forward(p):
            for d in (3, 2, 1):
                n = y * 4 + along_z[d]
                arrived(sbuf.at[p, n, c], ag_r.at[p, n])
                if d == 3:
                    ref = sbuf.at[p, n, c]
                    send_if(at_end, ref, ref, ay_s.at[p, 9], ag_r.at[p, n], dev_far)
                give_y(p, n, d)
                give_core(p, n)

        def spread_opposite(p):
            n = far * 4 + z
            arrived(sbuf.at[p, n, c], ag_r.at[p, n])
            ref = sbuf.at[p, n, c]
            for d in (3, 2, 1):
                what = (ref, ref, az_s.at[p, 4 + d], ag_r.at[p, n], at(1, f, y, along_z[d], c))
                if d == 3:
                    send_if(z % 3 != 0, *what)
                else:
                    send(*what)
            give_core(p, n)

        def taken(p, group, d):
            n = group * 4 + along_z[d]
            arrived(sbuf.at[p, n, c], ag_r.at[p, n])
            give_core(p, n)

        def over_fin(p):
            tt = jnp.sum(ss[p], axis=1, keepdims=True)
            top = tt.astype(BF).astype(F32)
            low = iota((128, 128), 1) < 64
            xs[p, :, :, 512:] = jnp.where(low, top, tt - top).astype(BF).reshape(4, 32, 128)
            xs[p, :, :, :512] = gu[p].astype(BF).reshape(4, 32, 512)
            for d in (2, 1, 3):
                ff = (f + d) % 4
                send(xs.at[p, ff], xr.at[p, f], xs_s.at[p, d], xs_r.at[p, f], at(1, ff, y, z, c))

        def hide(p):
            mine = pl.ds(pl.multiple_of(f * 32, 32), 32)
            both = gu[p, mine, :]
            square = xs[p, f][:, 512:].astype(F32)
            for d in (1, 3, 2):
                ff = (f + d) % 4
                arrived(xr.at[p, ff], xs_r.at[p, ff])
                both = both + xr[p, ff][:, :512].astype(F32)
                square = square + xr[p, ff][:, 512:].astype(F32)
            scale = lax.rsqrt((square[:, 0:1] + square[:, 64:65]) / D + 1e-05)
            gate = both[:, :256] * scale
            hid[p, mine, :] = (gate / (1.0 + jnp.exp(-gate)) * (both[:, 256:] * scale)).astype(BF)
            for d in (2, 1, 3):
                ff = (f + d) % 4
                ref = hid.at[p, mine]
                send(ref, ref, xh_s.at[p, d], xh_r.at[p, f], at(1, ff, y, z, c))

        def lower(p):
            for d in (1, 3, 2):
                ff = (f + d) % 4
                ref = hid.at[p, pl.ds(pl.multiple_of(ff * 32, 32), 32)]
                arrived(ref, xh_r.at[p, ff])

            def columns(core):
                parts = []
                for half in range(2):
                    start = core * 2048 + half * 1024
                    w = dw[:, pl.ds(pl.multiple_of(start, 1024), 1024)]
                    value = jnp.dot(hid[p], w, preferred_element_type=F32)
                    parts.append(value.reshape(16, 8, 1024))
                return jnp.concatenate(parts, axis=1)

            cs2[p] = columns(oc).astype(BF)
            for g in range(4):
                part = pl.ds((y + ORDER[g]) % 4 * 4, 4)
                send(cs2.at[p, part], cr2.at[p, part], c2_s.at[p, g], c2_r.at[p, g], dev_core)
            own2[p] = columns(c)

        def paired2(p, n):
            return own2[p, n] + cr2[p, n].astype(F32)

        def beside2(p, g):
            yy = (y + ORDER[g]) % 4
            arrived(cr2.at[p, pl.ds(yy * 4, 4)], c2_r.at[p, g])
            to, dev = ((yfm2, dev_up), (yfp2, dev_down))[g - 1]
            for d in (3, 2, 1, 0):
                k = 3 - along_z[d]
                qs2[p, yy, k] = paired2(p, yy * 4 + k).astype(BF)
                send(
                    qs2.at[p, yy, k], to.at[p, k],
                    y2_s.at[p, (g - 1) * 4 + d], y2_r.at[p, (g - 1) * 4 + k], dev,
                )

        def opposite2(p):
            arrived(cr2.at[p, pl.ds(far * 4, 4)], c2_r.at[p, 0])
            for d in (3, 2, 1):
                zz = along_z[d]
                qs2[p, far, zz] = paired2(p, far * 4 + (3 - zz)).astype(BF)
                what = (
                    qs2.at[p, far, zz], zfar2.at[p, z], zf2_s.at[p, d], zf2_r.at[p, z],
                    at(1, f, y, zz, c),
                )
                if d == 3:
                    send_if(z % 3 != 0, *what)
                    send_if(
                        at_end, qs2.at[p, far, zz], yd2.at[p], y2_s.at[p, 9], y2_r.at[p, 9], dev_far
                    )
                else:
                    send(*what)

        def onward2(p):
            value = paired2(p, far * 4 + zt)
            for d in (2, 1):
                zz = along_z[d]
                arrived(zfar2.at[p, zz], zf2_r.at[p, zz])
                value = value + zfar2[p, zz].astype(F32)
            sum2[...] = value

            @pl.when(z % 3 != 0)
            def _from_third():
                arrived(zfar2.at[p, zt], zf2_r.at[p, zt])
                sum2[...] += zfar2[p, zt].astype(F32)

            fs2[p] = sum2[...].astype(BF)
            send(fs2.at[p], ffar2.at[p], y2_s.at[p, 8], y2_r.at[p, 8], dev_far)

        def over_z2(p):
            part = pl.ds(y * 4, 4)
            arrived(cr2.at[p, part], c2_r.at[p, 3])

            def summed(k):
                arrived(yfm2.at[p, k], y2_r.at[p, k])
                arrived(yfp2.at[p, k], y2_r.at[p, 4 + k])
                return paired2(p, y * 4 + k) + yfm2[p, k].astype(F32) + yfp2[p, k].astype(F32)

            for d in (3, 2, 1):
                zz = along_z[d]
                value = summed(3 - zz)
                if d == 3:
                    sum2[...] = value

                    @pl.when(at_end)
                    def _from_opposite():
                        arrived(yd2.at[p], y2_r.at[p, 9])
                        sum2[...] += yd2[p].astype(F32)

                    value = sum2[...]
                zs2[p, zz] = value.astype(BF)
                send(
                    zs2.at[p, zz], zin2.at[p, z], z2_s.at[p, d], z2_r.at[p, z], at(1, f, y, zz, c)
                )
            slab = pl.ds(pl.multiple_of(((y * 4 + zt) % 8) // 2 * 16, 16), 16)
            halves = []
            for half in range(2):
                kept = [
                    sbuf[p, c * 8 + half * 4 + m, y // 2, slab, :].astype(F32) for m in range(4)
                ]
                kept = jnp.concatenate(kept, axis=1)
                halves.append(jnp.where(zt % 2 == 0, kept[:8], kept[8:]))
            tot2[p] = summed(zt) + jnp.concatenate(halves, axis=0)

        def finish(p):
            total = tot2[p]
            for d in (3, 2, 1):
                zz = along_z[d]
                arrived(zin2.at[p, zz], z2_r.at[p, zz])
                total = total + zin2[p, zz].astype(F32)
            arrived(ffar2.at[p], y2_r.at[p, 8])
            total = total + ffar2[p].astype(F32)
            for k in range(16):
                rows = slice(k // 8 * 8, k // 8 * 8 + 8)
                fo[:, k, :] = total[rows, k % 8 * 128 : (k % 8 + 1) * 128]
            fb[p] = fo[...].astype(BF)
            for d in range(8):
                ff = (f + d // 2) % 4
                send(
                    fb.at[p, pl.ds(ff * 2, 2)], fin_in.at[j], f_s.at[p, d], f_r.at[j],
                    at(d % 2, ff, y, zt, p),
                )

        project(0)
        project(1)
        opposite(0)
        opposite(1)
        beside(0, 1)
        project(2)
        beside(1, 1)
        beside(0, 2)
        project(3)
        beside(1, 2)
        onward(0)
        over_z(0)
        onward(1)
        over_z(1)
        near(0)
        near(1)
        weights[1].wait()
        weights[2].wait()
        forward(0)
        forward(1)
        for p in range(2):
            spread_opposite(p)
            taken(p, up, 0)
            taken(p, down, 0)
        use(0, y)
        use(1, y)
        for d in (3, 2, 1):
            taken(0, up, d)
            taken(0, down, d)
            taken(0, far, d)
        use(0, up)
        use(0, down)
        use(0, far)
        over_fin(0)
        for d in (3, 2, 1):
            taken(1, far, d)
            taken(1, up, d)
            taken(1, down, d)
        use(1, far)
        use(1, up)
        use(1, down)
        over_fin(1)
        hide(0)
        hide(1)
        weights[3].wait()
        lower(0)
        opposite2(0)
        beside2(0, 1)
        beside2(0, 2)
        lower(1)
        opposite2(1)
        beside2(1, 1)
        beside2(1, 2)
        onward2(0)
        over_z2(0)
        onward2(1)
        over_z2(1)
        finish(0)
        finish(1)
        deliver()
        for cp in copies:
            cp.wait_send()
        for cond, what in maybe:
            pl.when(cond)(lambda what=what: make(*what).wait_send())


def moved(*args):
    def v(*shape, dtype=BF):
        return pltpu.VMEM(shape, dtype)

    scratch = [
        v(2, D), v(2, 128, 128, dtype=F32), v(2, 2048), v(2, 16, 128, dtype=F32), v(256, 128),
        v(4, 64, 128), v(4096), v(32, 128, dtype=F32), v(8, 2, 16, 128, dtype=F32),
        v(2, 256, 2048), v(256, 256, dtype=F32), v(256, 128),
        v(640, 4096), v(4096, 512), v(256, 4096),
        v(256, 128), v(4, 16, 128, dtype=F32), v(128, 128), v(4, 2, 128, 128), v(256, 640),
        v(4, 64, 128), v(256, 128, dtype=F32),
        v(2, 16, 64, 256, dtype=F32), v(2, 16, 64, 256), v(2, 16, 64, 256), v(2, 4, 4, 64, 256),
        v(2, 64, 256), v(64, 256, dtype=F32),
        v(2, 4, 64, 256), v(2, 64, 256), v(2, 64, 256), v(2, 4, 64, 256), v(2, 4, 64, 256),
        v(2, 4, 64, 256), v(2, 4, 64, 256), v(2, 64, 256, dtype=F32),
        v(2, 16, 2, 64, 256), v(2, 128, 512, dtype=F32), v(2, 128, 128, dtype=F32),
        v(2, 4, 32, 640), v(2, 4, 32, 640), v(2, 128, 256),
        v(2, 16, 16, 1024, dtype=F32), v(2, 16, 16, 1024), v(2, 16, 16, 1024),
        v(2, 4, 4, 16, 1024), v(2, 16, 1024), v(16, 1024, dtype=F32),
        v(2, 4, 16, 1024), v(2, 16, 1024), v(2, 16, 1024),
        v(2, 4, 16, 1024), v(2, 4, 16, 1024), v(2, 4, 16, 1024), v(2, 4, 16, 1024),
        v(2, 16, 1024, dtype=F32), v(8, 16, 128, dtype=F32), v(2, 8, 16, 128), v(8, 2, 16, 128),
    ]
    counts = [
        (2,), (4,), (4,), (16,), (16,), (4,), (4,), (8, 4), (8, 4),
        (2, 4), (2, 4), (2, 10), (2, 10), (2, 4), (2, 4), (2, 4), (2, 4),
        (2, 8), (2, 12), (2, 16), (2, 16), (2, 16),
        (2, 4), (2, 4), (2, 4), (2, 4), (2, 4), (2, 4), (2, 10), (2, 10), (2, 4), (2, 4),
        (2, 4), (2, 4), (2, 8), (8,),
    ]
    scratch += [pltpu.SemaphoreType.DMA(k) for k in counts]
    vm, hbm = pl.BlockSpec(memory_space=pltpu.VMEM), pl.BlockSpec(memory_space=pl.ANY)
    sm = pl.BlockSpec(memory_space=pltpu.SMEM)
    return pl.pallas_call(
        kernel,
        out_shape=jax.ShapeDtypeStruct((2, D), BF),
        in_specs=[hbm, hbm, sm, hbm, hbm, hbm, hbm, hbm, hbm, hbm],
        out_specs=vm,
        scratch_shapes=scratch,
        compiler_params=pltpu.CompilerParams(
            collective_id=0, has_side_effects=True, vmem_limit_bytes=56 * 1024 * 1024
        ),
    )(*args)


def on_device(
    queries, new_entries, cached_entries, lengths, residual, norm_gain,
    out_weight, gate_weight, up_weight, down_weight,
):
    return moved(
        queries, new_entries, lengths, cached_entries[0], residual, norm_gain,
        out_weight[0], gate_weight[0], up_weight[0], down_weight[0],
    )


def solution(mesh):
    placed = (
        P(("fin", "fhid"), None),
        P(("fin", "fhid"), None),
        P("side", ("fin", "fhid"), None, None),
        P(("fin", "fhid")),
        P(("fin", "fhid"), None),
        P("fin"),
        P("side", "fhid", "fin"),
        P("side", "fin", "fhid"),
        P("side", "fin", "fhid"),
        P("side", "fhid", "fin"),
    )
    return jax.shard_map(
        on_device, mesh=mesh, in_specs=placed, out_specs=P(("fin", "fhid"), None), check_vma=False
    )
```

```python
import math

import jax
import jax.numpy as jnp
from jax import lax
from jax.experimental import pallas as pl
from jax.experimental.pallas import tpu as pltpu
from jax.sharding import PartitionSpec as P

D = 16384
BF = jnp.bfloat16
F32 = jnp.float32
MESH = pl.DeviceIdType.MESH
ORDER = (2, 1, 3, 0)


def iota(shape, axis):
    return lax.broadcasted_iota(jnp.int32, shape, axis)


def selection(source, rows=256):
    t = iota((rows, 256), 0)
    return (iota((rows, 256), 1) == source(t)).astype(F32).astype(BF)


def arrived(ref, sem):
    pltpu.make_async_copy(ref, ref, sem).wait()


def attend(q, fresh, lens, kv, kv_copies, sco):
    scale = 1.0 / math.sqrt(128)
    for i in range(2):
        kv_copies[i * 2].wait()
        for g in range(8):
            at = (i * 8 + g) * 16
            sco[at : at + 16, :] = lax.dot_general(
                q[at : at + 16, :],
                kv[i, :, g * 128 : (g + 1) * 128],
                (((1,), (1,)), ((), ())),
                preferred_element_type=F32,
            )
    first = iota((256, 1), 0) < 128
    length = jnp.where(first, lens[0], lens[1])
    scores = jnp.where(iota((256, 256), 1) < length, sco[...] * scale, jnp.float32(-1e30))

    def spread(offset):
        rows = [
            jnp.broadcast_to(fresh[i * 16 + offset + g : i * 16 + offset + g + 1, :], (16, 128))
            for i in range(2)
            for g in range(8)
        ]
        return jnp.concatenate(rows, axis=0)

    own = jnp.sum(q[...].astype(F32) * spread(0), axis=1, keepdims=True) * scale
    top = jnp.maximum(jnp.max(scores, axis=1, keepdims=True), own)
    expo = jnp.exp(scores - top)
    own_exp = jnp.exp(own - top)
    total = jnp.sum(expo, axis=1, keepdims=True) + own_exp
    weights = (expo / total).astype(BF)
    own_weight = (own_exp / total).astype(BF).astype(F32)
    parts = []
    for i in range(2):
        kv_copies[i * 2 + 1].wait()
        for g in range(8):
            at = (i * 8 + g) * 16
            parts.append(
                jnp.dot(
                    weights[at : at + 16, :],
                    kv[i, :, 1024 + g * 128 : 1024 + (g + 1) * 128],
                    preferred_element_type=F32,
                )
            )
    return (jnp.concatenate(parts, axis=0) + own_weight * spread(8)).astype(BF)


def kernel(
    q_hbm, fresh_hbm, lens, kv_hbm, res_hbm, gain_hbm, ow_hbm, gw_hbm, uw_hbm, dw_hbm, out,
    wide, wide_f, narrow, narrow_f, q, res_src, gain_in, gain, fin_f,
    kv, sco, m2s,
    ow, guw, dw, m2, comb, m2o, m2all, lhs, rin, resid,
    own, cs, cr, qs, yd, sum1, zfar, fs, ffar, yfm, yfp, zs, zin, tot,
    sbuf, gu, ss, xs, xr, hid,
    own2, cs2, cr2, qs2, yd2, sum2, zfar2, fs2, ffar2, yfm2, yfp2, zs2, zin2, tot2, fo, fb, fin_in,
    in_sem, w_sem, kv_sem, m2_s, m2_r, rs_s, rs_r, xa_s, xa_r,
    c_s, c_r, y_s, y_r, z_s, z_r, zf_s, zf_r, az_s, ay_s, ac_s, ag_r, ac_r,
    xs_s, xs_r, xh_s, xh_r, c2_s, c2_r, y2_s, y2_r, z2_s, z2_r, zf2_s, zf2_r, f_s, f_r,
):
    side, f, h = lax.axis_index("side"), lax.axis_index("fin"), lax.axis_index("fhid")
    y, z, c = h // 8, (h // 2) % 4, h % 2
    yz = h // 2
    oc = 1 - c
    j = f * 2 + c
    zt = 3 - z
    along_z = (z, z + 1 - 2 * (z % 2), (z + 2) % 4, 3 - z)
    at_end = z % 3 == 0
    copies = []

    def at(s, ff, yy, zz, cc):
        return (s, ff, (yy * 4 + zz) * 2 + cc)

    def make(src, dst, s_sem, r_sem, dev):
        return pltpu.make_async_remote_copy(
            src_ref=src, dst_ref=dst, send_sem=s_sem, recv_sem=r_sem,
            device_id=dev, device_id_type=MESH,
        )

    def send(*what):
        cp = make(*what)
        cp.start()
        copies.append(cp)

    maybe = []

    def send_if(cond, *what):
        pl.when(cond)(lambda: make(*what).start())
        maybe.append((cond, what))

    barrier = pltpu.get_barrier_semaphore()

    def greet(dev):
        pl.semaphore_signal(barrier, inc=1, device_id=dev, device_id_type=MESH)

    def deliver():
        for s in range(8):
            arrived(fin_in.at[s], f_r.at[s])
            fin_f[s] = fin_in[s].astype(F32)
            parts = [fin_f[s, :, k, :] for k in range(16)]
            out[:, s * 2048 : (s + 1) * 2048] = jnp.concatenate(parts, axis=1).astype(BF)

    @pl.when(side == 0)
    def _attention_side():
        kv_copies = []
        for i in range(2):
            for k in range(2):
                part = (i, slice(None), pl.ds(k * 1024, 1024))
                cp = pltpu.make_async_copy(kv_hbm.at[part], kv.at[part], kv_sem.at[i * 2 + k])
                cp.start()
                kv_copies.append(cp)
        first_in = pltpu.make_async_copy(q_hbm, wide, in_sem.at[0])
        second_in = pltpu.make_async_copy(fresh_hbm, narrow, in_sem.at[1])
        first_in.start()
        second_in.start()
        for d in range(8):
            greet(at(1, d // 2, y, zt, d % 2))
        first_in.wait()
        second_in.wait()
        value = wide[...].astype(F32)
        for k in range(128):
            wide_f[:, k, :] = value[:, k * 128 : (k + 1) * 128]
        q[...] = wide_f[...].reshape(256, 128).astype(BF)
        value = narrow[...].astype(F32)
        for k in range(16):
            narrow_f[:, k, :] = value[:, k * 128 : (k + 1) * 128]
        fresh = narrow_f[...].reshape(32, 128)
        mixed = attend(q, fresh, lens, kv, kv_copies, sco)
        sel = selection(
            lambda t: (t // 4) % 2 * 128 + t // 16 * 8 + (t // 8) % 2 * 4 + t % 4
        )
        m2s[...] = jnp.dot(sel, mixed, preferred_element_type=F32).astype(BF)
        pl.semaphore_wait(barrier, 16)
        for b in range(16):
            send(
                m2s.at[pl.ds(b * 16, 16)],
                m2.at[pl.ds(pl.multiple_of(yz * 16, 16), 16)],
                m2_s.at[b],
                m2_r.at[yz],
                at(1, f, b // 4, b % 4, c),
            )
        for cp in copies:
            cp.wait_send()
        deliver()

    @pl.when(side == 1)
    def _mlp_side():
        copies.clear()
        up, down, far = (y + 1) % 4, (y + 3) % 4, (y + 2) % 4
        dev_up, dev_down, dev_far = (at(1, f, yy, z, c) for yy in (up, down, far))
        dev_core = at(1, f, y, z, oc)
        first_in = pltpu.make_async_copy(res_hbm, wide, in_sem.at[0])
        second_in = pltpu.make_async_copy(gain_hbm, gain_in, in_sem.at[1])
        first_in.start()
        second_in.start()
        for d in range(16):
            greet(at(0, f, d // 4, d % 4, c))
        for d in range(1, 4):
            greet(at(1, (f + d) % 4, y, z, c))
            greet(at(1, (f + d) % 4, y, z, oc))
            greet(at(1, f, y, along_z[d], c))
        greet(dev_up)
        greet(dev_down)
        greet(dev_far)
        greet(dev_core)
        for d in range(8):
            greet(at(1, d // 2, y, zt, d % 2))
        weights = [
            pltpu.make_async_copy(a, b, w_sem.at[k])
            for k, (a, b) in enumerate(
                (
                    (ow_hbm, ow.at[pl.ds(0, 512)]),
                    (gw_hbm, guw.at[:, pl.ds(0, 256)]),
                    (uw_hbm, guw.at[:, pl.ds(256, 256)]),
                    (dw_hbm, dw),
                )
            )
        ]
        for cp in weights:
            cp.start()
        gu[...] = jnp.zeros_like(gu)
        ss[...] = jnp.zeros_like(ss)
        first_in.wait()
        second_in.wait()
        value = wide[...].astype(F32)
        for k in range(128):
            wide_f[:, k, :] = value[:, k * 128 : (k + 1) * 128]
        for k in range(4):
            rows = wide_f[:, k * 32 : (k + 1) * 32, :]
            res_src[k] = rows.reshape(64, 128).astype(BF)
        gain[...] = gain_in[...].astype(F32).reshape(32, 128)
        pl.semaphore_wait(barrier, 29)

        for d in range(1, 4):
            ff = (f + d) % 4
            send(res_src.at[ff], rin.at[f], rs_s.at[d], rs_r.at[f], at(1, ff, y, z, c))
        rin[f] = res_src[f]
        for d in range(1, 4):
            ff = (f + d) % 4
            arrived(rin.at[ff], rs_r.at[ff])
        sel = selection(
            lambda t: (t // 2) % 4 * 64 + ((t % 2) * 16 + (t // 8) % 16) * 2 + t // 128
        )
        resid[...] = jnp.dot(sel, rin[...].reshape(256, 128), preferred_element_type=F32)
        eight = [
            resid[half * 128 + n * 8 : half * 128 + n * 8 + 8, :] for n in range(16) for half in range(2)
        ]
        eight = jnp.concatenate(eight, axis=1)
        ow[512:528, :] = jnp.concatenate([eight, jnp.zeros_like(eight)], axis=0).astype(BF)
        ow[528:, :] = jnp.zeros((112, 4096), BF)
        t = iota((256, 128), 0)
        row_yz = ((t // 128 + c) % 2 * 64 + t % 64) // 8
        here = (row_yz == yz) & (t // 64 % 2 == c) & (t % 8 == iota((256, 128), 1))
        lhs[:, 512:] = here.astype(F32).astype(BF)

        pick = selection(
            lambda t: (t // 64) % 2 * 128
            + ((t // 128 + c) % 2 * 8 + (t // 8) % 8) * 8
            + t % 2 * 4
            + t // 256,
            1024,
        )
        row_fin = (iota((1024, 128), 0) // 2) % 4
        for e in (0, 1, 3, 2):
            yy = (y + e) % 4
            for k in range(4):
                n = yy * 4 + k
                arrived(m2.at[pl.ds(pl.multiple_of(n * 16, 16), 16)], m2_r.at[n])
            rows = pl.ds(pl.multiple_of(yy * 64, 64), 64)
            part = pl.ds(pl.multiple_of(yy * 32, 32), 32)
            comb[...] = m2[rows, :].astype(F32).reshape(4, 16, 128)
            other = comb[:, pl.ds(pl.multiple_of(oc * 8, 8), 8), :]
            m2o[part, :] = other.reshape(32, 128).astype(BF)
            mine = comb[:, pl.ds(pl.multiple_of(c * 8, 8), 8), :]
            m2all[f, c, part, :] = mine.reshape(32, 128).astype(BF)
            for d in (2, 1, 3):
                ff = (f + d) % 4
                to = m2all.at[f, c, part]
                send(to, to, xa_s.at[d, e], xa_r.at[j, yy], at(1, ff, y, z, c))
                send(m2o.at[part], to, xa_s.at[4 + d, e], xa_r.at[j, yy], at(1, ff, y, z, oc))
            send(m2o.at[part], m2all.at[f, c, part], xa_s.at[0, e], xa_r.at[j, yy], dev_core)

        def quarter(ff, cc):
            for k in range(4):
                arrived(m2all.at[ff, cc, pl.ds(k * 32, 32)], xa_r.at[ff * 2 + cc, k])

        quarter(f, oc)
        picked = jnp.where(
            row_fin == f, jnp.dot(pick, m2all[f].reshape(256, 128), preferred_element_type=F32), 0.0
        )
        for d in (1, 3, 2):
            ff = (f + d) % 4
            quarter(ff, c)
            quarter(ff, oc)
            picked = jnp.where(
                row_fin == ff,
                jnp.dot(pick, m2all[ff].reshape(256, 128), preferred_element_type=F32),
                picked,
            )
        for k in range(4):
            lhs[:, k * 128 : (k + 1) * 128] = picked[k * 256 : (k + 1) * 256, :].astype(BF)
        weights[0].wait()

        def project(g):
            yy = (y + ORDER[g]) % 4

            w = ow[:, pl.ds(pl.multiple_of(yy * 1024, 1024), 1024)]
            value = jnp.dot(lhs[...], w, preferred_element_type=F32)
            for p in range(2):
                for k in range(4):
                    cols = slice(k * 256, (k + 1) * 256)
                    cs[p, yy * 4 + k] = value[128 + p * 64 : 192 + p * 64, cols].astype(BF)
                    own[p, yy * 4 + k] = value[p * 64 : p * 64 + 64, cols]
            part = pl.ds(yy * 4, 4)
            for p in range(2):
                send(cs.at[p, part], cr.at[p, part], c_s.at[p, g], c_r.at[p, g], dev_core)

        def paired(p, n):
            return own[p, n] + cr[p, n].astype(F32)

        def beside(p, g):
            yy = (y + ORDER[g]) % 4
            arrived(cr.at[p, pl.ds(yy * 4, 4)], c_r.at[p, g])
            to, dev = ((yfm, dev_up), (yfp, dev_down))[g - 1]
            for d in (3, 2, 1, 0):
                k = along_z[d]
                qs[p, yy, k] = paired(p, yy * 4 + k).astype(BF)
                send(
                    qs.at[p, yy, k], to.at[p, k],
                    y_s.at[p, (g - 1) * 4 + d], y_r.at[p, (g - 1) * 4 + k], dev,
                )

        def opposite(p):
            arrived(cr.at[p, pl.ds(far * 4, 4)], c_r.at[p, 0])
            for d in (3, 2, 1):
                zz = along_z[d]
                qs[p, far, zz] = paired(p, far * 4 + zz).astype(BF)
                what = (
                    qs.at[p, far, zz], zfar.at[p, z], zf_s.at[p, d], zf_r.at[p, z],
                    at(1, f, y, zz, c),
                )
                if d == 3:
                    send_if(z % 3 != 0, *what)
                    send_if(
                        at_end, qs.at[p, far, zz], yd.at[p], y_s.at[p, 9], y_r.at[p, 9], dev_far
                    )
                else:
                    send(*what)

        def onward(p):
            value = paired(p, far * 4 + z)
            for d in (2, 1):
                zz = along_z[d]
                arrived(zfar.at[p, zz], zf_r.at[p, zz])
                value = value + zfar[p, zz].astype(F32)
            sum1[...] = value

            @pl.when(z % 3 != 0)
            def _from_third():
                arrived(zfar.at[p, zt], zf_r.at[p, zt])
                sum1[...] += zfar[p, zt].astype(F32)

            fs[p] = sum1[...].astype(BF)
            send(fs.at[p], ffar.at[p], y_s.at[p, 8], y_r.at[p, 8], dev_far)

        def over_z(p):
            part = pl.ds(y * 4, 4)
            arrived(cr.at[p, part], c_r.at[p, 3])

            def summed(k):
                arrived(yfm.at[p, k], y_r.at[p, k])
                arrived(yfp.at[p, k], y_r.at[p, 4 + k])
                return paired(p, y * 4 + k) + yfm[p, k].astype(F32) + yfp[p, k].astype(F32)

            for d in (3, 2, 1):
                zz = along_z[d]
                value = summed(zz)
                if d == 3:
                    sum1[...] = value

                    @pl.when(at_end)
                    def _from_opposite():
                        arrived(yd.at[p], y_r.at[p, 9])
                        sum1[...] += yd[p].astype(F32)

                    value = sum1[...]
                zs[p, zz] = value.astype(BF)
                send(zs.at[p, zz], zin.at[p, z], z_s.at[p, d], z_r.at[p, z], at(1, f, y, zz, c))
            tot[p] = summed(z)

        def give(p, n, slot, dev):
            ref = sbuf.at[p, n, c]
            send(ref, ref, ay_s.at[p, slot], ag_r.at[p, n], dev)

        def give_y(p, n, k):
            give(p, n, 2 * k, dev_up)
            give(p, n, 2 * k + 1, dev_down)

        def give_core(p, n):
            ref = sbuf.at[p, n, c]
            send(ref, ref, ac_s.at[p, n], ac_r.at[p, n], dev_core)

        def use(p, yy):
            parts = []
            for k in range(4):
                n = yy * 4 + k
                arrived(sbuf.at[p, n, oc], ac_r.at[p, n])
                x = sbuf[p, n].reshape(128, 256).astype(F32)
                sq = x * x
                ss[p] += sq[:, :128] + sq[:, 128:]
                pair = [gain[pl.ds(n * 2 + m, 1), :] for m in range(2)]
                parts.append((x * jnp.concatenate(pair, axis=1)).astype(BF))
            w = guw[pl.ds(pl.multiple_of(yy * 1024, 1024), 1024), :]
            gu[p] += jnp.dot(jnp.concatenate(parts, axis=1), w, preferred_element_type=F32)

        def near(p):
            total = tot[p]
            for d in (3, 2, 1):
                zz = along_z[d]
                arrived(zin.at[p, zz], z_r.at[p, zz])
                total = total + zin[p, zz].astype(F32)
            arrived(ffar.at[p], y_r.at[p, 8])
            total = total + ffar[p].astype(F32)
            sbuf[p, yz, c] = total.astype(BF)
            give(p, yz, 8, dev_far)
            for d in (3, 2, 1):
                zz = along_z[d]
                ref = sbuf.at[p, yz, c]
                send(ref, ref, az_s.at[p, d], ag_r.at[p, yz], at(1, f, y, zz, c))
            give_y(p, yz, 0)
            give_core(p, yz)

        def forward(p):
            for d in (3, 2, 1):
                n = y * 4 + along_z[d]
                arrived(sbuf.at[p, n, c], ag_r.at[p, n])
                if d == 3:
                    ref = sbuf.at[p, n, c]
                    send_if(at_end, ref, ref, ay_s.at[p, 9], ag_r.at[p, n], dev_far)
                give_y(p, n, d)
                give_core(p, n)

        def spread_opposite(p):
            n = far * 4 + z
            arrived(sbuf.at[p, n, c], ag_r.at[p, n])
            ref = sbuf.at[p, n, c]
            for d in (3, 2, 1):
                what = (ref, ref, az_s.at[p, 4 + d], ag_r.at[p, n], at(1, f, y, along_z[d], c))
                if d == 3:
                    send_if(z % 3 != 0, *what)
                else:
                    send(*what)
            give_core(p, n)

        def taken(p, group, d):
            n = group * 4 + along_z[d]
            arrived(sbuf.at[p, n, c], ag_r.at[p, n])
            give_core(p, n)

        def over_fin(p):
            tt = jnp.sum(ss[p], axis=1, keepdims=True)
            top = tt.astype(BF).astype(F32)
            low = iota((128, 128), 1) < 64
            xs[p, :, :, 512:] = jnp.where(low, top, tt - top).astype(BF).reshape(4, 32, 128)
            xs[p, :, :, :512] = gu[p].astype(BF).reshape(4, 32, 512)
            for d in (2, 1, 3):
                ff = (f + d) % 4
                send(xs.at[p, ff], xr.at[p, f], xs_s.at[p, d], xs_r.at[p, f], at(1, ff, y, z, c))

        def hide(p):
            mine = pl.ds(pl.multiple_of(f * 32, 32), 32)
            both = gu[p, mine, :]
            square = xs[p, f][:, 512:].astype(F32)
            for d in (1, 3, 2):
                ff = (f + d) % 4
                arrived(xr.at[p, ff], xs_r.at[p, ff])
                both = both + xr[p, ff][:, :512].astype(F32)
                square = square + xr[p, ff][:, 512:].astype(F32)
            scale = lax.rsqrt((square[:, 0:1] + square[:, 64:65]) / D + 1e-05)
            gate = both[:, :256] * scale
            hid[p, mine, :] = (gate / (1.0 + jnp.exp(-gate)) * (both[:, 256:] * scale)).astype(BF)
            for d in (2, 1, 3):
                ff = (f + d) % 4
                ref = hid.at[p, mine]
                send(ref, ref, xh_s.at[p, d], xh_r.at[p, f], at(1, ff, y, z, c))

        def lower(p):
            for d in (1, 3, 2):
                ff = (f + d) % 4
                ref = hid.at[p, pl.ds(pl.multiple_of(ff * 32, 32), 32)]
                arrived(ref, xh_r.at[p, ff])

            def columns(core):
                parts = []
                for half in range(2):
                    start = core * 2048 + half * 1024
                    w = dw[:, pl.ds(pl.multiple_of(start, 1024), 1024)]
                    value = jnp.dot(hid[p], w, preferred_element_type=F32)
                    parts.append(value.reshape(16, 8, 1024))
                return jnp.concatenate(parts, axis=1)

            cs2[p] = columns(oc).astype(BF)
            for g in range(4):
                part = pl.ds((y + ORDER[g]) % 4 * 4, 4)
                send(cs2.at[p, part], cr2.at[p, part], c2_s.at[p, g], c2_r.at[p, g], dev_core)
            own2[p] = columns(c)

        def paired2(p, n):
            return own2[p, n] + cr2[p, n].astype(F32)

        def beside2(p, g):
            yy = (y + ORDER[g]) % 4
            arrived(cr2.at[p, pl.ds(yy * 4, 4)], c2_r.at[p, g])
            to, dev = ((yfm2, dev_up), (yfp2, dev_down))[g - 1]
            for d in (3, 2, 1, 0):
                k = 3 - along_z[d]
                qs2[p, yy, k] = paired2(p, yy * 4 + k).astype(BF)
                send(
                    qs2.at[p, yy, k], to.at[p, k],
                    y2_s.at[p, (g - 1) * 4 + d], y2_r.at[p, (g - 1) * 4 + k], dev,
                )

        def opposite2(p):
            arrived(cr2.at[p, pl.ds(far * 4, 4)], c2_r.at[p, 0])
            for d in (3, 2, 1):
                zz = along_z[d]
                qs2[p, far, zz] = paired2(p, far * 4 + (3 - zz)).astype(BF)
                what = (
                    qs2.at[p, far, zz], zfar2.at[p, z], zf2_s.at[p, d], zf2_r.at[p, z],
                    at(1, f, y, zz, c),
                )
                if d == 3:
                    send_if(z % 3 != 0, *what)
                    send_if(
                        at_end, qs2.at[p, far, zz], yd2.at[p], y2_s.at[p, 9], y2_r.at[p, 9], dev_far
                    )
                else:
                    send(*what)

        def onward2(p):
            value = paired2(p, far * 4 + zt)
            for d in (2, 1):
                zz = along_z[d]
                arrived(zfar2.at[p, zz], zf2_r.at[p, zz])
                value = value + zfar2[p, zz].astype(F32)
            sum2[...] = value

            @pl.when(z % 3 != 0)
            def _from_third():
                arrived(zfar2.at[p, zt], zf2_r.at[p, zt])
                sum2[...] += zfar2[p, zt].astype(F32)

            fs2[p] = sum2[...].astype(BF)
            send(fs2.at[p], ffar2.at[p], y2_s.at[p, 8], y2_r.at[p, 8], dev_far)

        def over_z2(p):
            part = pl.ds(y * 4, 4)
            arrived(cr2.at[p, part], c2_r.at[p, 3])

            def summed(k):
                arrived(yfm2.at[p, k], y2_r.at[p, k])
                arrived(yfp2.at[p, k], y2_r.at[p, 4 + k])
                return paired2(p, y * 4 + k) + yfm2[p, k].astype(F32) + yfp2[p, k].astype(F32)

            for d in (3, 2, 1):
                zz = along_z[d]
                value = summed(3 - zz)
                if d == 3:
                    sum2[...] = value

                    @pl.when(at_end)
                    def _from_opposite():
                        arrived(yd2.at[p], y2_r.at[p, 9])
                        sum2[...] += yd2[p].astype(F32)

                    value = sum2[...]
                zs2[p, zz] = value.astype(BF)
                send(
                    zs2.at[p, zz], zin2.at[p, z], z2_s.at[p, d], z2_r.at[p, z], at(1, f, y, zz, c)
                )
            slab = pl.ds(pl.multiple_of(((y * 4 + zt) % 8) // 2 * 16, 16), 16)
            halves = []
            for half in range(2):
                kept = [
                    sbuf[p, c * 8 + half * 4 + m, y // 2, slab, :].astype(F32) for m in range(4)
                ]
                kept = jnp.concatenate(kept, axis=1)
                halves.append(jnp.where(zt % 2 == 0, kept[:8], kept[8:]))
            tot2[p] = summed(zt) + jnp.concatenate(halves, axis=0)

        def finish(p):
            total = tot2[p]
            for d in (3, 2, 1):
                zz = along_z[d]
                arrived(zin2.at[p, zz], z2_r.at[p, zz])
                total = total + zin2[p, zz].astype(F32)
            arrived(ffar2.at[p], y2_r.at[p, 8])
            total = total + ffar2[p].astype(F32)
            for k in range(16):
                rows = slice(k // 8 * 8, k // 8 * 8 + 8)
                fo[:, k, :] = total[rows, k % 8 * 128 : (k % 8 + 1) * 128]
            fb[p] = fo[...].astype(BF)
            for d in range(8):
                ff = (f + d // 2) % 4
                send(
                    fb.at[p, pl.ds(ff * 2, 2)], fin_in.at[j], f_s.at[p, d], f_r.at[j],
                    at(d % 2, ff, y, zt, p),
                )

        project(0)
        project(1)
        opposite(0)
        project(2)
        beside(0, 1)
        opposite(1)
        beside(0, 2)
        beside(1, 1)
        beside(1, 2)
        project(3)
        onward(0)
        over_z(0)
        onward(1)
        over_z(1)
        near(0)
        near(1)
        weights[1].wait()
        weights[2].wait()
        forward(0)
        spread_opposite(0)
        spread_opposite(1)
        forward(1)
        for p in range(2):
            taken(p, up, 0)
            taken(p, down, 0)
        use(0, y)
        use(1, y)
        for d in (3, 2, 1):
            taken(0, up, d)
            taken(0, down, d)
            taken(0, far, d)
        use(0, up)
        use(0, down)
        use(0, far)
        over_fin(0)
        for d in (3, 2, 1):
            taken(1, far, d)
            taken(1, up, d)
            taken(1, down, d)
        use(1, far)
        use(1, up)
        use(1, down)
        over_fin(1)
        hide(0)
        hide(1)
        weights[3].wait()
        lower(0)
        opposite2(0)
        beside2(0, 1)
        beside2(0, 2)
        lower(1)
        opposite2(1)
        beside2(1, 1)
        beside2(1, 2)
        onward2(0)
        over_z2(0)
        onward2(1)
        over_z2(1)
        finish(0)
        finish(1)
        deliver()
        for cp in copies:
            cp.wait_send()
        for cond, what in maybe:
            pl.when(cond)(lambda what=what: make(*what).wait_send())


def moved(*args):
    def v(*shape, dtype=BF):
        return pltpu.VMEM(shape, dtype)

    scratch = [
        v(2, D), v(2, 128, 128, dtype=F32), v(2, 2048), v(2, 16, 128, dtype=F32), v(256, 128),
        v(4, 64, 128), v(4096), v(32, 128, dtype=F32), v(8, 2, 16, 128, dtype=F32),
        v(2, 256, 2048), v(256, 256, dtype=F32), v(256, 128),
        v(640, 4096), v(4096, 512), v(256, 4096),
        v(256, 128), v(4, 16, 128, dtype=F32), v(128, 128), v(4, 2, 128, 128), v(256, 640),
        v(4, 64, 128), v(256, 128, dtype=F32),
        v(2, 16, 64, 256, dtype=F32), v(2, 16, 64, 256), v(2, 16, 64, 256), v(2, 4, 4, 64, 256),
        v(2, 64, 256), v(64, 256, dtype=F32),
        v(2, 4, 64, 256), v(2, 64, 256), v(2, 64, 256), v(2, 4, 64, 256), v(2, 4, 64, 256),
        v(2, 4, 64, 256), v(2, 4, 64, 256), v(2, 64, 256, dtype=F32),
        v(2, 16, 2, 64, 256), v(2, 128, 512, dtype=F32), v(2, 128, 128, dtype=F32),
        v(2, 4, 32, 640), v(2, 4, 32, 640), v(2, 128, 256),
        v(2, 16, 16, 1024, dtype=F32), v(2, 16, 16, 1024), v(2, 16, 16, 1024),
        v(2, 4, 4, 16, 1024), v(2, 16, 1024), v(16, 1024, dtype=F32),
        v(2, 4, 16, 1024), v(2, 16, 1024), v(2, 16, 1024),
        v(2, 4, 16, 1024), v(2, 4, 16, 1024), v(2, 4, 16, 1024), v(2, 4, 16, 1024),
        v(2, 16, 1024, dtype=F32), v(8, 16, 128, dtype=F32), v(2, 8, 16, 128), v(8, 2, 16, 128),
    ]
    counts = [
        (2,), (4,), (4,), (16,), (16,), (4,), (4,), (8, 4), (8, 4),
        (2, 4), (2, 4), (2, 10), (2, 10), (2, 4), (2, 4), (2, 4), (2, 4),
        (2, 8), (2, 12), (2, 16), (2, 16), (2, 16),
        (2, 4), (2, 4), (2, 4), (2, 4), (2, 4), (2, 4), (2, 10), (2, 10), (2, 4), (2, 4),
        (2, 4), (2, 4), (2, 8), (8,),
    ]
    scratch += [pltpu.SemaphoreType.DMA(k) for k in counts]
    vm, hbm = pl.BlockSpec(memory_space=pltpu.VMEM), pl.BlockSpec(memory_space=pl.ANY)
    sm = pl.BlockSpec(memory_space=pltpu.SMEM)
    return pl.pallas_call(
        kernel,
        out_shape=jax.ShapeDtypeStruct((2, D), BF),
        in_specs=[hbm, hbm, sm, hbm, hbm, hbm, hbm, hbm, hbm, hbm],
        out_specs=vm,
        scratch_shapes=scratch,
        compiler_params=pltpu.CompilerParams(
            collective_id=0, has_side_effects=True, vmem_limit_bytes=56 * 1024 * 1024
        ),
    )(*args)


def on_device(
    queries, new_entries, cached_entries, lengths, residual, norm_gain,
    out_weight, gate_weight, up_weight, down_weight,
):
    return moved(
        queries, new_entries, lengths, cached_entries[0], residual, norm_gain,
        out_weight[0], gate_weight[0], up_weight[0], down_weight[0],
    )


def solution(mesh):
    placed = (
        P(("fin", "fhid"), None),
        P(("fin", "fhid"), None),
        P("side", ("fin", "fhid"), None, None),
        P(("fin", "fhid")),
        P(("fin", "fhid"), None),
        P("fin"),
        P("side", "fhid", "fin"),
        P("side", "fin", "fhid"),
        P("side", "fin", "fhid"),
        P("side", "fhid", "fin"),
    )
    return jax.shard_map(
        on_device, mesh=mesh, in_specs=placed, out_specs=P(("fin", "fhid"), None), check_vma=False
    )
```
